512 devices in a mesh: gx: 16 (over z_hi, y), gy: 32 (over x, z_lo, core).
Axes of the slice: x: 4, y: 8, z: 8 (z_hi: 2, z_lo: 4; z = z_hi * 4 + z_lo), core: 2. Of those that a mesh axis runs over, the one named last changes fastest.
Arguments:
- populations: float32 [27, 64, 256, 128], P(None, 'gx', 'gy'), may hold values from 0 to 1, as said below
- cotangent: float32 [27, 64, 256, 128], P(None, 'gx', 'gy'), may hold values from -6 to 6
- porosity: float32 [64, 256, 128], P('gx', 'gy'), may hold values from 0 to 1
- cell_type: int32 [64, 256, 128], P('gx', 'gy'), may hold values from 0 to 4, as said below
- rates: float32 [27], replicated, may hold values from 0.6 to 1.9
- start_step: int32 [1], replicated, may hold values from 0 to 1023
Outputs:
- flow: float32 [27, 64, 256, 128], P(None, 'gx', 'gy')
- adjoint_populations: float32 [27, 64, 256, 128], P(None, 'gx', 'gy')
- sensitivity: float32 [64, 256, 128], P('gx', 'gy')
The draws below stay inside these ranges and needn't reach their ends.
Inputs may be any that keep to these rules, and one draw needn't show every extreme that they name: `populations`: every population is positive. `cell_type`: 0 fluid, 1 solid, 2 inlet, 3 outlet, 4 wall; fluid cells are the most common type.
All inputs are finite; a program needn't handle non-finite values.
Results may differ from the reference program's by a relative error of at most 0.0003.
Values sent between devices are 32-bit elements; how exact they have to be, the bound alone decides.
No kernel may reach another device: no remote copies, remote signals or barrier semaphores. Data moves between devices by JAX's collectives and lax.ppermute only.
A program may use at most 64 MiB of HBM per device.

```python
import math
import jax
import jax.numpy as jnp
import numpy as np
from jax import lax

STEPS = 4
NX = 64
NY = 256
NZ = 128
N_GX = 16


line_weight = np.array([1.0 / 6.0, 2.0 / 3.0, 1.0 / 6.0])


lattice_weight = np.kron(np.kron(line_weight, line_weight), line_weight)


def draw_populations(key, part):
    key = jax.random.fold_in(key, 11)
    weights = jnp.asarray(lattice_weight, jnp.float32).reshape(27, 1, 1, 1)
    noise = jax.random.normal(key, (27, NX, NY, NZ), jnp.float32)
    return weights * jnp.exp(0.25 * jnp.clip(noise, -3.0, 3.0))


def draw_cell_type(key, part):
    key = jax.random.fold_in(key, 23)
    codes = jax.random.randint(key, (NX, NY, NZ), 0, 20)
    return jnp.where(codes < 13, 0, jnp.where(codes < 16, 1, jnp.where(codes == 16, 2, jnp.where(codes == 17, 3, 4)))).astype(jnp.int32)


def steps_of(rng, dims, cuts, smallest, largest):
    def one(dim, blocks):
        steps = jax.random.uniform(jax.random.fold_in(jax.random.fold_in(rng, 6), dim), (blocks,), jnp.float32, smallest / len(cuts), largest / len(cuts))
        return jnp.repeat(jnp.exp(steps), dims[dim] // blocks).reshape((-1,) + (1,) * (len(dims) - dim - 1))

    factor_of = one(*cuts[0])
    for cut in cuts[1:]:
        factor_of = factor_of * one(*cut)
    return factor_of


def normal_values(stream_key, extent, scale, reach, cuts=(), kind=jnp.bfloat16):
    loudness = steps_of(stream_key, extent, cuts, -0.22, 0.18) if cuts else 1.0
    drawn = jax.random.normal(stream_key, extent, jnp.float32) * scale * loudness
    return jnp.minimum(jnp.maximum(drawn, -reach), reach).astype(kind)


def setup_inputs(seed: int = 0) -> dict:
    arg_keys = jax.random.split(jax.random.key(seed), 7)
    populations = draw_populations(jax.random.fold_in(arg_keys[6], 71), 0)
    cotangent = normal_values(arg_keys[1], (27, NX, NY, NZ), 1.0, 6.0, ((1, 16), (2, 32)), jnp.float32)
    porosity = jnp.clip(1.0 * jax.random.uniform(arg_keys[2], (NX, NY, NZ), jnp.float32) ** steps_of(arg_keys[2], (NX, NY, NZ), ((0, 16), (1, 32)), -0.2, 0.2), 0.0, 1.0)
    cell_type = draw_cell_type(jax.random.fold_in(arg_keys[6], 71), 0)
    rates = jnp.clip(jnp.exp(jax.random.uniform(arg_keys[4], (27,), jnp.float32, math.log(0.6), math.log(1.9))), 0.6, 1.9)
    start_step = jax.random.randint(arg_keys[5], (1,), 0, 1024).astype(jnp.int32)
    return {"populations": populations, "cotangent": cotangent, "porosity": porosity, "cell_type": cell_type, "rates": rates, "start_step": start_step}


line_basis = np.array([[1.0, 1.0, 1.0], [-1.0, 0.0, 1.0], [1.0, -2.0, 1.0]])
line_inverse = line_basis.T / np.array([3.0, 2.0, 6.0])
moment_basis = np.kron(np.kron(line_basis, line_basis), line_basis)
moment_inverse = np.kron(np.kron(line_inverse, line_inverse), line_inverse)
line_weight = np.array([1.0 / 6.0, 2.0 / 3.0, 1.0 / 6.0])
lattice_weight = np.kron(np.kron(line_weight, line_weight), line_weight)
lattice_vel = np.array([[a - 1.0, b - 1.0, d - 1.0] for a in range(3) for b in range(3) for d in range(3)])
drag_max = 1.0
ramp_q = 0.1
inlet_speed = 0.3
pulse_period = 64.0

def collision_matrix(rates):
    scaled = jnp.asarray(moment_inverse, jnp.float32) * rates[None, :]
    return jnp.dot(scaled, jnp.asarray(moment_basis, jnp.float32), precision=lax.Precision.HIGHEST)

def equilibrium(density, speed_x, speed_y, speed_z):
    velocity = jnp.asarray(lattice_vel, jnp.float32)
    weights = jnp.asarray(lattice_weight, jnp.float32)
    along = velocity[:, 0, None, None, None] * speed_x + velocity[:, 1, None, None, None] * speed_y + velocity[:, 2, None, None, None] * speed_z
    speed_sq = speed_x * speed_x + speed_y * speed_y + speed_z * speed_z
    return weights[:, None, None, None] * density * (1.0 + 3.0 * along + 4.5 * along * along - 1.5 * speed_sq)

def collide(state_now, gamma, cell_kind, collision, time_value):
    blocks = state_now.reshape((3, 3, 3) + state_now.shape[1:])
    density = lax.optimization_barrier(jnp.sum(state_now, axis=0))
    speed_x = lax.optimization_barrier(jnp.sum(blocks[2] - blocks[0], axis=(0, 1))) / density
    speed_y = lax.optimization_barrier(jnp.sum(blocks[:, 2] - blocks[:, 0], axis=(0, 1))) / density
    speed_z = lax.optimization_barrier(jnp.sum(blocks[:, :, 2] - blocks[:, :, 0], axis=(0, 1))) / density
    drag_coef = drag_max * ramp_q * (1.0 - gamma) / (ramp_q + gamma)
    damping = jnp.where(cell_kind == 1, 0.0, 1.0 / (1.0 + drag_coef))
    target = equilibrium(density, speed_x * damping, speed_y * damping, speed_z * damping)
    relaxed = state_now - jnp.einsum('ij,jxyz->ixyz', collision, state_now - target, precision=lax.Precision.HIGHEST)
    unity = jnp.ones_like(density)
    inlet_eq = equilibrium(unity, 0.0 * unity, 0.0 * unity, inlet_speed * jnp.sin(2.0 * np.pi * time_value / pulse_period) * unity)
    outlet = equilibrium(unity, speed_x, speed_y, speed_z)
    bounce = state_now[::-1]
    kinds = cell_kind[None]
    return jnp.where(kinds == 2, inlet_eq, jnp.where(kinds == 3, outlet, jnp.where(kinds == 4, bounce, relaxed)))

def stream(post, direction):
    moved = []
    for index in range(27):
        offsets = tuple((direction * int(lattice_vel[index][axis]) for axis in range(3)))
        moved.append(jnp.roll(post[index], offsets, axis=(0, 1, 2)))
    return jnp.stack(moved)

def slabs(array):
    leading = array.shape[:-3]
    shaped = array.reshape(leading + (N_GX, NX // N_GX) + array.shape[-2:])
    return jnp.moveaxis(shaped, len(leading), 0)

def unslab(array):
    moved = jnp.moveaxis(array, 0, array.ndim - 4)
    leading = moved.shape[:-4]
    return moved.reshape(leading + (NX,) + moved.shape[-2:])

def step_time(start_step, step):
    return (start_step[0] + step).astype(jnp.float32)

def reference(populations, cotangent, porosity, cell_type, rates, start_step):
    collision = collision_matrix(rates)
    states = []
    current = populations
    for step in range(STEPS):
        states.append(current)
        moment = step_time(start_step, step)

        def forward_slab(pieces):
            return collide(pieces[0], pieces[1], pieces[2], collision, moment)
        post = unslab(lax.map(forward_slab, (slabs(current), slabs(porosity), slabs(cell_type))))
        current = stream(post, 1)
    adjoint = cotangent
    sensitivity = jnp.zeros(porosity.shape, jnp.float32)
    for step in reversed(range(STEPS)):
        pulled = stream(adjoint, -1)
        moment = step_time(start_step, step)

        def adjoint_slab(pieces):
            state_now, gamma, cell_kind, incoming = pieces

            def local(values, design):
                return collide(values, design, cell_kind, collision, moment)
            _, pullback = jax.vjp(local, state_now, gamma)
            return pullback(incoming)
        grads = lax.map(adjoint_slab, (slabs(states[step]), slabs(porosity), slabs(cell_type), slabs(pulled)))
        adjoint = unslab(grads[0])
        sensitivity = sensitivity + unslab(grads[1])
    return (current, adjoint, sensitivity)
```

```python
import jax
import jax.numpy as jnp
import numpy as np
from jax import lax
from jax.experimental import pallas as pl
from jax.experimental.pallas import tpu as pltpu
from jax.sharding import PartitionSpec as P

DRAG_MAX = 1.0
RAMP_Q = 0.1
INLET_SPEED = 0.3
PULSE_PERIOD = 64

NX, NY, LANES = 4, 8, 128
HALO = 3
PLANES = NX + 2 * HALO
ROWS = 3 * NY
VMEM_LIMIT = 48 * 1024 * 1024

SCALE = [
    float(s)
    for s in np.kron(np.kron([1 / 3, 1 / 2, 1 / 6], [1 / 3, 1 / 2, 1 / 6]), [1 / 3, 1 / 2, 1 / 6])
]
VEL = [(a - 1, b - 1, d - 1) for a in range(3) for b in range(3) for d in range(3)]
ODD = [(c[0] == 0) ^ (c[1] == 0) ^ (c[2] == 0) for c in VEL]


def reach(component, side, width, direction):
    if direction == 0:
        return width
    inward = -side * direction
    return max(0, width - (0 if component == inward else 1 if component == 0 else 2))


def member_reach(field, i, axis, side):
    _, _, width, direction = field
    return reach(VEL[i][axis] if direction else 0, side, width, direction)


def plan_x(fields, side):
    places = {}
    for field in fields:
        for layer in range(1, field[2] + 1):
            for i in range(field[1]):
                if member_reach(field, i, 0, side) >= layer:
                    places[field[0], i, layer] = len(places)
    return places, len(places)


def plan_y(fields, side):
    entries, start = [], 0
    for field in fields:
        for plane in range(-field[2], NX + field[2]):
            for i in range(field[1]):
                if plane < 0 and member_reach(field, i, 0, -1) < -plane:
                    continue
                if plane >= NX and member_reach(field, i, 0, 1) < plane - NX + 1:
                    continue
                rows = member_reach(field, i, 1, side)
                if rows:
                    entries.append((field[0], i, plane, start, rows))
                    start += rows
    return entries, -(-start // 8) * 8


FIRST = (("post", 27, 3, 1), ("adjoint", 27, 1, -1), ("cell", 2, 2, 0))
SECOND = (("adjoint", 27, 3, -1), ("post", 27, 1, 1), ("speed", 4, 2, 0))
PLAN_X = {(f, s): plan_x(f, s) for f in (FIRST, SECOND) for s in (-1, 1)}
PLAN_Y = {(f, s): plan_y(f, s) for f in (FIRST, SECOND) for s in (-1, 1)}


def pack_x(fields, side, read, out):
    for (name, i, layer), place in PLAN_X[fields, side][0].items():
        out[place] = read(name, i, layer - 1 if side > 0 else NX - layer)


def halo_tile(fields, from_low, from_high, name, i, plane):
    if plane < 0:
        return from_low, PLAN_X[fields, -1][0][name, i, -plane]
    return from_high, PLAN_X[fields, 1][0][name, i, plane - NX + 1]


def pack_y(fields, side, own, from_low, from_high, out):
    for name, i, plane, start, rows in PLAN_Y[fields, side][0]:
        first = 0 if side > 0 else NY - rows
        if 0 <= plane < NX:
            out[start : start + rows] = own(name, i, plane, first, rows)
        else:
            ref, place = halo_tile(fields, from_low, from_high, name, i, plane)
            out[start : start + rows] = ref[place, first : first + rows]


def unpack(fields, wide, from_x, from_y):
    for side, ref in zip((-1, 1), from_x):
        for (name, i, layer), place in PLAN_X[fields, side][0].items():
            plane = NX - 1 + layer if side > 0 else -layer
            wide[name][i, plane + HALO, NY : 2 * NY] = ref[place]
    for side, ref in zip((-1, 1), from_y):
        for name, i, plane, start, rows in PLAN_Y[fields, side][0]:
            first = 2 * NY if side > 0 else NY - rows
            wide[name][i, plane + HALO, first : first + rows] = ref[start : start + rows]


def moments(f):
    v = list(f)
    for stride in (9, 3, 1):
        for i in range(27):
            if (i // stride) % 3 == 0:
                a, b, c = v[i], v[i + stride], v[i + 2 * stride]
                s = (a + c) + b
                v[i], v[i + stride], v[i + 2 * stride] = s, c - a, s - 3.0 * b
    return v


def moments_transposed(m):
    v = list(m)
    for stride in (9, 3, 1):
        for i in range(27):
            if (i // stride) % 3 == 0:
                s, d, q = v[i], v[i + stride], v[i + 2 * stride]
                t = s + q
                v[i], v[i + stride], v[i + 2 * stride] = t - d, s - (q + q), t + d
    return v


def rate_of(rates, i, relaxing, even, odd):
    return jnp.where(relaxing, rates[i], odd if ODD[i] else even)


def kinds_of(kind):
    relaxing = kind < 1.5
    even = jnp.where((kind > 1.5) & (kind < 3.5), 1.0, 0.0)
    odd = jnp.where(kind > 3.5, 2.0, even)
    return relaxing, even, odd


def collide(f, kappa, kind, rates, inlet):
    m = moments(f)
    relaxing, even, odd = kinds_of(kind)
    rho = m[0]
    inverse = 1.0 / rho
    ux, uy, uz = m[9] * inverse, m[3] * inverse, m[1] * inverse
    vx, vy = kappa * ux, kappa * uy
    vz = jnp.where((kind > 1.5) & (kind < 2.5), inlet, kappa * uz)
    den = jnp.where(relaxing, rho, 1.0)
    jx, jy, jz = den * vx, den * vy, den * vz
    xy, xz, yz = jx * vy, jx * vz, jy * vz
    xx, yy, zz = 3.0 * (jx * vx), 3.0 * (jy * vy), 3.0 * (jz * vz)
    x2, y2, z2 = xx - den, yy - den, zz - den
    e = [None] * 27
    e[0] = den
    e[18], e[6], e[2] = x2, y2, z2
    e[24], e[20], e[8] = -(x2 + yy), -(x2 + zz), -(y2 + zz)
    e[26] = (x2 + yy) + zz
    e[9], e[15], e[11], e[17] = jx, -jx, -jx, jx
    e[3], e[21], e[5], e[23] = jy, -jy, -jy, jy
    e[1], e[19], e[7], e[25] = jz, -jz, -jz, jz
    e[12], e[14] = xy, -xy
    e[10], e[16] = xz, -xz
    e[4], e[22] = yz, -yz
    out = []
    for i in range(27):
        rate = rate_of(rates, i, relaxing, even, odd)
        gap = -m[i] if e[i] is None else e[i] - m[i]
        out.append(SCALE[i] * (m[i] + rate * gap))
    return moments_transposed(out), (ux, uy, uz, inverse, rho)


def collide_back(h, kappa, kind, rates, speed, rho=None):
    y = moments(h)
    relaxing, even, odd = kinds_of(kind)
    ux, uy, uz, inverse = speed
    w, z = [], []
    for i in range(27):
        yi = SCALE[i] * y[i]
        wi = rate_of(rates, i, relaxing, even, odd) * yi
        w.append(wi)
        z.append(yi - wi)
    vx, vy, vz = kappa * ux, kappa * uy, kappa * uz
    w222 = w[26]
    a_x = (w[18] - w[24]) - (w[20] - w222)
    a_y = (w[6] - w[24]) - (w[8] - w222)
    a_z = (w[2] - w[20]) - (w[8] - w222)
    b_x = (w[9] - w[15]) - (w[11] - w[17])
    b_y = (w[3] - w[21]) - (w[5] - w[23])
    b_z = (w[1] - w[19]) - (w[7] - w[25])
    c_xy, c_xz, c_yz = w[12] - w[14], w[10] - w[16], w[4] - w[22]
    base = ((w[0] - w[18]) - (w[6] + w[2])) + ((w[24] + w[20]) + (w[8] - w222))
    p_x, p_y, p_z = 3.0 * (a_x * vx), 3.0 * (a_y * vy), 3.0 * (a_z * vz)
    q_x, q_y, q_z = c_xy * vy + c_xz * vz, c_xy * vx + c_yz * vz, c_xz * vx + c_yz * vy
    r_x, r_y, r_z = b_x + p_x, b_y + p_y, b_z + p_z
    value = base + vx * (r_x + 0.5 * q_x) + vy * (r_y + 0.5 * q_y) + vz * (r_z + 0.5 * q_z)
    g_x, g_y, g_z = r_x + p_x + q_x, r_y + p_y + q_y, r_z + p_z + q_z
    factor = jnp.where(relaxing, kappa, kappa * inverse)
    along = ux * g_x + uy * g_y + uz * g_z
    z[0] = z[0] + (jnp.where(relaxing, value, 0.0) - factor * along)
    z[9] = z[9] + factor * g_x
    z[3] = z[3] + factor * g_y
    z[1] = z[1] + factor * g_z
    return moments_transposed(z), None if rho is None else rho * along


def turned(value, shift):
    return value if shift == 0 else pltpu.roll(value, shift % LANES, axis=1)


def pulled(wide, plane, row, direction):
    tiles = []
    for i, (cx, cy, cz) in enumerate(VEL):
        tile = wide[i, plane - direction * cx, pl.ds(row - direction * cy, NY)]
        tiles.append(turned(tile, direction * cz))
    return tiles


def inlet_speed(start, step):
    time = jnp.full((NY, LANES), (start[0] + step) % PULSE_PERIOD, jnp.int32).astype(jnp.float32)
    return INLET_SPEED * jnp.sin(time * (2.0 * np.pi / PULSE_PERIOD))


def kappa_of(porosity, kind):
    damping = (RAMP_Q + porosity) / (
        RAMP_Q * (1.0 + DRAG_MAX) + (1.0 - DRAG_MAX * RAMP_Q) * porosity
    )
    return jnp.where(kind < 0.5, damping, jnp.where((kind > 2.5) & (kind < 3.5), 1.0, 0.0))


def first_kernel(rates, start, populations, cotangent, porosity, cell_type, post, cell, speed, to_low, to_high):
    inlet = inlet_speed(start, 0)

    def plane_step(plane, carry):
        kind = cell_type[plane].astype(jnp.float32)
        kappa = kappa_of(porosity[plane], kind)
        cell[0, plane] = kappa
        cell[1, plane] = kind
        out, values = collide([populations[i, plane] for i in range(27)], kappa, kind, rates, inlet)
        for i in range(27):
            post[i, plane] = out[i]
        for i in range(5):
            speed[i, plane] = values[i]
        return carry

    lax.fori_loop(0, NX, plane_step, 0)
    sources = {"post": post, "adjoint": cotangent, "cell": cell}

    def read(name, i, plane):
        return sources[name][i, plane]

    pack_x(FIRST, 1, read, to_low)
    pack_x(FIRST, -1, read, to_high)


def second_kernel(post, cotangent, cell, from_low, from_high, to_low, to_high):
    sources = {"post": post, "adjoint": cotangent, "cell": cell}

    def own(name, i, plane, first, rows):
        return sources[name][i, plane, first : first + rows]

    pack_y(FIRST, 1, own, from_low, from_high, to_low)
    pack_y(FIRST, -1, own, from_low, from_high, to_high)


def third_kernel(
    rates, start, post, cotangent, cell, low_x, high_x, low_y, high_y,
    last_post, adjoint, wide_cell, speed_one, speed_two, gain, to_low, to_high,
    wide_post, next_post, wide_adjoint,
):
    for i in range(27):
        wide_post[i, HALO : HALO + NX, NY : 2 * NY] = post[i]
        wide_adjoint[i, HALO : HALO + NX, NY : 2 * NY] = cotangent[i]
    for i in range(2):
        wide_cell[i, HALO : HALO + NX, NY : 2 * NY] = cell[i]
    wide = {"post": wide_post, "adjoint": wide_adjoint, "cell": wide_cell}
    unpack(FIRST, wide, (low_x, high_x), (low_y, high_y))

    def forward(step, source, target, speed, width):
        inlet = inlet_speed(start, step)

        def body(n, carry):
            plane = n // 2 + (HALO - width)
            row = (n % 2) * NY + NY // 2
            here = pl.ds(row, NY)
            f = pulled(source, plane, row, 1)
            out, values = collide(f, wide_cell[0, plane, here], wide_cell[1, plane, here], rates, inlet)
            for i in range(27):
                target[i, plane, here] = out[i]
            for i in range(5):
                speed[i, plane, here] = values[i]
            return carry

        lax.fori_loop(0, 2 * (NX + 2 * width), body, 0)

    forward(1, wide_post, next_post, speed_one, 2)
    forward(2, next_post, wide_post, speed_two, 1)
    inlet = inlet_speed(start, 3)

    def last(n, carry):
        plane = n + HALO
        here = pl.ds(NY, NY)
        kappa, kind = wide_cell[0, plane, here], wide_cell[1, plane, here]
        out, values = collide(pulled(wide_post, plane, NY, 1), kappa, kind, rates, inlet)
        for i in range(27):
            last_post[i, n] = out[i]
        back, grad = collide_back(
            pulled(wide_adjoint, plane, NY, -1), kappa, kind, rates, values[:4], values[4]
        )
        for i in range(27):
            adjoint[i, n] = back[i]
        gain[n] = grad
        return carry

    lax.fori_loop(0, NX, last, 0)

    def read(name, i, plane):
        if name == "speed":
            return speed_two[i, plane + HALO, NY : 2 * NY]
        return {"post": last_post, "adjoint": adjoint}[name][i, plane]

    pack_x(SECOND, 1, read, to_low)
    pack_x(SECOND, -1, read, to_high)


def fourth_kernel(post, adjoint, speed, from_low, from_high, to_low, to_high):
    def own(name, i, plane, first, rows):
        if name == "speed":
            return speed[i, plane + HALO, NY + first : NY + first + rows]
        return {"post": post, "adjoint": adjoint}[name][i, plane, first : first + rows]

    pack_y(SECOND, 1, own, from_low, from_high, to_low)
    pack_y(SECOND, -1, own, from_low, from_high, to_high)


def fifth_kernel(
    rates, post, adjoint, wide_cell, speed_zero, speed_one, speed_two, gain, porosity,
    low_x, high_x, low_y, high_y,
    flow, first_adjoint, sensitivity,
    wide_post, wide_adjoint, next_adjoint, wide_speed, gains,
):
    for i in range(27):
        wide_post[i, HALO : HALO + NX, NY : 2 * NY] = post[i]
        wide_adjoint[i, HALO : HALO + NX, NY : 2 * NY] = adjoint[i]
    wide_speed[...] = speed_two[...]
    wide = {"post": wide_post, "adjoint": wide_adjoint, "speed": wide_speed}
    unpack(SECOND, wide, (low_x, high_x), (low_y, high_y))

    def back(source, target, speed, width, place):
        def body(n, carry):
            plane = n // 2 + (HALO - width)
            row = (n % 2) * NY + NY // 2
            here = pl.ds(row, NY)
            h = pulled(source, plane, row, -1)
            values = [speed[i, plane, here] for i in range(5)]
            out, grad = collide_back(
                h, wide_cell[0, plane, here], wide_cell[1, plane, here], rates, values[:4], values[4]
            )
            for i in range(27):
                target[i, plane, here] = out[i]
            gains[place, plane, here] = grad
            return carry

        lax.fori_loop(0, 2 * (NX + 2 * width), body, 0)

    back(wide_adjoint, next_adjoint, wide_speed, 2, 0)
    back(next_adjoint, wide_adjoint, speed_one, 1, 1)

    def last(n, carry):
        plane = n + HALO
        here = pl.ds(NY, NY)
        kappa, kind = wide_cell[0, plane, here], wide_cell[1, plane, here]
        values = [speed_zero[i, n] for i in range(5)]
        out, grad = collide_back(
            pulled(wide_adjoint, plane, NY, -1), kappa, kind, rates, values[:4], values[4]
        )
        for i in range(27):
            first_adjoint[i, n] = out[i]
        total = ((gain[n] + gains[0, plane, here]) + gains[1, plane, here]) + grad
        ramp = RAMP_Q * (1.0 + DRAG_MAX) + (1.0 - DRAG_MAX * RAMP_Q) * porosity[n]
        slope = (DRAG_MAX * RAMP_Q * (1.0 + RAMP_Q)) / (ramp * ramp)
        sensitivity[n] = jnp.where(kind < 0.5, slope * total, 0.0)
        tiles = pulled(wide_post, plane, NY, 1)
        for i in range(27):
            flow[i, n] = tiles[i]
        return carry

    lax.fori_loop(0, NX, last, 0)


def f32(*shape):
    return jax.ShapeDtypeStruct(shape, jnp.float32)


def call(kernel, scalars, arrays, outs, scratch=()):
    smem = pl.BlockSpec(memory_space=pltpu.SMEM)
    vmem = pl.BlockSpec(memory_space=pltpu.VMEM)
    return pl.pallas_call(
        kernel,
        out_shape=tuple(f32(*s) for s in outs),
        in_specs=[smem] * len(scalars) + [vmem] * len(arrays),
        out_specs=tuple(vmem for _ in outs),
        scratch_shapes=[pltpu.VMEM(s, jnp.float32) for s in scratch],
        compiler_params=pltpu.CompilerParams(vmem_limit_bytes=VMEM_LIMIT),
        name=kernel.__name__,
    )(*scalars, *arrays)


def exchange(axis, to_low, to_high):
    count = lax.axis_size(axis)
    up = [(i, (i + 1) % count) for i in range(count)]
    down = [(b, a) for a, b in up]
    return lax.ppermute(to_high, axis, up), lax.ppermute(to_low, axis, down)


def body(populations, cotangent, porosity, cell_type, rates, start_step):
    block = (27, NX, NY, LANES)
    wide = (27, PLANES, ROWS, LANES)
    tiles = (PLAN_X[FIRST, 1][1], NY, LANES), (PLAN_X[FIRST, -1][1], NY, LANES)
    rows = (PLAN_Y[FIRST, 1][1], LANES), (PLAN_Y[FIRST, -1][1], LANES)
    post, cell, speed_zero, to_low, to_high = call(
        first_kernel, (rates, start_step), (populations, cotangent, porosity, cell_type),
        (block, (2, NX, NY, LANES), (5, NX, NY, LANES)) + tiles,
    )
    x_halos = exchange("gx", to_low, to_high)
    to_low, to_high = call(second_kernel, (), (post, cotangent, cell) + x_halos, rows)
    y_halos = exchange("gy", to_low, to_high)
    wide_values = (5, PLANES, ROWS, LANES)
    tiles = (PLAN_X[SECOND, 1][1], NY, LANES), (PLAN_X[SECOND, -1][1], NY, LANES)
    rows = (PLAN_Y[SECOND, 1][1], LANES), (PLAN_Y[SECOND, -1][1], LANES)
    post, adjoint, wide_cell, speed_one, speed_two, gain, to_low, to_high = call(
        third_kernel, (rates, start_step), (post, cotangent, cell) + x_halos + y_halos,
        (block, block, (2, PLANES, ROWS, LANES), wide_values, wide_values, (NX, NY, LANES)) + tiles,
        (wide, wide, wide),
    )
    x_halos = exchange("gx", to_low, to_high)
    to_low, to_high = call(fourth_kernel, (), (post, adjoint, speed_two) + x_halos, rows)
    y_halos = exchange("gy", to_low, to_high)
    return call(
        fifth_kernel, (rates,),
        (post, adjoint, wide_cell, speed_zero, speed_one, speed_two, gain, porosity) + x_halos + y_halos,
        (block, block, (NX, NY, LANES)),
        (wide, wide, wide, wide_values, (2, PLANES, ROWS, LANES)),
    )


def solution(mesh):
    return jax.shard_map(
        body,
        mesh=mesh,
        in_specs=(
            P(None, "gx", "gy", None),
            P(None, "gx", "gy", None),
            P("gx", "gy", None),
            P("gx", "gy", None),
            P(),
            P(),
        ),
        out_specs=(P(None, "gx", "gy", None), P(None, "gx", "gy", None), P("gx", "gy", None)),
        check_vma=False,
    )
```

```python
import jax
import jax.numpy as jnp
import numpy as np
from jax import lax
from jax.experimental import pallas as pl
from jax.experimental.pallas import tpu as pltpu
from jax.sharding import PartitionSpec as P

DRAG_MAX = 1.0
RAMP_Q = 0.1
INLET_SPEED = 0.3
PULSE_PERIOD = 64

NX, NY, LANES = 4, 8, 128
HALO = 3
PLANES = NX + 2 * HALO
ROWS = 3 * NY
VMEM_LIMIT = 48 * 1024 * 1024

SCALE = [
    float(s)
    for s in np.kron(np.kron([1 / 3, 1 / 2, 1 / 6], [1 / 3, 1 / 2, 1 / 6]), [1 / 3, 1 / 2, 1 / 6])
]
VEL = [(a - 1, b - 1, d - 1) for a in range(3) for b in range(3) for d in range(3)]
ODD = [(c[0] == 0) ^ (c[1] == 0) ^ (c[2] == 0) for c in VEL]


def reach(component, side, width, direction):
    if direction in (0, 2):
        return width
    inward = -side * direction
    return max(0, width - (0 if component == inward else 1 if component == 0 else 2))


def member_reach(field, i, axis, side):
    _, _, width, direction = field
    return reach(VEL[i][axis] if abs(direction) == 1 else 0, side, width, direction)


def first_layer(field):
    return field[2] if field[3] == 2 else 1


def plan_x(fields, side):
    places = {}
    for field in fields:
        for layer in range(first_layer(field), field[2] + 1):
            for i in range(field[1]):
                if member_reach(field, i, 0, side) >= layer:
                    places[field[0], i, layer] = len(places)
    return places, len(places)


def plan_y(fields, side):
    entries, start = [], 0
    for field in fields:
        for plane in range(-field[2], NX + field[2]):
            for i in range(field[1]):
                if plane < 0 and member_reach(field, i, 0, -1) < -plane:
                    continue
                if plane >= NX and member_reach(field, i, 0, 1) < plane - NX + 1:
                    continue
                rows = member_reach(field, i, 1, side)
                skip = first_layer(field) - 1 if -field[2] < plane < NX + field[2] - 1 else 0
                if rows > skip:
                    entries.append((field[0], i, plane, start, skip, rows - skip))
                    start += rows - skip
    return entries, -(-start // 8) * 8


FIRST = (("post", 27, 3, 1), ("adjoint", 27, 1, -1), ("cell", 2, 2, 0))
SECOND = (("adjoint", 27, 3, -1), ("post", 27, 1, 1), ("speed", 4, 2, 2))
PLAN_X = {(f, s): plan_x(f, s) for f in (FIRST, SECOND) for s in (-1, 1)}
PLAN_Y = {(f, s): plan_y(f, s) for f in (FIRST, SECOND) for s in (-1, 1)}


def pack_x(fields, side, read, out):
    for (name, i, layer), place in PLAN_X[fields, side][0].items():
        out[place] = read(name, i, layer - 1 if side > 0 else NX - layer)


def halo_tile(fields, from_low, from_high, name, i, plane):
    if plane < 0:
        return from_low, PLAN_X[fields, -1][0][name, i, -plane]
    return from_high, PLAN_X[fields, 1][0][name, i, plane - NX + 1]


def pack_y(fields, side, own, from_low, from_high, out):
    for name, i, plane, start, skip, rows in PLAN_Y[fields, side][0]:
        first = skip if side > 0 else NY - skip - rows
        if 0 <= plane < NX or (name == "speed" and -2 < plane < NX + 1):
            out[start : start + rows] = own(name, i, plane, first, rows)
        else:
            ref, place = halo_tile(fields, from_low, from_high, name, i, plane)
            out[start : start + rows] = ref[place, first : first + rows]


def by_parity(axis, run, from_even, from_odd):
    parity = lax.axis_index(axis) % 2

    @pl.when(parity == 0)
    def _():
        run(from_odd, from_even)

    @pl.when(parity == 1)
    def _():
        run(from_even, from_odd)


def unpack_x(fields, wide, *from_x):
    for side, ref in zip((-1, 1), from_x):
        for (name, i, layer), place in PLAN_X[fields, side][0].items():
            plane = NX - 1 + layer if side > 0 else -layer
            wide[name][i, plane + HALO, NY : 2 * NY] = ref[place]


def unpack_y(fields, wide, *from_y):
    for side, ref in zip((-1, 1), from_y):
        for name, i, plane, start, skip, rows in PLAN_Y[fields, side][0]:
            first = 2 * NY + skip if side > 0 else NY - skip - rows
            wide[name][i, plane + HALO, first : first + rows] = ref[start : start + rows]


def unpack(fields, wide, even_x, odd_x, even_y, odd_y):
    by_parity("gx", lambda low, high: unpack_x(fields, wide, low, high), even_x, odd_x)
    partner = even_y.at[1 - lax.axis_index("gy") % 2]
    by_parity("gy", lambda low, high: unpack_y(fields, wide, low, high), partner, odd_y)


def send_x(fields, read, to_even, to_odd):
    def run(to_low, to_high):
        pack_x(fields, 1, read, to_low)
        pack_x(fields, -1, read, to_high)

    by_parity("gx", run, to_even, to_odd)


def send_y(fields, own, even_x, odd_x, to_even, to_odd):
    def with_halo(from_low, from_high):
        def run(to_low, to_high):
            pack_y(fields, 1, own, from_low, from_high, to_low)
            pack_y(fields, -1, own, from_low, from_high, to_high)

        by_parity("gy", run, to_even, to_odd)

    by_parity("gx", with_halo, even_x, odd_x)


def moments(f):
    v = list(f)
    for stride in (9, 3, 1):
        for i in range(27):
            if (i // stride) % 3 == 0:
                a, b, c = v[i], v[i + stride], v[i + 2 * stride]
                s = (a + c) + b
                v[i], v[i + stride], v[i + 2 * stride] = s, c - a, s - 3.0 * b
    return v


def moments_transposed(m):
    v = list(m)
    for stride in (9, 3, 1):
        for i in range(27):
            if (i // stride) % 3 == 0:
                s, d, q = v[i], v[i + stride], v[i + 2 * stride]
                t = s + q
                v[i], v[i + stride], v[i + 2 * stride] = t - d, s - (q + q), t + d
    return v


def rate_of(rates, i, relaxing, even, odd):
    return jnp.where(relaxing, rates[i], odd if ODD[i] else even)


def kinds_of(kind):
    relaxing = kind < 1.5
    even = jnp.where((kind > 1.5) & (kind < 3.5), 1.0, 0.0)
    odd = jnp.where(kind > 3.5, 2.0, even)
    return relaxing, even, odd


def collide(f, kappa, kind, rates, inlet):
    m = moments(f)
    relaxing, even, odd = kinds_of(kind)
    rho = m[0]
    inverse = 1.0 / rho
    ux, uy, uz = m[9] * inverse, m[3] * inverse, m[1] * inverse
    vx, vy = kappa * ux, kappa * uy
    vz = jnp.where((kind > 1.5) & (kind < 2.5), inlet, kappa * uz)
    den = jnp.where(relaxing, rho, 1.0)
    jx, jy, jz = den * vx, den * vy, den * vz
    xy, xz, yz = jx * vy, jx * vz, jy * vz
    xx, yy, zz = 3.0 * (jx * vx), 3.0 * (jy * vy), 3.0 * (jz * vz)
    x2, y2, z2 = xx - den, yy - den, zz - den
    e = [None] * 27
    e[0] = den
    e[18], e[6], e[2] = x2, y2, z2
    e[24], e[20], e[8] = -(x2 + yy), -(x2 + zz), -(y2 + zz)
    e[26] = (x2 + yy) + zz
    e[9], e[15], e[11], e[17] = jx, -jx, -jx, jx
    e[3], e[21], e[5], e[23] = jy, -jy, -jy, jy
    e[1], e[19], e[7], e[25] = jz, -jz, -jz, jz
    e[12], e[14] = xy, -xy
    e[10], e[16] = xz, -xz
    e[4], e[22] = yz, -yz
    out = []
    for i in range(27):
        rate = rate_of(rates, i, relaxing, even, odd)
        gap = -m[i] if e[i] is None else e[i] - m[i]
        out.append(SCALE[i] * (m[i] + rate * gap))
    return moments_transposed(out), (ux, uy, uz, inverse, rho)


def collide_back(h, kappa, kind, rates, speed, rho=None):
    y = moments(h)
    relaxing, even, odd = kinds_of(kind)
    ux, uy, uz, inverse = speed
    w, z = [], []
    for i in range(27):
        yi = SCALE[i] * y[i]
        wi = rate_of(rates, i, relaxing, even, odd) * yi
        w.append(wi)
        z.append(yi - wi)
    vx, vy, vz = kappa * ux, kappa * uy, kappa * uz
    w222 = w[26]
    a_x = (w[18] - w[24]) - (w[20] - w222)
    a_y = (w[6] - w[24]) - (w[8] - w222)
    a_z = (w[2] - w[20]) - (w[8] - w222)
    b_x = (w[9] - w[15]) - (w[11] - w[17])
    b_y = (w[3] - w[21]) - (w[5] - w[23])
    b_z = (w[1] - w[19]) - (w[7] - w[25])
    c_xy, c_xz, c_yz = w[12] - w[14], w[10] - w[16], w[4] - w[22]
    base = ((w[0] - w[18]) - (w[6] + w[2])) + ((w[24] + w[20]) + (w[8] - w222))
    p_x, p_y, p_z = 3.0 * (a_x * vx), 3.0 * (a_y * vy), 3.0 * (a_z * vz)
    q_x, q_y, q_z = c_xy * vy + c_xz * vz, c_xy * vx + c_yz * vz, c_xz * vx + c_yz * vy
    r_x, r_y, r_z = b_x + p_x, b_y + p_y, b_z + p_z
    value = base + vx * (r_x + 0.5 * q_x) + vy * (r_y + 0.5 * q_y) + vz * (r_z + 0.5 * q_z)
    g_x, g_y, g_z = r_x + p_x + q_x, r_y + p_y + q_y, r_z + p_z + q_z
    factor = jnp.where(relaxing, kappa, kappa * inverse)
    along = ux * g_x + uy * g_y + uz * g_z
    z[0] = z[0] + (jnp.where(relaxing, value, 0.0) - factor * along)
    z[9] = z[9] + factor * g_x
    z[3] = z[3] + factor * g_y
    z[1] = z[1] + factor * g_z
    return moments_transposed(z), None if rho is None else rho * along


def turned(value, shift):
    return value if shift == 0 else pltpu.roll(value, shift % LANES, axis=1)


def pulled(wide, plane, row, direction):
    tiles = []
    for i, (cx, cy, cz) in enumerate(VEL):
        tile = wide[i, plane - direction * cx, pl.ds(row - direction * cy, NY)]
        tiles.append(turned(tile, direction * cz))
    return tiles


def inlet_speed(start, step):
    time = jnp.full((NY, LANES), (start[0] + step) % PULSE_PERIOD, jnp.int32).astype(jnp.float32)
    return INLET_SPEED * jnp.sin(time * (2.0 * np.pi / PULSE_PERIOD))


def kappa_of(porosity, kind):
    damping = (RAMP_Q + porosity) / (
        RAMP_Q * (1.0 + DRAG_MAX) + (1.0 - DRAG_MAX * RAMP_Q) * porosity
    )
    return jnp.where(kind < 0.5, damping, jnp.where((kind > 2.5) & (kind < 3.5), 1.0, 0.0))


def first_kernel(
    rates, start, populations, cotangent, porosity, cell_type, post, cell, speed, to_even, to_odd,
    f, gamma, kinds, ends, sems,
):
    copies = [
        pltpu.make_async_copy(porosity, gamma, sems.at[0]),
        pltpu.make_async_copy(cell_type, kinds, sems.at[1]),
        pltpu.make_async_copy(populations, f, sems.at[2]),
        pltpu.make_async_copy(cotangent.at[18:27, 0], ends.at[0], sems.at[3]),
        pltpu.make_async_copy(cotangent.at[0:9, NX - 1], ends.at[1], sems.at[4]),
    ]
    for copy in copies:
        copy.start()
    inlet = inlet_speed(start, 0)
    for copy in copies:
        copy.wait()

    def plane_step(plane, carry):
        kind = kinds[plane].astype(jnp.float32)
        kappa = kappa_of(gamma[plane], kind)
        cell[0, plane] = kappa
        cell[1, plane] = kind
        out, values = collide([f[i, plane] for i in range(27)], kappa, kind, rates, inlet)
        for i in range(27):
            post[i, plane] = out[i]
        for i in range(5):
            speed[i, plane] = values[i]
        return carry

    lax.fori_loop(0, NX, plane_step, 0)

    def read(name, i, plane):
        if name == "adjoint":
            return ends[0, i - 18] if plane == 0 else ends[1, i]
        return {"post": post, "cell": cell}[name][i, plane]

    send_x(FIRST, read, to_even, to_odd)


def second_kernel(post, cotangent, cell, even_x, odd_x, to_even, to_odd):
    sources = {"post": post, "adjoint": cotangent, "cell": cell}

    def own(name, i, plane, first, rows):
        return sources[name][i, plane, first : first + rows]

    send_y(FIRST, own, even_x, odd_x, to_even, to_odd)


def third_kernel(
    rates, start, post, cotangent, cell, even_x, odd_x, even_y, odd_y,
    last_post, adjoint, wide_cell, speed_one, speed_two, gain, to_even, to_odd,
    wide_post, next_post, wide_adjoint,
):
    for i in range(27):
        wide_post[i, HALO : HALO + NX, NY : 2 * NY] = post[i]
        wide_adjoint[i, HALO : HALO + NX, NY : 2 * NY] = cotangent[i]
    for i in range(2):
        wide_cell[i, HALO : HALO + NX, NY : 2 * NY] = cell[i]
    wide = {"post": wide_post, "adjoint": wide_adjoint, "cell": wide_cell}
    unpack(FIRST, wide, even_x, odd_x, even_y, odd_y)

    def forward(step, source, target, speed, width):
        inlet = inlet_speed(start, step)

        def body(n, carry):
            plane = n // 2 + (HALO - width)
            row = (n % 2) * NY + NY // 2
            here = pl.ds(row, NY)
            f = pulled(source, plane, row, 1)
            out, values = collide(f, wide_cell[0, plane, here], wide_cell[1, plane, here], rates, inlet)
            for i in range(27):
                target[i, plane, here] = out[i]
            for i in range(5):
                speed[i, plane, here] = values[i]
            return carry

        lax.fori_loop(0, 2 * (NX + 2 * width), body, 0)

    forward(1, wide_post, next_post, speed_one, 2)
    forward(2, next_post, wide_post, speed_two, 1)
    inlet = inlet_speed(start, 3)

    def last(n, carry):
        plane = n + HALO
        here = pl.ds(NY, NY)
        kappa, kind = wide_cell[0, plane, here], wide_cell[1, plane, here]
        out, values = collide(pulled(wide_post, plane, NY, 1), kappa, kind, rates, inlet)
        for i in range(27):
            last_post[i, n] = out[i]
        back, grad = collide_back(
            pulled(wide_adjoint, plane, NY, -1), kappa, kind, rates, values[:4], values[4]
        )
        for i in range(27):
            adjoint[i, n] = back[i]
        gain[n] = grad
        return carry

    lax.fori_loop(0, NX, last, 0)

    def read(name, i, plane):
        if name == "speed":
            return speed_two[i, plane + HALO, NY : 2 * NY]
        return {"post": last_post, "adjoint": adjoint}[name][i, plane]

    send_x(SECOND, read, to_even, to_odd)


def fourth_kernel(post, adjoint, speed, even_x, odd_x, to_even, to_odd):
    def own(name, i, plane, first, rows):
        if name == "speed":
            return speed[i, plane + HALO, NY + first : NY + first + rows]
        return {"post": post, "adjoint": adjoint}[name][i, plane, first : first + rows]

    send_y(SECOND, own, even_x, odd_x, to_even, to_odd)


def fifth_kernel(
    rates, post, adjoint, wide_cell, speed_zero, speed_one, speed_two, gain, porosity,
    even_x, odd_x, even_y, odd_y,
    flow, first_adjoint, sensitivity,
    wide_post, wide_adjoint, next_adjoint, wide_speed, gains,
):
    for i in range(27):
        wide_post[i, HALO : HALO + NX, NY : 2 * NY] = post[i]
        wide_adjoint[i, HALO : HALO + NX, NY : 2 * NY] = adjoint[i]
    wide_speed[...] = speed_two[...]
    wide = {"post": wide_post, "adjoint": wide_adjoint, "speed": wide_speed}
    unpack(SECOND, wide, even_x, odd_x, even_y, odd_y)

    def back(source, target, speed, width, place):
        def body(n, carry):
            plane = n // 2 + (HALO - width)
            row = (n % 2) * NY + NY // 2
            here = pl.ds(row, NY)
            h = pulled(source, plane, row, -1)
            values = [speed[i, plane, here] for i in range(5)]
            out, grad = collide_back(
                h, wide_cell[0, plane, here], wide_cell[1, plane, here], rates, values[:4], values[4]
            )
            for i in range(27):
                target[i, plane, here] = out[i]
            gains[place, plane, here] = grad
            return carry

        lax.fori_loop(0, 2 * (NX + 2 * width), body, 0)

    back(wide_adjoint, next_adjoint, wide_speed, 2, 0)
    back(next_adjoint, wide_adjoint, speed_one, 1, 1)

    def last(n, carry):
        plane = n + HALO
        here = pl.ds(NY, NY)
        kappa, kind = wide_cell[0, plane, here], wide_cell[1, plane, here]
        values = [speed_zero[i, n] for i in range(5)]
        out, grad = collide_back(
            pulled(wide_adjoint, plane, NY, -1), kappa, kind, rates, values[:4], values[4]
        )
        for i in range(27):
            first_adjoint[i, n] = out[i]
        total = ((gain[n] + gains[0, plane, here]) + gains[1, plane, here]) + grad
        ramp = RAMP_Q * (1.0 + DRAG_MAX) + (1.0 - DRAG_MAX * RAMP_Q) * porosity[n]
        slope = (DRAG_MAX * RAMP_Q * (1.0 + RAMP_Q)) / (ramp * ramp)
        sensitivity[n] = jnp.where(kind < 0.5, slope * total, 0.0)
        tiles = pulled(wide_post, plane, NY, 1)
        for i in range(27):
            flow[i, n] = tiles[i]
        return carry

    lax.fori_loop(0, NX, last, 0)


def f32(*shape):
    return jax.ShapeDtypeStruct(shape, jnp.float32)


def call(kernel, scalars, arrays, outs, scratch=(), anywhere=False):
    smem = pl.BlockSpec(memory_space=pltpu.SMEM)
    vmem = pl.BlockSpec(memory_space=pltpu.VMEM)
    held = pl.BlockSpec(memory_space=pl.ANY) if anywhere else vmem
    return pl.pallas_call(
        kernel,
        out_shape=tuple(f32(*s) for s in outs),
        in_specs=[smem] * len(scalars) + [held] * len(arrays),
        out_specs=tuple(vmem for _ in outs),
        scratch_shapes=[pltpu.VMEM(s, jnp.float32) if isinstance(s, tuple) else s for s in scratch],
        compiler_params=pltpu.CompilerParams(vmem_limit_bytes=VMEM_LIMIT),
        name=kernel.__name__,
    )(*scalars, *arrays)


def partners(axis, first):
    count = lax.axis_size(axis)
    return [[i % count, (i + 1) % count] for i in range(first, count + first, 2)]


def swap(value, axis, first):
    pairs = partners(axis, first)
    return lax.ppermute(value, axis, [(a, b) for a, b in pairs] + [(b, a) for a, b in pairs])


def exchange_x(to_even, to_odd):
    from_odd = swap(to_odd, "gx", 1)
    return swap(to_even, "gx", 0), from_odd


def exchange_y(to_even, to_odd):
    from_odd = swap(to_odd, "gy", 1)
    return lax.all_gather(to_even, "gy", axis_index_groups=partners("gy", 0)), from_odd


def body(populations, cotangent, porosity, cell_type, rates, start_step):
    block = (27, NX, NY, LANES)
    wide = (27, PLANES, ROWS, LANES)
    tiles = (PLAN_X[FIRST, 1][1], NY, LANES), (PLAN_X[FIRST, -1][1], NY, LANES)
    rows = (PLAN_Y[FIRST, 1][1], LANES), (PLAN_Y[FIRST, -1][1], LANES)
    post, cell, speed_zero, to_even, to_odd = call(
        first_kernel, (rates, start_step), (populations, cotangent, porosity, cell_type),
        (block, (2, NX, NY, LANES), (5, NX, NY, LANES)) + tiles,
        (
            block, (NX, NY, LANES), pltpu.VMEM((NX, NY, LANES), jnp.int32), (2, 9, NY, LANES),
            pltpu.SemaphoreType.DMA((5,)),
        ),
        anywhere=True,
    )
    x_halos = exchange_x(to_even, to_odd)
    to_even, to_odd = call(second_kernel, (), (post, cotangent, cell) + x_halos, rows)
    y_halos = exchange_y(to_even, to_odd)
    wide_values = (5, PLANES, ROWS, LANES)
    tiles = (PLAN_X[SECOND, 1][1], NY, LANES), (PLAN_X[SECOND, -1][1], NY, LANES)
    rows = (PLAN_Y[SECOND, 1][1], LANES), (PLAN_Y[SECOND, -1][1], LANES)
    post, adjoint, wide_cell, speed_one, speed_two, gain, to_even, to_odd = call(
        third_kernel, (rates, start_step), (post, cotangent, cell) + x_halos + y_halos,
        (block, block, (2, PLANES, ROWS, LANES), wide_values, wide_values, (NX, NY, LANES)) + tiles,
        (wide, wide, wide),
    )
    x_halos = exchange_x(to_even, to_odd)
    to_even, to_odd = call(fourth_kernel, (), (post, adjoint, speed_two) + x_halos, rows)
    y_halos = exchange_y(to_even, to_odd)
    return call(
        fifth_kernel, (rates,),
        (post, adjoint, wide_cell, speed_zero, speed_one, speed_two, gain, porosity) + x_halos + y_halos,
        (block, block, (NX, NY, LANES)),
        (wide, wide, wide, wide_values, (2, PLANES, ROWS, LANES)),
    )


def solution(mesh):
    return jax.shard_map(
        body,
        mesh=mesh,
        in_specs=(
            P(None, "gx", "gy", None),
            P(None, "gx", "gy", None),
            P("gx", "gy", None),
            P("gx", "gy", None),
            P(),
            P(),
        ),
        out_specs=(P(None, "gx", "gy", None), P(None, "gx", "gy", None), P("gx", "gy", None)),
        check_vma=False,
    )
```

```python
import jax
import jax.numpy as jnp
import numpy as np
from jax import lax
from jax.experimental import pallas as pl
from jax.experimental.pallas import tpu as pltpu
from jax.sharding import PartitionSpec as P

DRAG_MAX = 1.0
RAMP_Q = 0.1
INLET_SPEED = 0.3
PULSE_PERIOD = 64

NX, NY, LANES = 4, 8, 128
HALO = 3
PLANES = NX + 2 * HALO
ROWS = 3 * NY
VMEM_LIMIT = 48 * 1024 * 1024

SCALE = [
    float(s)
    for s in np.kron(np.kron([1 / 3, 1 / 2, 1 / 6], [1 / 3, 1 / 2, 1 / 6]), [1 / 3, 1 / 2, 1 / 6])
]
VEL = [(a - 1, b - 1, d - 1) for a in range(3) for b in range(3) for d in range(3)]
ODD = [(c[0] == 0) ^ (c[1] == 0) ^ (c[2] == 0) for c in VEL]


def reach(component, side, width, direction):
    if direction in (0, 2):
        return width
    inward = -side * direction
    return max(0, width - (0 if component == inward else 1 if component == 0 else 2))


def member_reach(field, i, axis, side):
    _, _, width, direction = field
    return reach(VEL[i][axis] if abs(direction) == 1 else 0, side, width, direction)


def first_layer(field):
    return field[2] if field[3] == 2 else 1


def plan_x(fields, side):
    places = {}
    for field in fields:
        for layer in range(first_layer(field), field[2] + 1):
            for i in range(field[1]):
                if member_reach(field, i, 0, side) >= layer:
                    places[field[0], i, layer] = len(places)
    return places, len(places)


def plan_y(fields, side):
    entries, start = [], 0
    for field in fields:
        for plane in range(-field[2], NX + field[2]):
            for i in range(field[1]):
                if plane < 0 and member_reach(field, i, 0, -1) < -plane:
                    continue
                if plane >= NX and member_reach(field, i, 0, 1) < plane - NX + 1:
                    continue
                rows = member_reach(field, i, 1, side)
                skip = first_layer(field) - 1 if -field[2] < plane < NX + field[2] - 1 else 0
                if rows > skip:
                    entries.append((field[0], i, plane, start, skip, rows - skip))
                    start += rows - skip
    return entries, -(-start // 8) * 8


FIRST = (("post", 27, 3, 1), ("adjoint", 27, 1, -1), ("cell", 2, 2, 0))
SECOND = (("adjoint", 27, 3, -1), ("post", 27, 1, 1), ("speed", 4, 2, 2))
PLAN_X = {(f, s): plan_x(f, s) for f in (FIRST, SECOND) for s in (-1, 1)}
PLAN_Y = {(f, s): plan_y(f, s) for f in (FIRST, SECOND) for s in (-1, 1)}


def pack_x(fields, side, read, out):
    for (name, i, layer), place in PLAN_X[fields, side][0].items():
        out[place] = read(name, i, layer - 1 if side > 0 else NX - layer)


def halo_tile(fields, from_low, from_high, name, i, plane):
    if plane < 0:
        return from_low, PLAN_X[fields, -1][0][name, i, -plane]
    return from_high, PLAN_X[fields, 1][0][name, i, plane - NX + 1]


def pack_y(fields, side, own, from_low, from_high, out):
    for name, i, plane, start, skip, rows in PLAN_Y[fields, side][0]:
        first = skip if side > 0 else NY - skip - rows
        if 0 <= plane < NX or (name == "speed" and -2 < plane < NX + 1):
            out[start : start + rows] = own(name, i, plane, first, rows)
        else:
            ref, place = halo_tile(fields, from_low, from_high, name, i, plane)
            out[start : start + rows] = ref[place, first : first + rows]


def by_parity(axis, run, from_odd, from_even):
    parity = lax.axis_index(axis) % 2

    @pl.when(parity == 0)
    def _():
        run(from_odd, from_even)

    @pl.when(parity == 1)
    def _():
        run(from_even, from_odd)


def unpack_x(fields, wide, *from_x):
    for side, ref in zip((-1, 1), from_x):
        for (name, i, layer), place in PLAN_X[fields, side][0].items():
            plane = NX - 1 + layer if side > 0 else -layer
            wide[name][i, plane + HALO, NY : 2 * NY] = ref[place]


def unpack_y(fields, wide, *from_y):
    for side, ref in zip((-1, 1), from_y):
        for name, i, plane, start, skip, rows in PLAN_Y[fields, side][0]:
            first = 2 * NY + skip if side > 0 else NY - skip - rows
            wide[name][i, plane + HALO, first : first + rows] = ref[start : start + rows]


def unpack(fields, wide, odd_x, even_x, odd_y, even_y):
    by_parity("gx", lambda low, high: unpack_x(fields, wide, low, high), odd_x, even_x)
    partner = even_y.at[1 - lax.axis_index("gy") % 2]
    by_parity("gy", lambda low, high: unpack_y(fields, wide, low, high), odd_y, partner)


def send_x(fields, read, to_odd, to_even):
    def run(to_low, to_high):
        pack_x(fields, 1, read, to_low)
        pack_x(fields, -1, read, to_high)

    by_parity("gx", run, to_odd, to_even)


def send_y(fields, own, odd_x, even_x, to_odd, to_even):
    def with_halo(from_low, from_high):
        def run(to_low, to_high):
            pack_y(fields, 1, own, from_low, from_high, to_low)
            pack_y(fields, -1, own, from_low, from_high, to_high)

        by_parity("gy", run, to_odd, to_even)

    by_parity("gx", with_halo, odd_x, even_x)


def moments(f):
    v = list(f)
    for stride in (9, 3, 1):
        for i in range(27):
            if (i // stride) % 3 == 0:
                a, b, c = v[i], v[i + stride], v[i + 2 * stride]
                s = (a + c) + b
                v[i], v[i + stride], v[i + 2 * stride] = s, c - a, s - 3.0 * b
    return v


def moments_transposed(m):
    v = list(m)
    for stride in (9, 3, 1):
        for i in range(27):
            if (i // stride) % 3 == 0:
                s, d, q = v[i], v[i + stride], v[i + 2 * stride]
                t = s + q
                v[i], v[i + stride], v[i + 2 * stride] = t - d, s - (q + q), t + d
    return v


def rate_of(rates, i, relaxing, even, odd):
    return jnp.where(relaxing, rates[i], odd if ODD[i] else even)


def kinds_of(kind):
    relaxing = kind < 1.5
    even = jnp.where((kind > 1.5) & (kind < 3.5), 1.0, 0.0)
    odd = jnp.where(kind > 3.5, 2.0, even)
    return relaxing, even, odd


def collide(f, kappa, kind, rates, inlet):
    m = moments(f)
    relaxing, even, odd = kinds_of(kind)
    rho = m[0]
    inverse = 1.0 / rho
    ux, uy, uz = m[9] * inverse, m[3] * inverse, m[1] * inverse
    vx, vy = kappa * ux, kappa * uy
    vz = jnp.where((kind > 1.5) & (kind < 2.5), inlet, kappa * uz)
    den = jnp.where(relaxing, rho, 1.0)
    jx, jy, jz = den * vx, den * vy, den * vz
    xy, xz, yz = jx * vy, jx * vz, jy * vz
    xx, yy, zz = 3.0 * (jx * vx), 3.0 * (jy * vy), 3.0 * (jz * vz)
    x2, y2, z2 = xx - den, yy - den, zz - den
    e = [None] * 27
    e[0] = den
    e[18], e[6], e[2] = x2, y2, z2
    e[24], e[20], e[8] = -(x2 + yy), -(x2 + zz), -(y2 + zz)
    e[26] = (x2 + yy) + zz
    e[9], e[15], e[11], e[17] = jx, -jx, -jx, jx
    e[3], e[21], e[5], e[23] = jy, -jy, -jy, jy
    e[1], e[19], e[7], e[25] = jz, -jz, -jz, jz
    e[12], e[14] = xy, -xy
    e[10], e[16] = xz, -xz
    e[4], e[22] = yz, -yz
    out = []
    for i in range(27):
        rate = rate_of(rates, i, relaxing, even, odd)
        gap = -m[i] if e[i] is None else e[i] - m[i]
        out.append(SCALE[i] * (m[i] + rate * gap))
    return moments_transposed(out), (ux, uy, uz, inverse, rho)


def collide_back(h, kappa, kind, rates, speed, rho=None):
    y = moments(h)
    relaxing, even, odd = kinds_of(kind)
    ux, uy, uz, inverse = speed
    w, z = [], []
    for i in range(27):
        yi = SCALE[i] * y[i]
        wi = rate_of(rates, i, relaxing, even, odd) * yi
        w.append(wi)
        z.append(yi - wi)
    vx, vy, vz = kappa * ux, kappa * uy, kappa * uz
    w222 = w[26]
    a_x = (w[18] - w[24]) - (w[20] - w222)
    a_y = (w[6] - w[24]) - (w[8] - w222)
    a_z = (w[2] - w[20]) - (w[8] - w222)
    b_x = (w[9] - w[15]) - (w[11] - w[17])
    b_y = (w[3] - w[21]) - (w[5] - w[23])
    b_z = (w[1] - w[19]) - (w[7] - w[25])
    c_xy, c_xz, c_yz = w[12] - w[14], w[10] - w[16], w[4] - w[22]
    base = ((w[0] - w[18]) - (w[6] + w[2])) + ((w[24] + w[20]) + (w[8] - w222))
    p_x, p_y, p_z = 3.0 * (a_x * vx), 3.0 * (a_y * vy), 3.0 * (a_z * vz)
    q_x, q_y, q_z = c_xy * vy + c_xz * vz, c_xy * vx + c_yz * vz, c_xz * vx + c_yz * vy
    r_x, r_y, r_z = b_x + p_x, b_y + p_y, b_z + p_z
    value = base + vx * (r_x + 0.5 * q_x) + vy * (r_y + 0.5 * q_y) + vz * (r_z + 0.5 * q_z)
    g_x, g_y, g_z = r_x + p_x + q_x, r_y + p_y + q_y, r_z + p_z + q_z
    factor = jnp.where(relaxing, kappa, kappa * inverse)
    along = ux * g_x + uy * g_y + uz * g_z
    z[0] = z[0] + (jnp.where(relaxing, value, 0.0) - factor * along)
    z[9] = z[9] + factor * g_x
    z[3] = z[3] + factor * g_y
    z[1] = z[1] + factor * g_z
    return moments_transposed(z), None if rho is None else rho * along


def turned(value, shift):
    return value if shift == 0 else pltpu.roll(value, shift % LANES, axis=1)


def pulled(wide, plane, row, direction):
    tiles = []
    for i, (cx, cy, cz) in enumerate(VEL):
        tile = wide[i, plane - direction * cx, pl.ds(row - direction * cy, NY)]
        tiles.append(turned(tile, direction * cz))
    return tiles


def inlet_speed(start, step):
    time = jnp.full((NY, LANES), (start[0] + step) % PULSE_PERIOD, jnp.int32).astype(jnp.float32)
    return INLET_SPEED * jnp.sin(time * (2.0 * np.pi / PULSE_PERIOD))


def kappa_of(porosity, kind):
    damping = (RAMP_Q + porosity) / (
        RAMP_Q * (1.0 + DRAG_MAX) + (1.0 - DRAG_MAX * RAMP_Q) * porosity
    )
    return jnp.where(kind < 0.5, damping, jnp.where((kind > 2.5) & (kind < 3.5), 1.0, 0.0))


def first_kernel(
    rates_hbm, start_hbm, populations, cotangent, porosity, cell_type,
    post, held, gamma, cell, speed, to_odd, to_even,
    rates, start, f, kinds, sems,
):
    copies = [
        pltpu.make_async_copy(source, target, sems.at[n])
        for n, (source, target) in enumerate(
            (
                (rates_hbm, rates), (start_hbm, start), (porosity, gamma), (cell_type, kinds),
                (populations, f), (cotangent, held),
            )
        )
    ]
    for copy in copies:
        copy.start()
    for copy in copies[:5]:
        copy.wait()
    inlet = inlet_speed(start, 0)

    def plane_step(plane, carry):
        kind = kinds[plane].astype(jnp.float32)
        kappa = kappa_of(gamma[plane], kind)
        cell[0, plane] = kappa
        cell[1, plane] = kind
        out, values = collide([f[i, plane] for i in range(27)], kappa, kind, rates, inlet)
        for i in range(27):
            post[i, plane] = out[i]
        for i in range(5):
            speed[i, plane] = values[i]
        return carry

    lax.fori_loop(0, NX, plane_step, 0)
    copies[5].wait()

    def read(name, i, plane):
        return {"post": post, "adjoint": held, "cell": cell}[name][i, plane]

    send_x(FIRST, read, to_odd, to_even)


def second_kernel(post, cotangent, cell, odd_x, even_x, to_odd, to_even):
    sources = {"post": post, "adjoint": cotangent, "cell": cell}

    def own(name, i, plane, first, rows):
        return sources[name][i, plane, first : first + rows]

    send_y(FIRST, own, odd_x, even_x, to_odd, to_even)


def third_kernel(
    rates_hbm, start_hbm, post, cotangent, cell, odd_x, even_x, odd_y, even_y,
    last_post, adjoint, wide_cell, speed_one, speed_two, gain, to_odd, to_even,
    wide_post, next_post, wide_adjoint, rates, start, sems,
):
    copies = [
        pltpu.make_async_copy(rates_hbm, rates, sems.at[0]),
        pltpu.make_async_copy(start_hbm, start, sems.at[1]),
    ]
    for copy in copies:
        copy.start()
    for i in range(27):
        wide_post[i, HALO : HALO + NX, NY : 2 * NY] = post[i]
        wide_adjoint[i, HALO : HALO + NX, NY : 2 * NY] = cotangent[i]
    for i in range(2):
        wide_cell[i, HALO : HALO + NX, NY : 2 * NY] = cell[i]
    wide = {"post": wide_post, "adjoint": wide_adjoint, "cell": wide_cell}
    unpack(FIRST, wide, odd_x, even_x, odd_y, even_y)
    for copy in copies:
        copy.wait()

    def forward(step, source, target, speed, width):
        inlet = inlet_speed(start, step)

        def body(n, carry):
            plane = n // 2 + (HALO - width)
            row = (n % 2) * NY + NY // 2
            here = pl.ds(row, NY)
            f = pulled(source, plane, row, 1)
            out, values = collide(f, wide_cell[0, plane, here], wide_cell[1, plane, here], rates, inlet)
            for i in range(27):
                target[i, plane, here] = out[i]
            for i in range(5):
                speed[i, plane, here] = values[i]
            return carry

        lax.fori_loop(0, 2 * (NX + 2 * width), body, 0)

    forward(1, wide_post, next_post, speed_one, 2)
    forward(2, next_post, wide_post, speed_two, 1)
    inlet = inlet_speed(start, 3)

    def last(n, carry):
        plane = n + HALO
        here = pl.ds(NY, NY)
        kappa, kind = wide_cell[0, plane, here], wide_cell[1, plane, here]
        out, values = collide(pulled(wide_post, plane, NY, 1), kappa, kind, rates, inlet)
        for i in range(27):
            last_post[i, n] = out[i]
        back, grad = collide_back(
            pulled(wide_adjoint, plane, NY, -1), kappa, kind, rates, values[:4], values[4]
        )
        for i in range(27):
            adjoint[i, n] = back[i]
        gain[n] = grad
        return carry

    lax.fori_loop(0, NX, last, 0)

    def read(name, i, plane):
        if name == "speed":
            return speed_two[i, plane + HALO, NY : 2 * NY]
        return {"post": last_post, "adjoint": adjoint}[name][i, plane]

    send_x(SECOND, read, to_odd, to_even)


def fourth_kernel(post, adjoint, speed, odd_x, even_x, to_odd, to_even):
    def own(name, i, plane, first, rows):
        if name == "speed":
            return speed[i, plane + HALO, NY + first : NY + first + rows]
        return {"post": post, "adjoint": adjoint}[name][i, plane, first : first + rows]

    send_y(SECOND, own, odd_x, even_x, to_odd, to_even)


def fifth_kernel(
    rates_hbm, post, adjoint, wide_cell, speed_zero, speed_one, speed_two, gain, porosity,
    odd_x, even_x, odd_y, even_y,
    flow, first_adjoint, sensitivity,
    wide_post, wide_adjoint, next_adjoint, wide_speed, gains, rates, sem,
):
    copy = pltpu.make_async_copy(rates_hbm, rates, sem)
    copy.start()
    for i in range(27):
        wide_post[i, HALO : HALO + NX, NY : 2 * NY] = post[i]
        wide_adjoint[i, HALO : HALO + NX, NY : 2 * NY] = adjoint[i]
    wide_speed[...] = speed_two[...]
    wide = {"post": wide_post, "adjoint": wide_adjoint, "speed": wide_speed}
    unpack(SECOND, wide, odd_x, even_x, odd_y, even_y)
    copy.wait()

    def back(source, target, speed, width, place):
        def body(n, carry):
            plane = n // 2 + (HALO - width)
            row = (n % 2) * NY + NY // 2
            here = pl.ds(row, NY)
            h = pulled(source, plane, row, -1)
            values = [speed[i, plane, here] for i in range(5)]
            out, grad = collide_back(
                h, wide_cell[0, plane, here], wide_cell[1, plane, here], rates, values[:4], values[4]
            )
            for i in range(27):
                target[i, plane, here] = out[i]
            gains[place, plane, here] = grad
            return carry

        lax.fori_loop(0, 2 * (NX + 2 * width), body, 0)

    back(wide_adjoint, next_adjoint, wide_speed, 2, 0)
    back(next_adjoint, wide_adjoint, speed_one, 1, 1)

    def last(n, carry):
        plane = n + HALO
        here = pl.ds(NY, NY)
        kappa, kind = wide_cell[0, plane, here], wide_cell[1, plane, here]
        values = [speed_zero[i, n] for i in range(5)]
        out, grad = collide_back(
            pulled(wide_adjoint, plane, NY, -1), kappa, kind, rates, values[:4], values[4]
        )
        for i in range(27):
            first_adjoint[i, n] = out[i]
        total = ((gain[n] + gains[0, plane, here]) + gains[1, plane, here]) + grad
        ramp = RAMP_Q * (1.0 + DRAG_MAX) + (1.0 - DRAG_MAX * RAMP_Q) * porosity[n]
        slope = (DRAG_MAX * RAMP_Q * (1.0 + RAMP_Q)) / (ramp * ramp)
        sensitivity[n] = jnp.where(kind < 0.5, slope * total, 0.0)
        tiles = pulled(wide_post, plane, NY, 1)
        for i in range(27):
            flow[i, n] = tiles[i]
        return carry

    lax.fori_loop(0, NX, last, 0)


def f32(*shape):
    return jax.ShapeDtypeStruct(shape, jnp.float32)


def call(kernel, far, arrays, outs, scratch=()):
    hbm = pl.BlockSpec(memory_space=pltpu.HBM)
    vmem = pl.BlockSpec(memory_space=pltpu.VMEM)
    return pl.pallas_call(
        kernel,
        out_shape=tuple(f32(*s) for s in outs),
        in_specs=[hbm] * len(far) + [vmem] * len(arrays),
        out_specs=tuple(vmem for _ in outs),
        scratch_shapes=[pltpu.VMEM(s, jnp.float32) if isinstance(s, tuple) else s for s in scratch],
        compiler_params=pltpu.CompilerParams(vmem_limit_bytes=VMEM_LIMIT),
        name=kernel.__name__,
    )(*far, *arrays)


def partners(axis, first):
    count = lax.axis_size(axis)
    return [[i % count, (i + 1) % count] for i in range(first, count + first, 2)]


def swap(value, axis, first):
    pairs = partners(axis, first)
    return lax.ppermute(value, axis, [(a, b) for a, b in pairs] + [(b, a) for a, b in pairs])


def exchange_x(to_odd, to_even):
    return swap(to_odd, "gx", 1), swap(to_even, "gx", 0)


def exchange_y(to_odd, to_even):
    from_odd = swap(to_odd, "gy", 1)
    return from_odd, lax.all_gather(to_even, "gy", axis_index_groups=partners("gy", 0))


def body(populations, cotangent, porosity, cell_type, rates, start_step):
    block = (27, NX, NY, LANES)
    wide = (27, PLANES, ROWS, LANES)
    tiles = (PLAN_X[FIRST, 1][1], NY, LANES), (PLAN_X[FIRST, -1][1], NY, LANES)
    rows = (PLAN_Y[FIRST, 1][1], LANES), (PLAN_Y[FIRST, -1][1], LANES)
    rates_here, start_here = pltpu.SMEM((27,), jnp.float32), pltpu.SMEM((1,), jnp.int32)
    post, held, gamma, cell, speed_zero, to_odd, to_even = call(
        first_kernel, (rates, start_step, populations, cotangent, porosity, cell_type), (),
        (block, block, (NX, NY, LANES), (2, NX, NY, LANES), (5, NX, NY, LANES)) + tiles,
        (
            rates_here, start_here, block, pltpu.VMEM((NX, NY, LANES), jnp.int32),
            pltpu.SemaphoreType.DMA((6,)),
        ),
    )
    x_halos = exchange_x(to_odd, to_even)
    to_odd, to_even = call(second_kernel, (), (post, held, cell) + x_halos, rows)
    y_halos = exchange_y(to_odd, to_even)
    wide_values = (5, PLANES, ROWS, LANES)
    tiles = (PLAN_X[SECOND, 1][1], NY, LANES), (PLAN_X[SECOND, -1][1], NY, LANES)
    rows = (PLAN_Y[SECOND, 1][1], LANES), (PLAN_Y[SECOND, -1][1], LANES)
    post, adjoint, wide_cell, speed_one, speed_two, gain, to_odd, to_even = call(
        third_kernel, (rates, start_step), (post, held, cell) + x_halos + y_halos,
        (block, block, (2, PLANES, ROWS, LANES), wide_values, wide_values, (NX, NY, LANES)) + tiles,
        (wide, wide, wide, rates_here, start_here, pltpu.SemaphoreType.DMA((2,))),
    )
    x_halos = exchange_x(to_odd, to_even)
    to_odd, to_even = call(fourth_kernel, (), (post, adjoint, speed_two) + x_halos, rows)
    y_halos = exchange_y(to_odd, to_even)
    return call(
        fifth_kernel, (rates,),
        (post, adjoint, wide_cell, speed_zero, speed_one, speed_two, gain, gamma) + x_halos + y_halos,
        (block, block, (NX, NY, LANES)),
        (wide, wide, wide, wide_values, (2, PLANES, ROWS, LANES), rates_here, pltpu.SemaphoreType.DMA(())),
    )


def solution(mesh):
    return jax.shard_map(
        body,
        mesh=mesh,
        in_specs=(
            P(None, "gx", "gy", None),
            P(None, "gx", "gy", None),
            P("gx", "gy", None),
            P("gx", "gy", None),
            P(),
            P(),
        ),
        out_specs=(P(None, "gx", "gy", None), P(None, "gx", "gy", None), P("gx", "gy", None)),
        check_vma=False,
    )
```

```python
import jax
import jax.numpy as jnp
import numpy as np
from jax import lax
from jax.experimental import pallas as pl
from jax.experimental.pallas import tpu as pltpu
from jax.sharding import PartitionSpec as P

DRAG_MAX = 1.0
RAMP_Q = 0.1
INLET_SPEED = 0.3
PULSE_PERIOD = 64

NX, NY, LANES = 4, 8, 128
HALO = 3
PLANES = NX + 2 * HALO
ROWS = 3 * NY
VMEM_LIMIT = 48 * 1024 * 1024
FIRST_LIMIT = 64 * 1024 * 1024

SCALE = [
    float(s)
    for s in np.kron(np.kron([1 / 3, 1 / 2, 1 / 6], [1 / 3, 1 / 2, 1 / 6]), [1 / 3, 1 / 2, 1 / 6])
]
VEL = [(a - 1, b - 1, d - 1) for a in range(3) for b in range(3) for d in range(3)]
ODD = [(c[0] == 0) ^ (c[1] == 0) ^ (c[2] == 0) for c in VEL]


def reach(component, side, width, direction):
    if direction in (0, 2):
        return width
    inward = -side * direction
    return max(0, width - (0 if component == inward else 1 if component == 0 else 2))


def member_reach(field, i, axis, side):
    _, _, width, direction = field
    return reach(VEL[i][axis] if abs(direction) == 1 else 0, side, width, direction)


def first_layer(field):
    return field[2] if field[3] == 2 else 1


def plan_x(fields, side):
    places = {}
    for field in fields:
        for layer in range(first_layer(field), field[2] + 1):
            for i in range(field[1]):
                if member_reach(field, i, 0, side) >= layer:
                    places[field[0], i, layer] = len(places)
    return places, len(places)


def plan_y(fields, side):
    entries, start = [], 0
    for field in fields:
        for plane in range(-field[2], NX + field[2]):
            for i in range(field[1]):
                if plane < 0 and member_reach(field, i, 0, -1) < -plane:
                    continue
                if plane >= NX and member_reach(field, i, 0, 1) < plane - NX + 1:
                    continue
                rows = member_reach(field, i, 1, side)
                skip = first_layer(field) - 1 if -field[2] < plane < NX + field[2] - 1 else 0
                if rows > skip:
                    entries.append((field[0], i, plane, start, skip, rows - skip))
                    start += rows - skip
    return entries, -(-start // 8) * 8


FIRST = (("post", 27, 3, 1), ("adjoint", 27, 1, -1), ("cell", 2, 2, 0))
SECOND = (("adjoint", 27, 3, -1), ("post", 27, 1, 1), ("speed", 4, 2, 2))
PLAN_X = {(f, s): plan_x(f, s) for f in (FIRST, SECOND) for s in (-1, 1)}
PLAN_Y = {(f, s): plan_y(f, s) for f in (FIRST, SECOND) for s in (-1, 1)}


def pack_x(fields, side, read, out):
    for (name, i, layer), place in PLAN_X[fields, side][0].items():
        out[place] = read(name, i, layer - 1 if side > 0 else NX - layer)


def halo_tile(fields, from_low, from_high, name, i, plane):
    if plane < 0:
        return from_low, PLAN_X[fields, -1][0][name, i, -plane]
    return from_high, PLAN_X[fields, 1][0][name, i, plane - NX + 1]


def pack_y(fields, side, own, from_low, from_high, out):
    for name, i, plane, start, skip, rows in PLAN_Y[fields, side][0]:
        first = skip if side > 0 else NY - skip - rows
        if 0 <= plane < NX or (name == "speed" and -2 < plane < NX + 1):
            out[start : start + rows] = own(name, i, plane, first, rows)
        else:
            ref, place = halo_tile(fields, from_low, from_high, name, i, plane)
            out[start : start + rows] = ref[place, first : first + rows]


def by_parity(axis, run, from_odd, from_even):
    parity = lax.axis_index(axis) % 2

    @pl.when(parity == 0)
    def _():
        run(from_odd, from_even)

    @pl.when(parity == 1)
    def _():
        run(from_even, from_odd)


def unpack_x(fields, wide, *from_x):
    for side, ref in zip((-1, 1), from_x):
        for (name, i, layer), place in PLAN_X[fields, side][0].items():
            plane = NX - 1 + layer if side > 0 else -layer
            wide[name][i, plane + HALO, NY : 2 * NY] = ref[place]


def unpack_y(fields, wide, *from_y):
    for side, ref in zip((-1, 1), from_y):
        for name, i, plane, start, skip, rows in PLAN_Y[fields, side][0]:
            first = 2 * NY + skip if side > 0 else NY - skip - rows
            wide[name][i, plane + HALO, first : first + rows] = ref[start : start + rows]


def unpack(fields, wide, odd_x, even_x, odd_y, even_y):
    by_parity("gx", lambda low, high: unpack_x(fields, wide, low, high), odd_x, even_x)
    partner = even_y.at[1 - lax.axis_index("gy") % 2]
    by_parity("gy", lambda low, high: unpack_y(fields, wide, low, high), odd_y, partner)


def send_x(fields, read, to_odd, to_even):
    def run(to_low, to_high):
        pack_x(fields, 1, read, to_low)
        pack_x(fields, -1, read, to_high)

    by_parity("gx", run, to_odd, to_even)


def send_y(fields, own, odd_x, even_x, to_odd, to_even):
    def with_halo(from_low, from_high):
        def run(to_low, to_high):
            pack_y(fields, 1, own, from_low, from_high, to_low)
            pack_y(fields, -1, own, from_low, from_high, to_high)

        by_parity("gy", run, to_odd, to_even)

    by_parity("gx", with_halo, odd_x, even_x)


def moments(f):
    v = list(f)
    for stride in (9, 3, 1):
        for i in range(27):
            if (i // stride) % 3 == 0:
                a, b, c = v[i], v[i + stride], v[i + 2 * stride]
                s = (a + c) + b
                v[i], v[i + stride], v[i + 2 * stride] = s, c - a, s - 3.0 * b
    return v


def moments_transposed(m):
    v = list(m)
    for stride in (9, 3, 1):
        for i in range(27):
            if (i // stride) % 3 == 0:
                s, d, q = v[i], v[i + stride], v[i + 2 * stride]
                t = s + q
                v[i], v[i + stride], v[i + 2 * stride] = t - d, s - (q + q), t + d
    return v


def rate_of(rates, i, relaxing, even, odd):
    return jnp.where(relaxing, rates[i], odd if ODD[i] else even)


def kinds_of(kind):
    relaxing = kind < 1.5
    even = jnp.where((kind > 1.5) & (kind < 3.5), 1.0, 0.0)
    odd = jnp.where(kind > 3.5, 2.0, even)
    return relaxing, even, odd


def collide(f, kappa, kind, rates, inlet):
    m = moments(f)
    relaxing, even, odd = kinds_of(kind)
    rho = m[0]
    inverse = 1.0 / rho
    ux, uy, uz = m[9] * inverse, m[3] * inverse, m[1] * inverse
    vx, vy = kappa * ux, kappa * uy
    vz = jnp.where((kind > 1.5) & (kind < 2.5), inlet, kappa * uz)
    den = jnp.where(relaxing, rho, 1.0)
    jx, jy, jz = den * vx, den * vy, den * vz
    xy, xz, yz = jx * vy, jx * vz, jy * vz
    xx, yy, zz = 3.0 * (jx * vx), 3.0 * (jy * vy), 3.0 * (jz * vz)
    x2, y2, z2 = xx - den, yy - den, zz - den
    e = [None] * 27
    e[0] = den
    e[18], e[6], e[2] = x2, y2, z2
    e[24], e[20], e[8] = -(x2 + yy), -(x2 + zz), -(y2 + zz)
    e[26] = (x2 + yy) + zz
    e[9], e[15], e[11], e[17] = jx, -jx, -jx, jx
    e[3], e[21], e[5], e[23] = jy, -jy, -jy, jy
    e[1], e[19], e[7], e[25] = jz, -jz, -jz, jz
    e[12], e[14] = xy, -xy
    e[10], e[16] = xz, -xz
    e[4], e[22] = yz, -yz
    out = []
    for i in range(27):
        rate = rate_of(rates, i, relaxing, even, odd)
        gap = -m[i] if e[i] is None else e[i] - m[i]
        out.append(SCALE[i] * (m[i] + rate * gap))
    return moments_transposed(out), (ux, uy, uz, inverse, rho)


def collide_back(h, kappa, kind, rates, speed, rho=None):
    y = moments(h)
    relaxing, even, odd = kinds_of(kind)
    ux, uy, uz, inverse = speed
    w, z = [], []
    for i in range(27):
        yi = SCALE[i] * y[i]
        wi = rate_of(rates, i, relaxing, even, odd) * yi
        w.append(wi)
        z.append(yi - wi)
    vx, vy, vz = kappa * ux, kappa * uy, kappa * uz
    w222 = w[26]
    a_x = (w[18] - w[24]) - (w[20] - w222)
    a_y = (w[6] - w[24]) - (w[8] - w222)
    a_z = (w[2] - w[20]) - (w[8] - w222)
    b_x = (w[9] - w[15]) - (w[11] - w[17])
    b_y = (w[3] - w[21]) - (w[5] - w[23])
    b_z = (w[1] - w[19]) - (w[7] - w[25])
    c_xy, c_xz, c_yz = w[12] - w[14], w[10] - w[16], w[4] - w[22]
    base = ((w[0] - w[18]) - (w[6] + w[2])) + ((w[24] + w[20]) + (w[8] - w222))
    p_x, p_y, p_z = 3.0 * (a_x * vx), 3.0 * (a_y * vy), 3.0 * (a_z * vz)
    q_x, q_y, q_z = c_xy * vy + c_xz * vz, c_xy * vx + c_yz * vz, c_xz * vx + c_yz * vy
    r_x, r_y, r_z = b_x + p_x, b_y + p_y, b_z + p_z
    value = base + vx * (r_x + 0.5 * q_x) + vy * (r_y + 0.5 * q_y) + vz * (r_z + 0.5 * q_z)
    g_x, g_y, g_z = r_x + p_x + q_x, r_y + p_y + q_y, r_z + p_z + q_z
    factor = jnp.where(relaxing, kappa, kappa * inverse)
    along = ux * g_x + uy * g_y + uz * g_z
    z[0] = z[0] + (jnp.where(relaxing, value, 0.0) - factor * along)
    z[9] = z[9] + factor * g_x
    z[3] = z[3] + factor * g_y
    z[1] = z[1] + factor * g_z
    return moments_transposed(z), None if rho is None else rho * along


def turned(value, shift):
    return value if shift == 0 else pltpu.roll(value, shift % LANES, axis=1)


def pulled(wide, plane, row, direction):
    tiles = []
    for i, (cx, cy, cz) in enumerate(VEL):
        tile = wide[i, plane - direction * cx, pl.ds(row - direction * cy, NY)]
        tiles.append(turned(tile, direction * cz))
    return tiles


def inlet_speed(start, step):
    time = jnp.full((NY, LANES), (start[0] + step) % PULSE_PERIOD, jnp.int32).astype(jnp.float32)
    return INLET_SPEED * jnp.sin(time * (2.0 * np.pi / PULSE_PERIOD))


def kappa_of(porosity, kind):
    damping = (RAMP_Q + porosity) / (
        RAMP_Q * (1.0 + DRAG_MAX) + (1.0 - DRAG_MAX * RAMP_Q) * porosity
    )
    return jnp.where(kind < 0.5, damping, jnp.where((kind > 2.5) & (kind < 3.5), 1.0, 0.0))


def first_kernel(
    rates_hbm, start_hbm, populations, cotangent, porosity, cell_type,
    post, cell, speed, to_odd, to_even,
    rates, start, f, gamma, kinds, ends, sems,
):
    copies = [
        pltpu.make_async_copy(source, target, sems.at[n])
        for n, (source, target) in enumerate(
            (
                (rates_hbm, rates), (start_hbm, start), (porosity, gamma), (cell_type, kinds),
                (populations, f), (cotangent.at[18:27, 0], ends.at[0]), (cotangent.at[0:9, NX - 1], ends.at[1]),
            )
        )
    ]
    for copy in copies:
        copy.start()
    for copy in copies[:5]:
        copy.wait()
    inlet = inlet_speed(start, 0)

    def plane_step(plane, carry):
        kind = kinds[plane].astype(jnp.float32)
        kappa = kappa_of(gamma[plane], kind)
        cell[0, plane] = kappa
        cell[1, plane] = kind
        out, values = collide([f[i, plane] for i in range(27)], kappa, kind, rates, inlet)
        for i in range(27):
            post[i, plane] = out[i]
        for i in range(5):
            speed[i, plane] = values[i]
        return carry

    lax.fori_loop(0, NX, plane_step, 0)
    for copy in copies[5:]:
        copy.wait()

    def read(name, i, plane):
        if name == "adjoint":
            return ends[0, i - 18] if plane == 0 else ends[1, i]
        return {"post": post, "cell": cell}[name][i, plane]

    send_x(FIRST, read, to_odd, to_even)


def holding_kernel(*refs):
    half = len(refs) // 2
    for n in range(half):
        pltpu.make_async_copy(refs[n], refs[half + n], refs[-1].at[n]).start()
    for n in range(half):
        pltpu.make_async_copy(refs[n], refs[half + n], refs[-1].at[n]).wait()


def second_kernel(post, cotangent, cell, odd_x, even_x, to_odd, to_even):
    sources = {"post": post, "adjoint": cotangent, "cell": cell}

    def own(name, i, plane, first, rows):
        return sources[name][i, plane, first : first + rows]

    send_y(FIRST, own, odd_x, even_x, to_odd, to_even)


def third_kernel(
    rates_hbm, start_hbm, post, cotangent, cell, odd_x, even_x, odd_y, even_y,
    last_post, adjoint, wide_cell, speed_one, speed_two, gain, to_odd, to_even,
    wide_post, next_post, wide_adjoint, rates, start, sems,
):
    copies = [
        pltpu.make_async_copy(rates_hbm, rates, sems.at[0]),
        pltpu.make_async_copy(start_hbm, start, sems.at[1]),
    ]
    for copy in copies:
        copy.start()
    for i in range(27):
        wide_post[i, HALO : HALO + NX, NY : 2 * NY] = post[i]
        wide_adjoint[i, HALO : HALO + NX, NY : 2 * NY] = cotangent[i]
    for i in range(2):
        wide_cell[i, HALO : HALO + NX, NY : 2 * NY] = cell[i]
    wide = {"post": wide_post, "adjoint": wide_adjoint, "cell": wide_cell}
    unpack(FIRST, wide, odd_x, even_x, odd_y, even_y)
    for copy in copies:
        copy.wait()

    def forward(step, source, target, speed, width):
        inlet = inlet_speed(start, step)

        def body(n, carry):
            plane = n // 2 + (HALO - width)
            row = (n % 2) * NY + NY // 2
            here = pl.ds(row, NY)
            f = pulled(source, plane, row, 1)
            out, values = collide(f, wide_cell[0, plane, here], wide_cell[1, plane, here], rates, inlet)
            for i in range(27):
                target[i, plane, here] = out[i]
            for i in range(5):
                speed[i, plane, here] = values[i]
            return carry

        lax.fori_loop(0, 2 * (NX + 2 * width), body, 0)

    forward(1, wide_post, next_post, speed_one, 2)
    forward(2, next_post, wide_post, speed_two, 1)
    inlet = inlet_speed(start, 3)

    def last(n, carry):
        plane = n + HALO
        here = pl.ds(NY, NY)
        kappa, kind = wide_cell[0, plane, here], wide_cell[1, plane, here]
        out, values = collide(pulled(wide_post, plane, NY, 1), kappa, kind, rates, inlet)
        for i in range(27):
            last_post[i, n] = out[i]
        back, grad = collide_back(
            pulled(wide_adjoint, plane, NY, -1), kappa, kind, rates, values[:4], values[4]
        )
        for i in range(27):
            adjoint[i, n] = back[i]
        gain[n] = grad
        return carry

    lax.fori_loop(0, NX, last, 0)

    def read(name, i, plane):
        if name == "speed":
            return speed_two[i, plane + HALO, NY : 2 * NY]
        return {"post": last_post, "adjoint": adjoint}[name][i, plane]

    send_x(SECOND, read, to_odd, to_even)


def fourth_kernel(post, adjoint, speed, odd_x, even_x, to_odd, to_even):
    def own(name, i, plane, first, rows):
        if name == "speed":
            return speed[i, plane + HALO, NY + first : NY + first + rows]
        return {"post": post, "adjoint": adjoint}[name][i, plane, first : first + rows]

    send_y(SECOND, own, odd_x, even_x, to_odd, to_even)


def fifth_kernel(
    rates_hbm, post, adjoint, wide_cell, speed_zero, speed_one, speed_two, gain, porosity,
    odd_x, even_x, odd_y, even_y,
    flow, first_adjoint, sensitivity,
    wide_post, wide_adjoint, next_adjoint, wide_speed, gains, rates, sem,
):
    copy = pltpu.make_async_copy(rates_hbm, rates, sem)
    copy.start()
    for i in range(27):
        wide_post[i, HALO : HALO + NX, NY : 2 * NY] = post[i]
        wide_adjoint[i, HALO : HALO + NX, NY : 2 * NY] = adjoint[i]
    wide_speed[...] = speed_two[...]
    wide = {"post": wide_post, "adjoint": wide_adjoint, "speed": wide_speed}
    unpack(SECOND, wide, odd_x, even_x, odd_y, even_y)
    copy.wait()

    def back(source, target, speed, width, place):
        def body(n, carry):
            plane = n // 2 + (HALO - width)
            row = (n % 2) * NY + NY // 2
            here = pl.ds(row, NY)
            h = pulled(source, plane, row, -1)
            values = [speed[i, plane, here] for i in range(5)]
            out, grad = collide_back(
                h, wide_cell[0, plane, here], wide_cell[1, plane, here], rates, values[:4], values[4]
            )
            for i in range(27):
                target[i, plane, here] = out[i]
            gains[place, plane, here] = grad
            return carry

        lax.fori_loop(0, 2 * (NX + 2 * width), body, 0)

    back(wide_adjoint, next_adjoint, wide_speed, 2, 0)
    back(next_adjoint, wide_adjoint, speed_one, 1, 1)

    def last(n, carry):
        plane = n + HALO
        here = pl.ds(NY, NY)
        kappa, kind = wide_cell[0, plane, here], wide_cell[1, plane, here]
        values = [speed_zero[i, n] for i in range(5)]
        out, grad = collide_back(
            pulled(wide_adjoint, plane, NY, -1), kappa, kind, rates, values[:4], values[4]
        )
        for i in range(27):
            first_adjoint[i, n] = out[i]
        total = ((gain[n] + gains[0, plane, here]) + gains[1, plane, here]) + grad
        ramp = RAMP_Q * (1.0 + DRAG_MAX) + (1.0 - DRAG_MAX * RAMP_Q) * porosity[n]
        slope = (DRAG_MAX * RAMP_Q * (1.0 + RAMP_Q)) / (ramp * ramp)
        sensitivity[n] = jnp.where(kind < 0.5, slope * total, 0.0)
        tiles = pulled(wide_post, plane, NY, 1)
        for i in range(27):
            flow[i, n] = tiles[i]
        return carry

    lax.fori_loop(0, NX, last, 0)


def f32(*shape):
    return jax.ShapeDtypeStruct(shape, jnp.float32)


def call(kernel, far, arrays, outs, scratch=(), limit=VMEM_LIMIT):
    hbm = pl.BlockSpec(memory_space=pltpu.HBM)
    vmem = pl.BlockSpec(memory_space=pltpu.VMEM)
    return pl.pallas_call(
        kernel,
        out_shape=tuple(f32(*s) for s in outs),
        in_specs=[hbm] * len(far) + [vmem] * len(arrays),
        out_specs=tuple(vmem for _ in outs),
        scratch_shapes=[pltpu.VMEM(s, jnp.float32) if isinstance(s, tuple) else s for s in scratch],
        compiler_params=pltpu.CompilerParams(vmem_limit_bytes=limit),
        name=kernel.__name__,
    )(*far, *arrays)


def partners(axis, first):
    count = lax.axis_size(axis)
    return [[i % count, (i + 1) % count] for i in range(first, count + first, 2)]


def swap(value, axis, first):
    pairs = partners(axis, first)
    return lax.ppermute(value, axis, [(a, b) for a, b in pairs] + [(b, a) for a, b in pairs])


def exchange_x(to_odd, to_even):
    return swap(to_odd, "gx", 1), swap(to_even, "gx", 0)


def exchange_y(to_odd, to_even):
    from_odd = swap(to_odd, "gy", 1)
    return from_odd, lax.all_gather(to_even, "gy", axis_index_groups=partners("gy", 0))


def body(populations, cotangent, porosity, cell_type, rates, start_step):
    block = (27, NX, NY, LANES)
    wide = (27, PLANES, ROWS, LANES)
    tiles = (PLAN_X[FIRST, 1][1], NY, LANES), (PLAN_X[FIRST, -1][1], NY, LANES)
    rows = (PLAN_Y[FIRST, 1][1], LANES), (PLAN_Y[FIRST, -1][1], LANES)
    rates_here, start_here = pltpu.SMEM((27,), jnp.float32), pltpu.SMEM((1,), jnp.int32)
    post, cell, speed_zero, to_odd, to_even = call(
        first_kernel, (rates, start_step, populations, cotangent, porosity, cell_type), (),
        (block, (2, NX, NY, LANES), (5, NX, NY, LANES)) + tiles,
        (
            rates_here, start_here, block, (NX, NY, LANES), pltpu.VMEM((NX, NY, LANES), jnp.int32),
            (2, 9, NY, LANES), pltpu.SemaphoreType.DMA((7,)),
        ),
        FIRST_LIMIT,
    )
    kept = (post, cotangent, cell)
    post, held, cell = call(
        holding_kernel, kept, (), tuple(a.shape for a in kept), (pltpu.SemaphoreType.DMA((len(kept),)),)
    )
    x_halos = exchange_x(to_odd, to_even)
    to_odd, to_even = call(second_kernel, (), (post, held, cell) + x_halos, rows)
    y_halos = exchange_y(to_odd, to_even)
    wide_values = (5, PLANES, ROWS, LANES)
    tiles = (PLAN_X[SECOND, 1][1], NY, LANES), (PLAN_X[SECOND, -1][1], NY, LANES)
    rows = (PLAN_Y[SECOND, 1][1], LANES), (PLAN_Y[SECOND, -1][1], LANES)
    post, adjoint, wide_cell, speed_one, speed_two, gain, to_odd, to_even = call(
        third_kernel, (rates, start_step), (post, held, cell) + x_halos + y_halos,
        (block, block, (2, PLANES, ROWS, LANES), wide_values, wide_values, (NX, NY, LANES)) + tiles,
        (wide, wide, wide, rates_here, start_here, pltpu.SemaphoreType.DMA((2,))),
    )
    x_halos = exchange_x(to_odd, to_even)
    to_odd, to_even = call(fourth_kernel, (), (post, adjoint, speed_two) + x_halos, rows)
    y_halos = exchange_y(to_odd, to_even)
    return call(
        fifth_kernel, (rates,),
        (post, adjoint, wide_cell, speed_zero, speed_one, speed_two, gain, porosity) + x_halos + y_halos,
        (block, block, (NX, NY, LANES)),
        (wide, wide, wide, wide_values, (2, PLANES, ROWS, LANES), rates_here, pltpu.SemaphoreType.DMA(())),
    )


def solution(mesh):
    return jax.shard_map(
        body,
        mesh=mesh,
        in_specs=(
            P(None, "gx", "gy", None),
            P(None, "gx", "gy", None),
            P("gx", "gy", None),
            P("gx", "gy", None),
            P(),
            P(),
        ),
        out_specs=(P(None, "gx", "gy", None), P(None, "gx", "gy", None), P("gx", "gy", None)),
        check_vma=False,
    )
```

```python
import jax
import jax.numpy as jnp
import numpy as np
from jax import lax
from jax.experimental import pallas as pl
from jax.experimental.pallas import tpu as pltpu
from jax.sharding import PartitionSpec as P

DRAG_MAX = 1.0
RAMP_Q = 0.1
INLET_SPEED = 0.3
PULSE_PERIOD = 64

NX, NY, LANES = 4, 8, 128
HALO = 3
PLANES = NX + 2 * HALO
ROWS = 3 * NY
VMEM_LIMIT = 16 * 1024 * 1024
FIRST_LIMIT = 64 * 1024 * 1024

SCALE = [
    float(s)
    for s in np.kron(np.kron([1 / 3, 1 / 2, 1 / 6], [1 / 3, 1 / 2, 1 / 6]), [1 / 3, 1 / 2, 1 / 6])
]
VEL = [(a - 1, b - 1, d - 1) for a in range(3) for b in range(3) for d in range(3)]
ODD = [(c[0] == 0) ^ (c[1] == 0) ^ (c[2] == 0) for c in VEL]


def reach(component, side, width, direction):
    if direction in (0, 2):
        return width
    inward = -side * direction
    return max(0, width - (0 if component == inward else 1 if component == 0 else 2))


def member_reach(field, i, axis, side):
    _, _, width, direction = field
    return reach(VEL[i][axis] if abs(direction) == 1 else 0, side, width, direction)


def first_layer(field):
    return field[2] if field[3] == 2 else 1


def plan_x(fields, side):
    places = {}
    for field in fields:
        for layer in range(first_layer(field), field[2] + 1):
            for i in range(field[1]):
                if member_reach(field, i, 0, side) >= layer:
                    places[field[0], i, layer] = len(places)
    return places, len(places)


def plan_y(fields, side):
    entries, start = [], 0
    for field in fields:
        for plane in range(-field[2], NX + field[2]):
            for i in range(field[1]):
                if plane < 0 and member_reach(field, i, 0, -1) < -plane:
                    continue
                if plane >= NX and member_reach(field, i, 0, 1) < plane - NX + 1:
                    continue
                rows = member_reach(field, i, 1, side)
                skip = first_layer(field) - 1 if -field[2] < plane < NX + field[2] - 1 else 0
                if rows > skip:
                    entries.append((field[0], i, plane, start, skip, rows - skip))
                    start += rows - skip
    return entries, -(-start // 8) * 8


FIRST = (("post", 27, 3, 1), ("adjoint", 27, 1, -1), ("cell", 2, 2, 0))
SECOND = (("adjoint", 27, 3, -1), ("post", 27, 1, 1), ("speed", 4, 2, 2))
PLAN_X = {(f, s): plan_x(f, s) for f in (FIRST, SECOND) for s in (-1, 1)}
PLAN_Y = {(f, s): plan_y(f, s) for f in (FIRST, SECOND) for s in (-1, 1)}


def pack_x(fields, side, read, out):
    for (name, i, layer), place in PLAN_X[fields, side][0].items():
        out[place] = read(name, i, layer - 1 if side > 0 else NX - layer)


def halo_tile(fields, from_low, from_high, name, i, plane):
    if plane < 0:
        return from_low, PLAN_X[fields, -1][0][name, i, -plane]
    return from_high, PLAN_X[fields, 1][0][name, i, plane - NX + 1]


def pack_y(fields, side, own, from_low, from_high, out):
    for name, i, plane, start, skip, rows in PLAN_Y[fields, side][0]:
        first = skip if side > 0 else NY - skip - rows
        if 0 <= plane < NX or (name == "speed" and -2 < plane < NX + 1):
            out[start : start + rows] = own(name, i, plane, first, rows)
        else:
            ref, place = halo_tile(fields, from_low, from_high, name, i, plane)
            out[start : start + rows] = ref[place, first : first + rows]


def by_parity(axis, run, from_odd, from_even):
    parity = lax.axis_index(axis) % 2

    @pl.when(parity == 0)
    def _():
        run(from_odd, from_even)

    @pl.when(parity == 1)
    def _():
        run(from_even, from_odd)


def unpack_x(fields, wide, *from_x):
    for side, ref in zip((-1, 1), from_x):
        for (name, i, layer), place in PLAN_X[fields, side][0].items():
            plane = NX - 1 + layer if side > 0 else -layer
            wide[name][i, plane + HALO, NY : 2 * NY] = ref[place]


def unpack_y(fields, wide, *from_y):
    for side, ref in zip((-1, 1), from_y):
        for name, i, plane, start, skip, rows in PLAN_Y[fields, side][0]:
            first = 2 * NY + skip if side > 0 else NY - skip - rows
            wide[name][i, plane + HALO, first : first + rows] = ref[start : start + rows]


def receive_x(fields, wide, odd_x, even_x):
    by_parity("gx", lambda low, high: unpack_x(fields, wide, low, high), odd_x, even_x)


def receive_y(fields, wide, odd_y, even_y):
    partner = even_y.at[1 - lax.axis_index("gy") % 2]
    by_parity("gy", lambda low, high: unpack_y(fields, wide, low, high), odd_y, partner)


def send_x(fields, read, to_odd, to_even):
    def run(to_low, to_high):
        pack_x(fields, 1, read, to_low)
        pack_x(fields, -1, read, to_high)

    by_parity("gx", run, to_odd, to_even)


def send_y(fields, own, odd_x, even_x, to_odd, to_even):
    def with_halo(from_low, from_high):
        def run(to_low, to_high):
            pack_y(fields, 1, own, from_low, from_high, to_low)
            pack_y(fields, -1, own, from_low, from_high, to_high)

        by_parity("gy", run, to_odd, to_even)

    by_parity("gx", with_halo, odd_x, even_x)


def moments(f):
    v = list(f)
    for stride in (9, 3, 1):
        for i in range(27):
            if (i // stride) % 3 == 0:
                a, b, c = v[i], v[i + stride], v[i + 2 * stride]
                s = (a + c) + b
                v[i], v[i + stride], v[i + 2 * stride] = s, c - a, s - 3.0 * b
    return v


def moments_transposed(m):
    v = list(m)
    for stride in (9, 3, 1):
        for i in range(27):
            if (i // stride) % 3 == 0:
                s, d, q = v[i], v[i + stride], v[i + 2 * stride]
                t = s + q
                v[i], v[i + stride], v[i + 2 * stride] = t - d, s - (q + q), t + d
    return v


def rate_of(rates, i, relaxing, even, odd):
    return jnp.where(relaxing, rates[i], odd if ODD[i] else even)


def kinds_of(kind):
    relaxing = kind < 1.5
    even = jnp.where((kind > 1.5) & (kind < 3.5), 1.0, 0.0)
    odd = jnp.where(kind > 3.5, 2.0, even)
    return relaxing, even, odd


def collide(f, kappa, kind, rates, inlet):
    m = moments(f)
    relaxing, even, odd = kinds_of(kind)
    rho = m[0]
    inverse = 1.0 / rho
    ux, uy, uz = m[9] * inverse, m[3] * inverse, m[1] * inverse
    vx, vy = kappa * ux, kappa * uy
    vz = jnp.where((kind > 1.5) & (kind < 2.5), inlet, kappa * uz)
    den = jnp.where(relaxing, rho, 1.0)
    jx, jy, jz = den * vx, den * vy, den * vz
    xy, xz, yz = jx * vy, jx * vz, jy * vz
    xx, yy, zz = 3.0 * (jx * vx), 3.0 * (jy * vy), 3.0 * (jz * vz)
    x2, y2, z2 = xx - den, yy - den, zz - den
    e = [None] * 27
    e[0] = den
    e[18], e[6], e[2] = x2, y2, z2
    e[24], e[20], e[8] = -(x2 + yy), -(x2 + zz), -(y2 + zz)
    e[26] = (x2 + yy) + zz
    e[9], e[15], e[11], e[17] = jx, -jx, -jx, jx
    e[3], e[21], e[5], e[23] = jy, -jy, -jy, jy
    e[1], e[19], e[7], e[25] = jz, -jz, -jz, jz
    e[12], e[14] = xy, -xy
    e[10], e[16] = xz, -xz
    e[4], e[22] = yz, -yz
    out = []
    for i in range(27):
        rate = rate_of(rates, i, relaxing, even, odd)
        gap = -m[i] if e[i] is None else e[i] - m[i]
        out.append(SCALE[i] * (m[i] + rate * gap))
    return moments_transposed(out), (ux, uy, uz, inverse, rho)


def collide_back(h, kappa, kind, rates, speed, rho=None):
    y = moments(h)
    relaxing, even, odd = kinds_of(kind)
    ux, uy, uz, inverse = speed
    w, z = [], []
    for i in range(27):
        yi = SCALE[i] * y[i]
        wi = rate_of(rates, i, relaxing, even, odd) * yi
        w.append(wi)
        z.append(yi - wi)
    vx, vy, vz = kappa * ux, kappa * uy, kappa * uz
    w222 = w[26]
    a_x = (w[18] - w[24]) - (w[20] - w222)
    a_y = (w[6] - w[24]) - (w[8] - w222)
    a_z = (w[2] - w[20]) - (w[8] - w222)
    b_x = (w[9] - w[15]) - (w[11] - w[17])
    b_y = (w[3] - w[21]) - (w[5] - w[23])
    b_z = (w[1] - w[19]) - (w[7] - w[25])
    c_xy, c_xz, c_yz = w[12] - w[14], w[10] - w[16], w[4] - w[22]
    base = ((w[0] - w[18]) - (w[6] + w[2])) + ((w[24] + w[20]) + (w[8] - w222))
    p_x, p_y, p_z = 3.0 * (a_x * vx), 3.0 * (a_y * vy), 3.0 * (a_z * vz)
    q_x, q_y, q_z = c_xy * vy + c_xz * vz, c_xy * vx + c_yz * vz, c_xz * vx + c_yz * vy
    r_x, r_y, r_z = b_x + p_x, b_y + p_y, b_z + p_z
    value = base + vx * (r_x + 0.5 * q_x) + vy * (r_y + 0.5 * q_y) + vz * (r_z + 0.5 * q_z)
    g_x, g_y, g_z = r_x + p_x + q_x, r_y + p_y + q_y, r_z + p_z + q_z
    factor = jnp.where(relaxing, kappa, kappa * inverse)
    along = ux * g_x + uy * g_y + uz * g_z
    z[0] = z[0] + (jnp.where(relaxing, value, 0.0) - factor * along)
    z[9] = z[9] + factor * g_x
    z[3] = z[3] + factor * g_y
    z[1] = z[1] + factor * g_z
    return moments_transposed(z), None if rho is None else rho * along


def turned(value, shift):
    return value if shift == 0 else pltpu.roll(value, shift % LANES, axis=1)


def own_rows(ref, place):
    return ref[place + (slice(NY, 2 * NY),)]


def edge_rows(ref, place):
    low, high = ref[place + (slice(NY - 2, 2 * NY - 2),)], ref[place + (slice(NY + 2, 2 * NY + 2),)]
    return jnp.where(lax.broadcasted_iota(jnp.int32, (NY, LANES), 0) < NY // 2, low, high)


def put_edge_rows(ref, place, value):
    ref[place + (slice(NY - 2, NY + 2),)] = value[: NY // 2]
    ref[place + (slice(2 * NY - 2, 2 * NY + 2),)] = value[NY // 2 :]


def put_own_rows(ref, place, value):
    ref[place + (slice(NY, 2 * NY),)] = value


OWN = (own_rows, put_own_rows)
EDGE = (edge_rows, put_edge_rows)


def shifted(wide, shift):
    class View:
        def __getitem__(self, place):
            return wide[place[:-1] + (slice(place[-1].start + shift, place[-1].stop + shift),)]

    return View()


def pulled(wide, plane, rows, direction):
    tiles = []
    for i, (cx, cy, cz) in enumerate(VEL):
        tile = rows(shifted(wide, -direction * cy), (i, plane - direction * cx))
        tiles.append(turned(tile, direction * cz))
    return tiles


def forward(where, source, target, cell, speed, rates, inlet, width):
    get, put = where

    def body(plane, carry):
        out, values = collide(
            pulled(source, plane, get, 1), get(cell, (0, plane)), get(cell, (1, plane)), rates, inlet
        )
        for i in range(27):
            put(target, (i, plane), out[i])
        for i in range(5):
            put(speed, (i, plane), values[i])
        return carry

    lax.fori_loop(HALO - width, HALO + NX + width, body, 0)


def backward(where, source, target, cell, speed, gain, rates, width):
    get, put = where

    def body(plane, carry):
        values = [get(speed, (i, plane)) for i in range(5)]
        out, grad = collide_back(
            pulled(source, plane, get, -1), get(cell, (0, plane)), get(cell, (1, plane)), rates,
            values[:4], values[4],
        )
        for i in range(27):
            put(target, (i, plane), out[i])
        put(gain, (plane,), grad)
        return carry

    lax.fori_loop(HALO - width, HALO + NX + width, body, 0)


def inlet_speed(start, step):
    time = jnp.full((NY, LANES), (start[0] + step) % PULSE_PERIOD, jnp.int32).astype(jnp.float32)
    return INLET_SPEED * jnp.sin(time * (2.0 * np.pi / PULSE_PERIOD))


def kappa_of(porosity, kind):
    damping = (RAMP_Q + porosity) / (
        RAMP_Q * (1.0 + DRAG_MAX) + (1.0 - DRAG_MAX * RAMP_Q) * porosity
    )
    return jnp.where(kind < 0.5, damping, jnp.where((kind > 2.5) & (kind < 3.5), 1.0, 0.0))


def first_kernel(
    rates_hbm, start_hbm, populations, cotangent, porosity, cell_type,
    post, cell, speed, to_odd, to_even,
    rates, start, f, gamma, kinds, ends, sems,
):
    copies = [
        pltpu.make_async_copy(source, target, sems.at[n])
        for n, (source, target) in enumerate(
            (
                (rates_hbm, rates), (start_hbm, start), (porosity, gamma), (cell_type, kinds),
                (populations, f), (cotangent.at[18:27, 0], ends.at[0]), (cotangent.at[0:9, NX - 1], ends.at[1]),
            )
        )
    ]
    for copy in copies:
        copy.start()
    for copy in copies[:5]:
        copy.wait()
    inlet = inlet_speed(start, 0)

    def plane_step(plane, carry):
        kind = kinds[plane].astype(jnp.float32)
        kappa = kappa_of(gamma[plane], kind)
        cell[0, plane] = kappa
        cell[1, plane] = kind
        out, values = collide([f[i, plane] for i in range(27)], kappa, kind, rates, inlet)
        for i in range(27):
            post[i, plane] = out[i]
        for i in range(5):
            speed[i, plane] = values[i]
        return carry

    lax.fori_loop(0, NX, plane_step, 0)
    for copy in copies[5:]:
        copy.wait()

    def read(name, i, plane):
        if name == "adjoint":
            return ends[0, i - 18] if plane == 0 else ends[1, i]
        return {"post": post, "cell": cell}[name][i, plane]

    send_x(FIRST, read, to_odd, to_even)


def holding_kernel(*refs):
    half = len(refs) // 2
    for n in range(half):
        pltpu.make_async_copy(refs[n], refs[half + n], refs[-1].at[n]).start()
    for n in range(half):
        pltpu.make_async_copy(refs[n], refs[half + n], refs[-1].at[n]).wait()


def second_kernel(post, cotangent, cell, odd_x, even_x, to_odd, to_even):
    sources = {"post": post, "adjoint": cotangent, "cell": cell}

    def own(name, i, plane, first, rows):
        return sources[name][i, plane, first : first + rows]

    send_y(FIRST, own, odd_x, even_x, to_odd, to_even)


def fetch(sems, *pairs):
    copies = [pltpu.make_async_copy(a, b, sems.at[n]) for n, (a, b) in enumerate(pairs)]
    for copy in copies:
        copy.start()
    for copy in copies:
        copy.wait()


def put_block(wide, block, members):
    for i in range(members):
        wide[i, HALO : HALO + NX, NY : 2 * NY] = block[i]


def third_early_kernel(
    rates_hbm, start_hbm, post, cotangent, cell, odd_x, even_x,
    post_zero, post_one, post_two, wide_adjoint, wide_cell, speed_one, speed_two,
    rates, start, sems,
):
    fetch(sems, (rates_hbm, rates), (start_hbm, start))
    put_block(post_zero, post, 27)
    put_block(wide_adjoint, cotangent, 27)
    put_block(wide_cell, cell, 2)
    wide = {"post": post_zero, "adjoint": wide_adjoint, "cell": wide_cell}
    receive_x(FIRST, wide, odd_x, even_x)
    forward(OWN, post_zero, post_one, wide_cell, speed_one, rates, inlet_speed(start, 1), 2)
    forward(OWN, post_one, post_two, wide_cell, speed_two, rates, inlet_speed(start, 2), 1)


def third_late_kernel(
    rates_hbm, start_hbm, _0, _1, _2, _3, _4, _5, _6, odd_y, even_y,
    post_zero, post_one, post_two, wide_adjoint, wide_cell, speed_one, speed_two,
    last_post, adjoint, gain, to_odd, to_even,
    rates, start, sems,
):
    fetch(sems, (rates_hbm, rates), (start_hbm, start))
    wide = {"post": post_zero, "adjoint": wide_adjoint, "cell": wide_cell}
    receive_y(FIRST, wide, odd_y, even_y)
    forward(EDGE, post_zero, post_one, wide_cell, speed_one, rates, inlet_speed(start, 1), 2)
    forward(EDGE, post_one, post_two, wide_cell, speed_two, rates, inlet_speed(start, 2), 1)
    inlet = inlet_speed(start, 3)

    def last(n, carry):
        plane = n + HALO
        kappa, kind = own_rows(wide_cell, (0, plane)), own_rows(wide_cell, (1, plane))
        out, values = collide(pulled(post_two, plane, own_rows, 1), kappa, kind, rates, inlet)
        for i in range(27):
            last_post[i, n] = out[i]
        back, grad = collide_back(
            pulled(wide_adjoint, plane, own_rows, -1), kappa, kind, rates, values[:4], values[4]
        )
        for i in range(27):
            adjoint[i, n] = back[i]
        gain[n] = grad
        return carry

    lax.fori_loop(0, NX, last, 0)

    def read(name, i, plane):
        if name == "speed":
            return speed_two[i, plane + HALO, NY : 2 * NY]
        return {"post": last_post, "adjoint": adjoint}[name][i, plane]

    send_x(SECOND, read, to_odd, to_even)


def fourth_kernel(post, adjoint, speed, odd_x, even_x, to_odd, to_even):
    def own(name, i, plane, first, rows):
        if name == "speed":
            return speed[i, plane + HALO, NY + first : NY + first + rows]
        return {"post": post, "adjoint": adjoint}[name][i, plane, first : first + rows]

    send_y(SECOND, own, odd_x, even_x, to_odd, to_even)


def fifth_early_kernel(
    rates_hbm, post, adjoint, wide_cell, speed_one, _0, odd_x, even_x,
    speed_two, adjoint_three, adjoint_two, adjoint_one, wide_post, gain_two, gain_one,
    rates, sems,
):
    fetch(sems, (rates_hbm, rates))
    put_block(wide_post, post, 27)
    put_block(adjoint_three, adjoint, 27)
    wide = {"post": wide_post, "adjoint": adjoint_three, "speed": speed_two}
    receive_x(SECOND, wide, odd_x, even_x)
    backward(OWN, adjoint_three, adjoint_two, wide_cell, speed_two, gain_two, rates, 2)
    backward(OWN, adjoint_two, adjoint_one, wide_cell, speed_one, gain_one, rates, 1)


def fifth_late_kernel(
    rates_hbm, wide_cell, speed_zero, speed_one, gain, porosity, odd_y, even_y, _0, _1, _2, _3, _4, _5, _6,
    flow, first_adjoint, sensitivity,
    speed_two, adjoint_three, adjoint_two, adjoint_one, wide_post, gain_two, gain_one,
    rates, sems,
):
    fetch(sems, (rates_hbm, rates))
    wide = {"post": wide_post, "adjoint": adjoint_three, "speed": speed_two}
    receive_y(SECOND, wide, odd_y, even_y)
    backward(EDGE, adjoint_three, adjoint_two, wide_cell, speed_two, gain_two, rates, 2)
    backward(EDGE, adjoint_two, adjoint_one, wide_cell, speed_one, gain_one, rates, 1)

    def last(n, carry):
        plane = n + HALO
        kappa, kind = own_rows(wide_cell, (0, plane)), own_rows(wide_cell, (1, plane))
        values = [speed_zero[i, n] for i in range(5)]
        out, grad = collide_back(
            pulled(adjoint_one, plane, own_rows, -1), kappa, kind, rates, values[:4], values[4]
        )
        for i in range(27):
            first_adjoint[i, n] = out[i]
        total = ((gain[n] + own_rows(gain_two, (plane,))) + own_rows(gain_one, (plane,))) + grad
        ramp = RAMP_Q * (1.0 + DRAG_MAX) + (1.0 - DRAG_MAX * RAMP_Q) * porosity[n]
        slope = (DRAG_MAX * RAMP_Q * (1.0 + RAMP_Q)) / (ramp * ramp)
        sensitivity[n] = jnp.where(kind < 0.5, slope * total, 0.0)
        tiles = pulled(wide_post, plane, own_rows, 1)
        for i in range(27):
            flow[i, n] = tiles[i]
        return carry

    lax.fori_loop(0, NX, last, 0)


def f32(*shape):
    return jax.ShapeDtypeStruct(shape, jnp.float32)


def call(kernel, far, arrays, outs, scratch=(), limit=VMEM_LIMIT, aliases=None):
    hbm = pl.BlockSpec(memory_space=pltpu.HBM)
    vmem = pl.BlockSpec(memory_space=pltpu.VMEM)
    return pl.pallas_call(
        kernel,
        out_shape=tuple(f32(*s) for s in outs),
        in_specs=[hbm] * len(far) + [vmem] * len(arrays),
        out_specs=tuple(vmem for _ in outs),
        scratch_shapes=[pltpu.VMEM(s, jnp.float32) if isinstance(s, tuple) else s for s in scratch],
        compiler_params=pltpu.CompilerParams(vmem_limit_bytes=limit),
        input_output_aliases=aliases or {},
        name=kernel.__name__,
    )(*far, *arrays)


def partners(axis, first):
    count = lax.axis_size(axis)
    return [[i % count, (i + 1) % count] for i in range(first, count + first, 2)]


def swap(value, axis, first):
    pairs = partners(axis, first)
    return lax.ppermute(value, axis, [(a, b) for a, b in pairs] + [(b, a) for a, b in pairs])


def exchange_x(to_odd, to_even):
    return swap(to_odd, "gx", 1), swap(to_even, "gx", 0)


def exchange_y(to_odd, to_even):
    from_odd = swap(to_odd, "gy", 1)
    return from_odd, lax.all_gather(to_even, "gy", axis_index_groups=partners("gy", 0))


def body(populations, cotangent, porosity, cell_type, rates, start_step):
    block = (27, NX, NY, LANES)
    wide = (27, PLANES, ROWS, LANES)
    tiles = (PLAN_X[FIRST, 1][1], NY, LANES), (PLAN_X[FIRST, -1][1], NY, LANES)
    rows = (PLAN_Y[FIRST, 1][1], LANES), (PLAN_Y[FIRST, -1][1], LANES)
    rates_here, start_here = pltpu.SMEM((27,), jnp.float32), pltpu.SMEM((1,), jnp.int32)
    post, cell, speed_zero, to_odd, to_even = call(
        first_kernel, (rates, start_step, populations, cotangent, porosity, cell_type), (),
        (block, (2, NX, NY, LANES), (5, NX, NY, LANES)) + tiles,
        (
            rates_here, start_here, block, (NX, NY, LANES), pltpu.VMEM((NX, NY, LANES), jnp.int32),
            (2, 9, NY, LANES), pltpu.SemaphoreType.DMA((7,)),
        ),
        FIRST_LIMIT,
    )
    kept = (post, cotangent, cell)
    post, held, cell = call(
        holding_kernel, kept, (), tuple(a.shape for a in kept), (pltpu.SemaphoreType.DMA((len(kept),)),)
    )
    x_halos = exchange_x(to_odd, to_even)
    to_odd, to_even = call(second_kernel, (), (post, held, cell) + x_halos, rows)
    y_halos = exchange_y(to_odd, to_even)
    wide_values = (5, PLANES, ROWS, LANES)
    wides = (wide, wide, wide, wide, (2, PLANES, ROWS, LANES), wide_values, wide_values)
    scalars = (rates_here, start_here, pltpu.SemaphoreType.DMA((2,)))
    wides = call(
        third_early_kernel, (rates, start_step), (post, held, cell) + x_halos, wides, scalars
    )
    tiles = (PLAN_X[SECOND, 1][1], NY, LANES), (PLAN_X[SECOND, -1][1], NY, LANES)
    rows = (PLAN_Y[SECOND, 1][1], LANES), (PLAN_Y[SECOND, -1][1], LANES)
    *wides, post, adjoint, gain, to_odd, to_even = call(
        third_late_kernel, (rates, start_step), tuple(wides) + y_halos,
        tuple(a.shape for a in wides) + (block, block, (NX, NY, LANES)) + tiles,
        scalars, aliases={2 + n: n for n in range(len(wides))},
    )
    wide_cell, speed_one, speed_two = wides[4:]
    x_halos = exchange_x(to_odd, to_even)
    to_odd, to_even = call(fourth_kernel, (), (post, adjoint, speed_two) + x_halos, rows)
    y_halos = exchange_y(to_odd, to_even)
    scalars = (rates_here, pltpu.SemaphoreType.DMA((1,)))
    wide_gain = (PLANES, ROWS, LANES)
    wides = call(
        fifth_early_kernel, (rates,), (post, adjoint, wide_cell, speed_one, speed_two) + x_halos,
        (wide_values, wide, wide, wide, wide, wide_gain, wide_gain), scalars, aliases={5: 0},
    )
    return call(
        fifth_late_kernel, (rates,),
        (wide_cell, speed_zero, speed_one, gain, porosity) + y_halos + tuple(wides),
        (block, block, (NX, NY, LANES)) + tuple(a.shape for a in wides), scalars,
        aliases={8 + n: 3 + n for n in range(len(wides))},
    )[:3]


def solution(mesh):
    return jax.shard_map(
        body,
        mesh=mesh,
        in_specs=(
            P(None, "gx", "gy", None),
            P(None, "gx", "gy", None),
            P("gx", "gy", None),
            P("gx", "gy", None),
            P(),
            P(),
        ),
        out_specs=(P(None, "gx", "gy", None), P(None, "gx", "gy", None), P("gx", "gy", None)),
        check_vma=False,
    )
```

```python
import jax
import jax.numpy as jnp
import numpy as np
from jax import lax
from jax.experimental import pallas as pl
from jax.experimental.pallas import tpu as pltpu
from jax.sharding import PartitionSpec as P

DRAG_MAX = 1.0
RAMP_Q = 0.1
INLET_SPEED = 0.3
PULSE_PERIOD = 64

NX, NY, LANES = 4, 8, 128
HALO = 3
TOGETHER = {8: 4, 6: 3, 4: 4}
PLANES = NX + 2 * HALO
ROWS = 3 * NY
VMEM_LIMIT = 16 * 1024 * 1024
FIRST_LIMIT = 64 * 1024 * 1024

SCALE = [
    float(s)
    for s in np.kron(np.kron([1 / 3, 1 / 2, 1 / 6], [1 / 3, 1 / 2, 1 / 6]), [1 / 3, 1 / 2, 1 / 6])
]
VEL = [(a - 1, b - 1, d - 1) for a in range(3) for b in range(3) for d in range(3)]
ODD = [(c[0] == 0) ^ (c[1] == 0) ^ (c[2] == 0) for c in VEL]


def reach(component, side, width, direction):
    if direction in (0, 2):
        return width
    inward = -side * direction
    return max(0, width - (0 if component == inward else 1 if component == 0 else 2))


def member_reach(field, i, axis, side):
    _, _, width, direction = field
    return reach(VEL[i][axis] if abs(direction) == 1 else 0, side, width, direction)


def first_layer(field):
    return field[2] if field[3] == 2 else 1


def plan_x(fields, side):
    places = {}
    for field in fields:
        for layer in range(first_layer(field), field[2] + 1):
            for i in range(field[1]):
                if member_reach(field, i, 0, side) >= layer:
                    places[field[0], i, layer] = len(places)
    return places, len(places)


def plan_y(fields, side):
    entries, start = [], 0
    for field in fields:
        for plane in range(-field[2], NX + field[2]):
            for i in range(field[1]):
                if plane < 0 and member_reach(field, i, 0, -1) < -plane:
                    continue
                if plane >= NX and member_reach(field, i, 0, 1) < plane - NX + 1:
                    continue
                rows = member_reach(field, i, 1, side)
                skip = first_layer(field) - 1 if -field[2] < plane < NX + field[2] - 1 else 0
                if rows > skip:
                    entries.append((field[0], i, plane, start, skip, rows - skip))
                    start += rows - skip
    return entries, -(-start // 8) * 8


FIRST = (("post", 27, 3, 1), ("adjoint", 27, 1, -1), ("cell", 2, 2, 0))
SECOND = (("adjoint", 27, 3, -1), ("post", 27, 1, 1), ("speed", 4, 2, 2))
PLAN_X = {(f, s): plan_x(f, s) for f in (FIRST, SECOND) for s in (-1, 1)}
PLAN_Y = {(f, s): plan_y(f, s) for f in (FIRST, SECOND) for s in (-1, 1)}


def pack_x(fields, side, read, out):
    for (name, i, layer), place in PLAN_X[fields, side][0].items():
        out[place] = read(name, i, layer - 1 if side > 0 else NX - layer)


def halo_tile(fields, from_low, from_high, name, i, plane):
    if plane < 0:
        return from_low, PLAN_X[fields, -1][0][name, i, -plane]
    return from_high, PLAN_X[fields, 1][0][name, i, plane - NX + 1]


def pack_y(fields, side, own, from_low, from_high, out):
    for name, i, plane, start, skip, rows in PLAN_Y[fields, side][0]:
        first = skip if side > 0 else NY - skip - rows
        if 0 <= plane < NX or (name == "speed" and -2 < plane < NX + 1):
            out[start : start + rows] = own(name, i, plane, first, rows)
        else:
            ref, place = halo_tile(fields, from_low, from_high, name, i, plane)
            out[start : start + rows] = ref[place, first : first + rows]


def by_parity(axis, run, from_odd, from_even):
    parity = lax.axis_index(axis) % 2

    @pl.when(parity == 0)
    def _():
        run(from_odd, from_even)

    @pl.when(parity == 1)
    def _():
        run(from_even, from_odd)


def unpack_x(fields, wide, *from_x):
    for side, ref in zip((-1, 1), from_x):
        for (name, i, layer), place in PLAN_X[fields, side][0].items():
            plane = NX - 1 + layer if side > 0 else -layer
            wide[name][i, plane + HALO, NY : 2 * NY] = ref[place]


def unpack_y(fields, wide, *from_y):
    for side, ref in zip((-1, 1), from_y):
        for name, i, plane, start, skip, rows in PLAN_Y[fields, side][0]:
            first = 2 * NY + skip if side > 0 else NY - skip - rows
            wide[name][i, plane + HALO, first : first + rows] = ref[start : start + rows]


def receive_x(fields, wide, odd_x, even_x):
    by_parity("gx", lambda low, high: unpack_x(fields, wide, low, high), odd_x, even_x)


def receive_y(fields, wide, odd_y, even_y):
    partner = even_y.at[1 - lax.axis_index("gy") % 2]
    by_parity("gy", lambda low, high: unpack_y(fields, wide, low, high), odd_y, partner)


def send_x(fields, read, to_odd, to_even):
    def run(to_low, to_high):
        pack_x(fields, 1, read, to_low)
        pack_x(fields, -1, read, to_high)

    by_parity("gx", run, to_odd, to_even)


def send_y(fields, own, odd_x, even_x, to_odd, to_even):
    def with_halo(from_low, from_high):
        def run(to_low, to_high):
            pack_y(fields, 1, own, from_low, from_high, to_low)
            pack_y(fields, -1, own, from_low, from_high, to_high)

        by_parity("gy", run, to_odd, to_even)

    by_parity("gx", with_halo, odd_x, even_x)


def moments(f):
    v = list(f)
    for stride in (9, 3, 1):
        for i in range(27):
            if (i // stride) % 3 == 0:
                a, b, c = v[i], v[i + stride], v[i + 2 * stride]
                s = (a + c) + b
                v[i], v[i + stride], v[i + 2 * stride] = s, c - a, s - 3.0 * b
    return v


def moments_transposed(m):
    v = list(m)
    for stride in (9, 3, 1):
        for i in range(27):
            if (i // stride) % 3 == 0:
                s, d, q = v[i], v[i + stride], v[i + 2 * stride]
                t = s + q
                v[i], v[i + stride], v[i + 2 * stride] = t - d, s - (q + q), t + d
    return v


def rate_of(rates, i, relaxing, even, odd):
    return jnp.where(relaxing, rates[i], odd if ODD[i] else even)


def kinds_of(kind):
    relaxing = kind < 1.5
    even = jnp.where((kind > 1.5) & (kind < 3.5), 1.0, 0.0)
    odd = jnp.where(kind > 3.5, 2.0, even)
    return relaxing, even, odd


def collide(f, kappa, kind, rates, inlet):
    m = moments(f)
    relaxing, even, odd = kinds_of(kind)
    rho = m[0]
    inverse = 1.0 / rho
    ux, uy, uz = m[9] * inverse, m[3] * inverse, m[1] * inverse
    vx, vy = kappa * ux, kappa * uy
    vz = jnp.where((kind > 1.5) & (kind < 2.5), inlet, kappa * uz)
    den = jnp.where(relaxing, rho, 1.0)
    jx, jy, jz = den * vx, den * vy, den * vz
    xy, xz, yz = jx * vy, jx * vz, jy * vz
    xx, yy, zz = 3.0 * (jx * vx), 3.0 * (jy * vy), 3.0 * (jz * vz)
    x2, y2, z2 = xx - den, yy - den, zz - den
    e = [None] * 27
    e[0] = den
    e[18], e[6], e[2] = x2, y2, z2
    e[24], e[20], e[8] = -(x2 + yy), -(x2 + zz), -(y2 + zz)
    e[26] = (x2 + yy) + zz
    e[9], e[15], e[11], e[17] = jx, -jx, -jx, jx
    e[3], e[21], e[5], e[23] = jy, -jy, -jy, jy
    e[1], e[19], e[7], e[25] = jz, -jz, -jz, jz
    e[12], e[14] = xy, -xy
    e[10], e[16] = xz, -xz
    e[4], e[22] = yz, -yz
    out = []
    for i in range(27):
        rate = rate_of(rates, i, relaxing, even, odd)
        gap = -m[i] if e[i] is None else e[i] - m[i]
        out.append(SCALE[i] * (m[i] + rate * gap))
    return moments_transposed(out), (ux, uy, uz, inverse, rho)


def collide_back(h, kappa, kind, rates, speed, rho=None):
    y = moments(h)
    relaxing, even, odd = kinds_of(kind)
    ux, uy, uz, inverse = speed
    w, z = [], []
    for i in range(27):
        yi = SCALE[i] * y[i]
        wi = rate_of(rates, i, relaxing, even, odd) * yi
        w.append(wi)
        z.append(yi - wi)
    vx, vy, vz = kappa * ux, kappa * uy, kappa * uz
    w222 = w[26]
    a_x = (w[18] - w[24]) - (w[20] - w222)
    a_y = (w[6] - w[24]) - (w[8] - w222)
    a_z = (w[2] - w[20]) - (w[8] - w222)
    b_x = (w[9] - w[15]) - (w[11] - w[17])
    b_y = (w[3] - w[21]) - (w[5] - w[23])
    b_z = (w[1] - w[19]) - (w[7] - w[25])
    c_xy, c_xz, c_yz = w[12] - w[14], w[10] - w[16], w[4] - w[22]
    base = ((w[0] - w[18]) - (w[6] + w[2])) + ((w[24] + w[20]) + (w[8] - w222))
    p_x, p_y, p_z = 3.0 * (a_x * vx), 3.0 * (a_y * vy), 3.0 * (a_z * vz)
    q_x, q_y, q_z = c_xy * vy + c_xz * vz, c_xy * vx + c_yz * vz, c_xz * vx + c_yz * vy
    r_x, r_y, r_z = b_x + p_x, b_y + p_y, b_z + p_z
    value = base + vx * (r_x + 0.5 * q_x) + vy * (r_y + 0.5 * q_y) + vz * (r_z + 0.5 * q_z)
    g_x, g_y, g_z = r_x + p_x + q_x, r_y + p_y + q_y, r_z + p_z + q_z
    factor = jnp.where(relaxing, kappa, kappa * inverse)
    along = ux * g_x + uy * g_y + uz * g_z
    z[0] = z[0] + (jnp.where(relaxing, value, 0.0) - factor * along)
    z[9] = z[9] + factor * g_x
    z[3] = z[3] + factor * g_y
    z[1] = z[1] + factor * g_z
    return moments_transposed(z), None if rho is None else rho * along


def turned(value, shift):
    return value if shift == 0 else pltpu.roll(value, shift % LANES, axis=1)


def own_rows(ref, place):
    return ref[place + (slice(NY, 2 * NY),)]


def edge_rows(ref, place):
    low, high = ref[place + (slice(NY - 2, 2 * NY - 2),)], ref[place + (slice(NY + 2, 2 * NY + 2),)]
    return jnp.where(lax.broadcasted_iota(jnp.int32, (NY, LANES), 0) < NY // 2, low, high)


def put_edge_rows(ref, place, value):
    ref[place + (slice(NY - 2, NY + 2),)] = value[: NY // 2]
    ref[place + (slice(2 * NY - 2, 2 * NY + 2),)] = value[NY // 2 :]


def put_own_rows(ref, place, value):
    ref[place + (slice(NY, 2 * NY),)] = value


OWN = (own_rows, put_own_rows)
EDGE = (edge_rows, put_edge_rows)


def shifted(wide, shift):
    class View:
        def __getitem__(self, place):
            return wide[place[:-1] + (slice(place[-1].start + shift, place[-1].stop + shift),)]

    return View()


def pulled(wide, plane, rows, direction):
    tiles = []
    for i, (cx, cy, cz) in enumerate(VEL):
        tile = rows(shifted(wide, -direction * cy), (i, plane - direction * cx))
        tiles.append(turned(tile, direction * cz))
    return tiles


def planes_loop(first, last, load, work, store):
    together = TOGETHER[last - first]

    def body(n, carry):
        planes = [first + together * n + k for k in range(together)]
        loaded = [load(plane) for plane in planes]
        results = [work(*values) for values in loaded]
        for plane, result in zip(planes, results):
            store(plane, result)
        return carry

    lax.fori_loop(0, (last - first) // together, body, 0)


def forward(where, source, target, cell, speed, rates, inlet, width):
    get, put = where

    def load(plane):
        return pulled(source, plane, get, 1), get(cell, (0, plane)), get(cell, (1, plane))

    def work(f, kappa, kind):
        return collide(f, kappa, kind, rates, inlet)

    def store(plane, result):
        out, values = result
        for i in range(27):
            put(target, (i, plane), out[i])
        for i in range(5):
            put(speed, (i, plane), values[i])

    planes_loop(HALO - width, HALO + NX + width, load, work, store)


def backward(where, source, target, cell, speed, gain, rates, width):
    get, put = where

    def load(plane):
        values = [get(speed, (i, plane)) for i in range(5)]
        return pulled(source, plane, get, -1), get(cell, (0, plane)), get(cell, (1, plane)), values

    def work(h, kappa, kind, values):
        return collide_back(h, kappa, kind, rates, values[:4], values[4])

    def store(plane, result):
        out, grad = result
        for i in range(27):
            put(target, (i, plane), out[i])
        put(gain, (plane,), grad)

    planes_loop(HALO - width, HALO + NX + width, load, work, store)


def inlet_speed(start, step):
    time = jnp.full((NY, LANES), (start[0] + step) % PULSE_PERIOD, jnp.int32).astype(jnp.float32)
    return INLET_SPEED * jnp.sin(time * (2.0 * np.pi / PULSE_PERIOD))


def kappa_of(porosity, kind):
    damping = (RAMP_Q + porosity) / (
        RAMP_Q * (1.0 + DRAG_MAX) + (1.0 - DRAG_MAX * RAMP_Q) * porosity
    )
    return jnp.where(kind < 0.5, damping, jnp.where((kind > 2.5) & (kind < 3.5), 1.0, 0.0))


def first_kernel(
    rates_hbm, start_hbm, populations, cotangent, porosity, cell_type,
    post_hbm, cell_hbm, speed_hbm, to_odd_hbm, to_even_hbm,
    rates, start, f, gamma, kinds, ends, post, cell, speed, to_odd, to_even, sems,
):
    small = start_copies(
        sems, (rates_hbm, rates), (start_hbm, start), (porosity, gamma), (cell_type, kinds)
    )
    halves = [
        start_copies(sems.at[4 + n : 5 + n], (populations.at[:, 2 * n : 2 * n + 2], f.at[:, 2 * n : 2 * n + 2]))
        for n in range(NX // 2)
    ]
    tail = start_copies(
        sems.at[6:8], (cotangent.at[18:27, 0], ends.at[0]), (cotangent.at[0:9, NX - 1], ends.at[1])
    )
    small()
    inlet = inlet_speed(start, 0)
    done = []
    for n, arrived in enumerate(halves):
        arrived()
        planes = range(2 * n, 2 * n + 2)
        results = []
        for plane in planes:
            kind = kinds[plane].astype(jnp.float32)
            kappa = kappa_of(gamma[plane], kind)
            cell[0, plane] = kappa
            cell[1, plane] = kind
            results.append(collide([f[i, plane] for i in range(27)], kappa, kind, rates, inlet))
        for plane, (out, values) in zip(planes, results):
            for i in range(27):
                post[i, plane] = out[i]
            for i in range(5):
                speed[i, plane] = values[i]
        part = slice(2 * n, 2 * n + 2)
        done.append(start_copies(sems.at[4 + n : 5 + n], (post.at[:, part], post_hbm.at[:, part])))
    done.append(start_copies(sems, (cell, cell_hbm), (speed, speed_hbm)))
    tail()

    def read(name, i, plane):
        if name == "adjoint":
            return ends[0, i - 18] if plane == 0 else ends[1, i]
        return {"post": post, "cell": cell}[name][i, plane]

    send_x(FIRST, read, to_odd, to_even)
    done.append(start_copies(sems.at[6:8], (to_odd, to_odd_hbm), (to_even, to_even_hbm)))
    for wait in done:
        wait()


def holding_kernel(*refs):
    half = len(refs) // 2
    for n in range(half):
        pltpu.make_async_copy(refs[n], refs[half + n], refs[-1].at[n]).start()
    for n in range(half):
        pltpu.make_async_copy(refs[n], refs[half + n], refs[-1].at[n]).wait()


def second_kernel(post, cotangent, cell, odd_x, even_x, to_odd, to_even):
    sources = {"post": post, "adjoint": cotangent, "cell": cell}

    def own(name, i, plane, first, rows):
        return sources[name][i, plane, first : first + rows]

    send_y(FIRST, own, odd_x, even_x, to_odd, to_even)


def start_copies(sems, *pairs):
    copies = [pltpu.make_async_copy(a, b, sems.at[n]) for n, (a, b) in enumerate(pairs)]
    for copy in copies:
        copy.start()

    def wait():
        for copy in copies:
            copy.wait()

    return wait


def put_block(wide, block, members):
    for i in range(members):
        wide[i, HALO : HALO + NX, NY : 2 * NY] = block[i]


def third_early_kernel(
    rates_hbm, start_hbm, post, cotangent, cell, odd_x, even_x,
    post_zero, post_one, post_two, wide_adjoint, wide_cell, speed_one, speed_two,
    rates, start, sems,
):
    wait = start_copies(sems, (rates_hbm, rates), (start_hbm, start))
    put_block(post_zero, post, 27)
    put_block(wide_adjoint, cotangent, 27)
    put_block(wide_cell, cell, 2)
    wide = {"post": post_zero, "adjoint": wide_adjoint, "cell": wide_cell}
    receive_x(FIRST, wide, odd_x, even_x)
    wait()
    forward(OWN, post_zero, post_one, wide_cell, speed_one, rates, inlet_speed(start, 1), 2)
    forward(OWN, post_one, post_two, wide_cell, speed_two, rates, inlet_speed(start, 2), 1)


def third_late_kernel(
    rates_hbm, start_hbm, _0, _1, _2, _3, _4, _5, _6, odd_y, even_y,
    post_zero, post_one, post_two, wide_adjoint, wide_cell, speed_one, speed_two,
    last_post, adjoint, gain, to_odd, to_even,
    rates, start, sems,
):
    wait = start_copies(sems, (rates_hbm, rates), (start_hbm, start))
    wide = {"post": post_zero, "adjoint": wide_adjoint, "cell": wide_cell}
    receive_y(FIRST, wide, odd_y, even_y)
    wait()
    forward(EDGE, post_zero, post_one, wide_cell, speed_one, rates, inlet_speed(start, 1), 2)
    forward(EDGE, post_one, post_two, wide_cell, speed_two, rates, inlet_speed(start, 2), 1)
    inlet = inlet_speed(start, 3)

    def load(n):
        plane = n + HALO
        return (
            pulled(post_two, plane, own_rows, 1), pulled(wide_adjoint, plane, own_rows, -1),
            own_rows(wide_cell, (0, plane)), own_rows(wide_cell, (1, plane)),
        )

    def work(f, h, kappa, kind):
        out, values = collide(f, kappa, kind, rates, inlet)
        return out, collide_back(h, kappa, kind, rates, values[:4], values[4])

    def store(n, result):
        out, (back, grad) = result
        for i in range(27):
            last_post[i, n] = out[i]
            adjoint[i, n] = back[i]
        gain[n] = grad

    planes_loop(0, NX, load, work, store)

    def read(name, i, plane):
        if name == "speed":
            return speed_two[i, plane + HALO, NY : 2 * NY]
        return {"post": last_post, "adjoint": adjoint}[name][i, plane]

    send_x(SECOND, read, to_odd, to_even)


def fourth_kernel(post, adjoint, speed, odd_x, even_x, to_odd, to_even):
    def own(name, i, plane, first, rows):
        if name == "speed":
            return speed[i, plane + HALO, NY + first : NY + first + rows]
        return {"post": post, "adjoint": adjoint}[name][i, plane, first : first + rows]

    send_y(SECOND, own, odd_x, even_x, to_odd, to_even)


def fifth_early_kernel(
    rates_hbm, post, adjoint, wide_cell, speed_one, _0, odd_x, even_x,
    speed_two, adjoint_three, adjoint_two, adjoint_one, wide_post, gain_two, gain_one,
    rates, sems,
):
    wait = start_copies(sems, (rates_hbm, rates))
    put_block(wide_post, post, 27)
    put_block(adjoint_three, adjoint, 27)
    wide = {"post": wide_post, "adjoint": adjoint_three, "speed": speed_two}
    receive_x(SECOND, wide, odd_x, even_x)
    wait()
    backward(OWN, adjoint_three, adjoint_two, wide_cell, speed_two, gain_two, rates, 2)
    backward(OWN, adjoint_two, adjoint_one, wide_cell, speed_one, gain_one, rates, 1)


def fifth_late_kernel(
    rates_hbm, wide_cell, speed_zero, speed_one, gain, porosity, odd_y, even_y, _0, _1, _2, _3, _4, _5, _6,
    flow, first_adjoint, sensitivity,
    speed_two, adjoint_three, adjoint_two, adjoint_one, wide_post, gain_two, gain_one,
    rates, flow_here, adjoint_here, sensitivity_here, sems,
):
    wait = start_copies(sems, (rates_hbm, rates))
    wide = {"post": wide_post, "adjoint": adjoint_three, "speed": speed_two}
    receive_y(SECOND, wide, odd_y, even_y)

    def run(n, carry):
        tiles = pulled(wide_post, n + HALO, own_rows, 1)
        for i in range(27):
            flow_here[i, n] = tiles[i]
        return carry

    lax.fori_loop(0, NX, run, 0)
    wait()
    wait = start_copies(sems, (flow_here, flow))
    backward(EDGE, adjoint_three, adjoint_two, wide_cell, speed_two, gain_two, rates, 2)
    backward(EDGE, adjoint_two, adjoint_one, wide_cell, speed_one, gain_one, rates, 1)

    def load(n):
        plane = n + HALO
        total = (gain[n] + own_rows(gain_two, (plane,))) + own_rows(gain_one, (plane,))
        ramp = RAMP_Q * (1.0 + DRAG_MAX) + (1.0 - DRAG_MAX * RAMP_Q) * porosity[n]
        slope = (DRAG_MAX * RAMP_Q * (1.0 + RAMP_Q)) / (ramp * ramp)
        kappa, kind = own_rows(wide_cell, (0, plane)), own_rows(wide_cell, (1, plane))
        values = [speed_zero[i, n] for i in range(5)]
        return pulled(adjoint_one, plane, own_rows, -1), kappa, kind, values, total, slope

    def work(h, kappa, kind, values, total, slope):
        out, grad = collide_back(h, kappa, kind, rates, values[:4], values[4])
        return out, jnp.where(kind < 0.5, slope * (total + grad), 0.0)

    def store(n, result):
        out, gradient = result
        for i in range(27):
            adjoint_here[i, n] = out[i]
        sensitivity_here[n] = gradient

    planes_loop(0, NX, load, work, store)
    last = start_copies(sems.at[1:3], (adjoint_here, first_adjoint), (sensitivity_here, sensitivity))
    wait()
    last()


def f32(*shape):
    return jax.ShapeDtypeStruct(shape, jnp.float32)


def call(kernel, far, arrays, outs, scratch=(), limit=VMEM_LIMIT, aliases=None, far_outs=0):
    hbm = pl.BlockSpec(memory_space=pltpu.HBM)
    vmem = pl.BlockSpec(memory_space=pltpu.VMEM)
    return pl.pallas_call(
        kernel,
        out_shape=tuple(f32(*s) for s in outs),
        in_specs=[hbm] * len(far) + [vmem] * len(arrays),
        out_specs=(hbm,) * far_outs + (vmem,) * (len(outs) - far_outs),
        scratch_shapes=[pltpu.VMEM(s, jnp.float32) if isinstance(s, tuple) else s for s in scratch],
        compiler_params=pltpu.CompilerParams(vmem_limit_bytes=limit),
        input_output_aliases=aliases or {},
        name=kernel.__name__,
    )(*far, *arrays)


def partners(axis, first):
    count = lax.axis_size(axis)
    return [[i % count, (i + 1) % count] for i in range(first, count + first, 2)]


def swap(value, axis, first):
    pairs = partners(axis, first)
    return lax.ppermute(value, axis, [(a, b) for a, b in pairs] + [(b, a) for a, b in pairs])


def exchange_x(to_odd, to_even):
    return swap(to_odd, "gx", 1), swap(to_even, "gx", 0)


def exchange_y(to_odd, to_even):
    from_odd = swap(to_odd, "gy", 1)
    return from_odd, lax.all_gather(to_even, "gy", axis_index_groups=partners("gy", 0))


def body(populations, cotangent, porosity, cell_type, rates, start_step):
    block = (27, NX, NY, LANES)
    wide = (27, PLANES, ROWS, LANES)
    tiles = (PLAN_X[FIRST, 1][1], NY, LANES), (PLAN_X[FIRST, -1][1], NY, LANES)
    rows = (PLAN_Y[FIRST, 1][1], LANES), (PLAN_Y[FIRST, -1][1], LANES)
    rates_here, start_here = pltpu.SMEM((27,), jnp.float32), pltpu.SMEM((1,), jnp.int32)
    post, cell, speed_zero, to_odd, to_even = call(
        first_kernel, (rates, start_step, populations, cotangent, porosity, cell_type), (),
        (block, (2, NX, NY, LANES), (5, NX, NY, LANES)) + tiles,
        (
            rates_here, start_here, block, (NX, NY, LANES), pltpu.VMEM((NX, NY, LANES), jnp.int32),
            (2, 9, NY, LANES), block, (2, NX, NY, LANES), (5, NX, NY, LANES), *tiles,
            pltpu.SemaphoreType.DMA((8,)),
        ),
        FIRST_LIMIT,
        far_outs=5,
    )
    kept = (post, cotangent, cell)
    post, held, cell = call(
        holding_kernel, kept, (), tuple(a.shape for a in kept), (pltpu.SemaphoreType.DMA((len(kept),)),)
    )
    x_halos = exchange_x(to_odd, to_even)
    to_odd, to_even = call(second_kernel, (), (post, held, cell) + x_halos, rows)
    y_halos = exchange_y(to_odd, to_even)
    wide_values = (5, PLANES, ROWS, LANES)
    wides = (wide, wide, wide, wide, (2, PLANES, ROWS, LANES), wide_values, wide_values)
    scalars = (rates_here, start_here, pltpu.SemaphoreType.DMA((2,)))
    wides = call(
        third_early_kernel, (rates, start_step), (post, held, cell) + x_halos, wides, scalars
    )
    tiles = (PLAN_X[SECOND, 1][1], NY, LANES), (PLAN_X[SECOND, -1][1], NY, LANES)
    rows = (PLAN_Y[SECOND, 1][1], LANES), (PLAN_Y[SECOND, -1][1], LANES)
    *wides, post, adjoint, gain, to_odd, to_even = call(
        third_late_kernel, (rates, start_step), tuple(wides) + y_halos,
        tuple(a.shape for a in wides) + (block, block, (NX, NY, LANES)) + tiles,
        scalars, aliases={2 + n: n for n in range(len(wides))},
    )
    wide_cell, speed_one, speed_two = wides[4:]
    x_halos = exchange_x(to_odd, to_even)
    to_odd, to_even = call(fourth_kernel, (), (post, adjoint, speed_two) + x_halos, rows)
    y_halos = exchange_y(to_odd, to_even)
    scalars = (rates_here, pltpu.SemaphoreType.DMA((1,)))
    wide_gain = (PLANES, ROWS, LANES)
    wides = call(
        fifth_early_kernel, (rates,), (post, adjoint, wide_cell, speed_one, speed_two) + x_halos,
        (wide_values, wide, wide, wide, wide, wide_gain, wide_gain), scalars, aliases={5: 0},
    )
    return call(
        fifth_late_kernel, (rates,),
        (wide_cell, speed_zero, speed_one, gain, porosity) + y_halos + tuple(wides),
        (block, block, (NX, NY, LANES)) + tuple(a.shape for a in wides),
        (rates_here, block, block, (NX, NY, LANES), pltpu.SemaphoreType.DMA((3,))),
        aliases={8 + n: 3 + n for n in range(len(wides))}, far_outs=3,
    )[:3]


def solution(mesh):
    return jax.shard_map(
        body,
        mesh=mesh,
        in_specs=(
            P(None, "gx", "gy", None),
            P(None, "gx", "gy", None),
            P("gx", "gy", None),
            P("gx", "gy", None),
            P(),
            P(),
        ),
        out_specs=(P(None, "gx", "gy", None), P(None, "gx", "gy", None), P("gx", "gy", None)),
        check_vma=False,
    )
```

```python
import jax
import jax.numpy as jnp
import numpy as np
from jax import lax
from jax.experimental import pallas as pl
from jax.experimental.pallas import tpu as pltpu
from jax.sharding import PartitionSpec as P

DRAG_MAX = 1.0
RAMP_Q = 0.1
INLET_SPEED = 0.3
PULSE_PERIOD = 64

NX, NY, LANES = 4, 8, 128
HALO = 3
TOGETHER = {6: 3, 4: 4, 2: 2}
PLANES = NX + 2 * HALO
ROWS = 3 * NY
VMEM_LIMIT = 16 * 1024 * 1024
FIRST_LIMIT = 64 * 1024 * 1024

SCALE = [
    float(s)
    for s in np.kron(np.kron([1 / 3, 1 / 2, 1 / 6], [1 / 3, 1 / 2, 1 / 6]), [1 / 3, 1 / 2, 1 / 6])
]
VEL = [(a - 1, b - 1, d - 1) for a in range(3) for b in range(3) for d in range(3)]
ODD = [(c[0] == 0) ^ (c[1] == 0) ^ (c[2] == 0) for c in VEL]


def reach(component, side, width, direction):
    inward = -side * direction
    return max(0, width - (0 if component == inward else 1 if component == 0 else 2))


def layers_x(field, i, side):
    _, _, kind, width, _, direction = field
    if kind == "stream":
        return 1, reach(VEL[i][0], side, width, direction)
    if kind == "strip":
        return (reach(VEL[i][0], side, width, direction),) * 2
    if kind == "next":
        return width, width if VEL[i][0] == -side * direction else 0
    return (width if kind == "ring" else 1), width


def layers_y(field, i, side, plane):
    _, _, kind, _, width, direction = field
    if kind in ("stream", "strip"):
        return 0, reach(VEL[i][1], side, width, direction)
    if kind == "next":
        return width - 1, width if VEL[i][1] == -side * direction else 0
    return (width - 1 if kind == "ring" and -width < plane < NX + width - 1 else 0), width


def strip_rows(field, i):
    return {1: (NY - 2, NY - 1), 0: (0, NY - 1), -1: (0, 1)}[VEL[i][1] * field[5]]


def plan_x(fields, side):
    places, strips, tile = {}, [], 0
    for field in fields:
        for layer in range(1, NX):
            for i in range(field[1]):
                first, last = layers_x(field, i, side)
                if not first <= layer <= last:
                    continue
                if field[2] == "strip":
                    strips.append((field, i, layer))
                else:
                    places[field, i, layer] = tile, 0
                    tile += 1
    for n, key in enumerate(strips):
        places[key] = tile + n // (NY // 2), n % (NY // 2) * 2
    return places, tile - (-len(strips) // (NY // 2))


def plan_y(fields, side):
    entries, start = [], 0
    for field in fields:
        for plane in range(1 - NX, 2 * NX - 1):
            for i in range(field[1]):
                if plane < 0 or plane >= NX:
                    first, last = layers_x(field, i, -1 if plane < 0 else 1)
                    inner = field[2] == "ring" and -field[3] < plane < NX + field[3] - 1
                    if not inner and not first <= (-plane if plane < 0 else plane - NX + 1) <= last:
                        continue
                elif field[2] in ("strip", "next"):
                    continue
                skip, last = layers_y(field, i, side, plane)
                if last > skip:
                    entries.append((field, i, plane, start, skip, last - skip))
                    start += last - skip
    return entries, -(-start // 8) * 8


FIRST = (
    ("post", 27, "stream", 2, 3, 1), ("strip", 27, "strip", 3, 2, 1), ("next", 27, "next", 2, 2, 1),
    ("adjoint", 27, "stream", 1, 1, -1), ("cell", 2, "plain", 2, 2, 0),
)
SECOND = (
    ("adjoint", 27, "stream", 2, 3, -1), ("strip", 27, "strip", 3, 2, -1), ("next", 27, "next", 2, 2, -1),
    ("post", 27, "stream", 1, 1, 1), ("speed", 4, "ring", 2, 2, 0),
)
PLAN_X = {(f, s): plan_x(f, s) for f in (FIRST, SECOND) for s in (-1, 1)}
PLAN_Y = {(f, s): plan_y(f, s) for f in (FIRST, SECOND) for s in (-1, 1)}


def pack_x(fields, side, read, out):
    for (field, i, layer), (tile, row) in PLAN_X[fields, side][0].items():
        value = read(field[0], i, layer - 1 if side > 0 else NX - layer)
        if field[2] == "strip":
            low, high = strip_rows(field, i)
            out[tile, row : row + 1] = value[low : low + 1]
            out[tile, row + 1 : row + 2] = value[high : high + 1]
        else:
            out[tile] = value


def halo_rows(fields, from_low, from_high, field, i, plane, first, rows):
    ref, side, layer = (from_low, -1, -plane) if plane < 0 else (from_high, 1, plane - NX + 1)
    tile, row = PLAN_X[fields, side][0][field, i, layer]
    if field[2] == "strip":
        first = strip_rows(field, i).index(first)
    return ref[tile, row + first : row + first + rows]


def pack_y(fields, side, own, from_low, from_high, out):
    for field, i, plane, start, skip, rows in PLAN_Y[fields, side][0]:
        first = skip if side > 0 else NY - skip - rows
        if 0 <= plane < NX or (field[2] == "ring" and -field[3] < plane < NX + field[3] - 1):
            out[start : start + rows] = own(field[0], i, plane, first, rows)
        else:
            out[start : start + rows] = halo_rows(fields, from_low, from_high, field, i, plane, first, rows)


def by_parity(axis, run, from_odd, from_even):
    parity = lax.axis_index(axis) % 2

    @pl.when(parity == 0)
    def _():
        run(from_odd, from_even)

    @pl.when(parity == 1)
    def _():
        run(from_even, from_odd)


def unpack_x(fields, wide, *from_x):
    for side, ref in zip((-1, 1), from_x):
        for (field, i, layer), (tile, row) in PLAN_X[fields, side][0].items():
            plane = (NX - 1 + layer if side > 0 else -layer) + HALO
            if field[2] == "strip":
                for n, at in enumerate(strip_rows(field, i)):
                    wide[field[0]][i, plane, NY + at : NY + at + 1] = ref[tile, row + n : row + n + 1]
            else:
                wide[field[0]][i, plane, NY : 2 * NY] = ref[tile]


def unpack_y(fields, wide, *from_y):
    for side, ref in zip((-1, 1), from_y):
        for field, i, plane, start, skip, rows in PLAN_Y[fields, side][0]:
            first = 2 * NY + skip if side > 0 else NY - skip - rows
            wide[field[0]][i, plane + HALO, first : first + rows] = ref[start : start + rows]


def receive_x(fields, wide, odd_x, even_x):
    by_parity("gx", lambda low, high: unpack_x(fields, wide, low, high), odd_x, even_x)


def receive_y(fields, wide, odd_y, even_y):
    partner = even_y.at[1 - lax.axis_index("gy") % 2]
    by_parity("gy", lambda low, high: unpack_y(fields, wide, low, high), odd_y, partner)


def send_x(fields, read, to_odd, to_even):
    def run(to_low, to_high):
        pack_x(fields, 1, read, to_low)
        pack_x(fields, -1, read, to_high)

    by_parity("gx", run, to_odd, to_even)


def send_y(fields, own, odd_x, even_x, to_odd, to_even):
    def with_halo(from_low, from_high):
        def run(to_low, to_high):
            pack_y(fields, 1, own, from_low, from_high, to_low)
            pack_y(fields, -1, own, from_low, from_high, to_high)

        by_parity("gy", run, to_odd, to_even)

    by_parity("gx", with_halo, odd_x, even_x)


def moments(f):
    v = list(f)
    for stride in (9, 3, 1):
        for i in range(27):
            if (i // stride) % 3 == 0:
                a, b, c = v[i], v[i + stride], v[i + 2 * stride]
                s = (a + c) + b
                v[i], v[i + stride], v[i + 2 * stride] = s, c - a, s - 3.0 * b
    return v


def moments_transposed(m):
    v = list(m)
    for stride in (9, 3, 1):
        for i in range(27):
            if (i // stride) % 3 == 0:
                s, d, q = v[i], v[i + stride], v[i + 2 * stride]
                t = s + q
                v[i], v[i + stride], v[i + 2 * stride] = t - d, s - (q + q), t + d
    return v


def rate_of(rates, i, relaxing, even, odd):
    return jnp.where(relaxing, rates[i], odd if ODD[i] else even)


def kinds_of(kind):
    relaxing = kind < 1.5
    even = jnp.where((kind > 1.5) & (kind < 3.5), 1.0, 0.0)
    odd = jnp.where(kind > 3.5, 2.0, even)
    return relaxing, even, odd


def collide(f, kappa, kind, rates, inlet):
    m = moments(f)
    relaxing, even, odd = kinds_of(kind)
    rho = m[0]
    inverse = 1.0 / rho
    ux, uy, uz = m[9] * inverse, m[3] * inverse, m[1] * inverse
    vx, vy = kappa * ux, kappa * uy
    vz = jnp.where((kind > 1.5) & (kind < 2.5), inlet, kappa * uz)
    den = jnp.where(relaxing, rho, 1.0)
    jx, jy, jz = den * vx, den * vy, den * vz
    xy, xz, yz = jx * vy, jx * vz, jy * vz
    xx, yy, zz = 3.0 * (jx * vx), 3.0 * (jy * vy), 3.0 * (jz * vz)
    x2, y2, z2 = xx - den, yy - den, zz - den
    e = [None] * 27
    e[0] = den
    e[18], e[6], e[2] = x2, y2, z2
    e[24], e[20], e[8] = -(x2 + yy), -(x2 + zz), -(y2 + zz)
    e[26] = (x2 + yy) + zz
    e[9], e[15], e[11], e[17] = jx, -jx, -jx, jx
    e[3], e[21], e[5], e[23] = jy, -jy, -jy, jy
    e[1], e[19], e[7], e[25] = jz, -jz, -jz, jz
    e[12], e[14] = xy, -xy
    e[10], e[16] = xz, -xz
    e[4], e[22] = yz, -yz
    out = []
    for i in range(27):
        rate = rate_of(rates, i, relaxing, even, odd)
        gap = -m[i] if e[i] is None else e[i] - m[i]
        out.append(SCALE[i] * (m[i] + rate * gap))
    return moments_transposed(out), (ux, uy, uz, inverse, rho)


def collide_back(h, kappa, kind, rates, speed, rho=None):
    y = moments(h)
    relaxing, even, odd = kinds_of(kind)
    ux, uy, uz, inverse = speed
    w, z = [], []
    for i in range(27):
        yi = SCALE[i] * y[i]
        wi = rate_of(rates, i, relaxing, even, odd) * yi
        w.append(wi)
        z.append(yi - wi)
    vx, vy, vz = kappa * ux, kappa * uy, kappa * uz
    w222 = w[26]
    a_x = (w[18] - w[24]) - (w[20] - w222)
    a_y = (w[6] - w[24]) - (w[8] - w222)
    a_z = (w[2] - w[20]) - (w[8] - w222)
    b_x = (w[9] - w[15]) - (w[11] - w[17])
    b_y = (w[3] - w[21]) - (w[5] - w[23])
    b_z = (w[1] - w[19]) - (w[7] - w[25])
    c_xy, c_xz, c_yz = w[12] - w[14], w[10] - w[16], w[4] - w[22]
    base = ((w[0] - w[18]) - (w[6] + w[2])) + ((w[24] + w[20]) + (w[8] - w222))
    p_x, p_y, p_z = 3.0 * (a_x * vx), 3.0 * (a_y * vy), 3.0 * (a_z * vz)
    q_x, q_y, q_z = c_xy * vy + c_xz * vz, c_xy * vx + c_yz * vz, c_xz * vx + c_yz * vy
    r_x, r_y, r_z = b_x + p_x, b_y + p_y, b_z + p_z
    value = base + vx * (r_x + 0.5 * q_x) + vy * (r_y + 0.5 * q_y) + vz * (r_z + 0.5 * q_z)
    g_x, g_y, g_z = r_x + p_x + q_x, r_y + p_y + q_y, r_z + p_z + q_z
    factor = jnp.where(relaxing, kappa, kappa * inverse)
    along = ux * g_x + uy * g_y + uz * g_z
    z[0] = z[0] + (jnp.where(relaxing, value, 0.0) - factor * along)
    z[9] = z[9] + factor * g_x
    z[3] = z[3] + factor * g_y
    z[1] = z[1] + factor * g_z
    return moments_transposed(z), None if rho is None else rho * along


def turned(value, shift):
    return value if shift == 0 else pltpu.roll(value, shift % LANES, axis=1)


def own_rows(ref, place):
    return ref[place + (slice(NY, 2 * NY),)]


def edge_rows(ref, place):
    low, high = ref[place + (slice(NY - 2, 2 * NY - 2),)], ref[place + (slice(NY + 2, 2 * NY + 2),)]
    return jnp.where(lax.broadcasted_iota(jnp.int32, (NY, LANES), 0) < NY // 2, low, high)


def put_edge_rows(ref, place, value):
    ref[place + (slice(NY - 2, NY + 2),)] = value[: NY // 2]
    ref[place + (slice(2 * NY - 2, 2 * NY + 2),)] = value[NY // 2 :]


def put_own_rows(ref, place, value):
    ref[place + (slice(NY, 2 * NY),)] = value


def put_narrow_edge_rows(ref, place, value):
    ref[place + (slice(NY - 1, NY + 1),)] = value[1:3]
    ref[place + (slice(2 * NY - 1, 2 * NY + 1),)] = value[5:7]


OWN = (own_rows, put_own_rows)
OUTER = (HALO - 2, HALO + NX + 1)
EDGE = (edge_rows, put_edge_rows)
NARROW_EDGE = (edge_rows, put_narrow_edge_rows)


def shifted(wide, shift):
    class View:
        def __getitem__(self, place):
            return wide[place[:-1] + (slice(place[-1].start + shift, place[-1].stop + shift),)]

    return View()


def pulled(wide, plane, rows, direction):
    tiles = []
    for i, (cx, cy, cz) in enumerate(VEL):
        tile = rows(shifted(wide, -direction * cy), (i, plane - direction * cx))
        tiles.append(turned(tile, direction * cz))
    return tiles


def planes_loop(first, last, load, work, store, step=1):
    together = TOGETHER[last - first]

    def body(n, carry):
        planes = [first + together * n + k * step for k in range(together)]
        loaded = [load(plane) for plane in planes]
        results = [work(*values) for values in loaded]
        for plane, result in zip(planes, results):
            store(plane, result)
        return carry

    lax.fori_loop(0, (last - first) // together, body, 0)


def put_inner(ahead, direction, load, work):
    results = [work(*values) for values in [load(1), load(NX - 2)]]
    for n, out in enumerate(results):
        for i in range(27):
            if VEL[i][0] == (direction if n else -direction):
                ahead[n, i] = out[i]


def forward(where, source, target, cell, speed, rates, inlet, outer=False):
    get, put = where

    def load(plane):
        return pulled(source, plane, get, 1), get(cell, (0, plane)), get(cell, (1, plane))

    def work(f, kappa, kind):
        return collide(f, kappa, kind, rates, inlet)

    def store(plane, result):
        out, values = result
        for i in range(27):
            put(target, (i, plane), out[i])
        if not outer:
            for i in range(5):
                put(speed, (i, plane), values[i])

    if outer:
        planes_loop(OUTER[0], OUTER[0] + 2, load, work, store, OUTER[1] - OUTER[0])
    else:
        planes_loop(HALO - 1, HALO + NX + 1, load, work, store)


def backward(where, source, target, cell, speed, gain, rates, outer=False):
    get, put = where

    def load(plane):
        values = [get(speed, (i, plane)) for i in range(5)]
        return pulled(source, plane, get, -1), get(cell, (0, plane)), get(cell, (1, plane)), values

    def work(h, kappa, kind, values):
        return collide_back(h, kappa, kind, rates, values[:4], values[4])

    def store(plane, result):
        out, grad = result
        for i in range(27):
            put(target, (i, plane), out[i])
        if not outer:
            put(gain, (plane,), grad)

    if outer:
        planes_loop(OUTER[0], OUTER[0] + 2, load, work, store, OUTER[1] - OUTER[0])
    else:
        planes_loop(HALO - 1, HALO + NX + 1, load, work, store)


def inlet_speed(start, step):
    time = jnp.full((NY, LANES), (start[0] + step) % PULSE_PERIOD, jnp.int32).astype(jnp.float32)
    return INLET_SPEED * jnp.sin(time * (2.0 * np.pi / PULSE_PERIOD))


def kappa_of(porosity, kind):
    damping = (RAMP_Q + porosity) / (
        RAMP_Q * (1.0 + DRAG_MAX) + (1.0 - DRAG_MAX * RAMP_Q) * porosity
    )
    return jnp.where(kind < 0.5, damping, jnp.where((kind > 2.5) & (kind < 3.5), 1.0, 0.0))


def first_kernel(
    rates_hbm, start_hbm, populations, cotangent, porosity, cell_type,
    post_hbm, cell_hbm, speed_hbm, to_odd_hbm, to_even_hbm,
    rates, start, f, gamma, kinds, ends, post, cell, speed, to_odd, to_even, ahead, sems,
):
    small = start_copies(
        sems, (rates_hbm, rates), (start_hbm, start), (porosity, gamma), (cell_type, kinds)
    )
    halves = [
        start_copies(sems.at[4 + n : 5 + n], (populations.at[:, 2 * n : 2 * n + 2], f.at[:, 2 * n : 2 * n + 2]))
        for n in range(NX // 2)
    ]
    tail = start_copies(
        sems.at[6:8], (cotangent.at[18:27, 0], ends.at[0]), (cotangent.at[0:9, NX - 1], ends.at[1])
    )
    small()
    inlet = inlet_speed(start, 0)
    done = []
    for n, arrived in enumerate(halves):
        arrived()
        planes = range(2 * n, 2 * n + 2)
        results = []
        for plane in planes:
            kind = kinds[plane].astype(jnp.float32)
            kappa = kappa_of(gamma[plane], kind)
            cell[0, plane] = kappa
            cell[1, plane] = kind
            results.append(collide([f[i, plane] for i in range(27)], kappa, kind, rates, inlet))
        for plane, (out, values) in zip(planes, results):
            for i in range(27):
                post[i, plane, NY : 2 * NY] = out[i]
            for i in range(5):
                speed[i, plane] = values[i]
        part = slice(2 * n, 2 * n + 2)
        done.append(start_copies(sems.at[4 + n : 5 + n], (post.at[:, part, NY : 2 * NY], post_hbm.at[:, part])))
    done.append(start_copies(sems, (cell, cell_hbm), (speed, speed_hbm)))
    later = inlet_speed(start, 1)
    put_inner(
        ahead, 1,
        lambda plane: (pulled(post, plane, own_rows, 1), cell[0, plane], cell[1, plane]),
        lambda f, kappa, kind: collide(f, kappa, kind, rates, later)[0],
    )
    tail()

    def read(name, i, plane):
        if name == "adjoint":
            return ends[0, i - 18] if plane == 0 else ends[1, i]
        if name == "next":
            return ahead[plane - 1, i]
        return cell[i, plane] if name == "cell" else post[i, plane, NY : 2 * NY]

    send_x(FIRST, read, to_odd, to_even)
    done.append(start_copies(sems.at[6:8], (to_odd, to_odd_hbm), (to_even, to_even_hbm)))
    for wait in done:
        wait()


def holding_kernel(*refs):
    half = len(refs) // 2
    for n in range(half):
        pltpu.make_async_copy(refs[n], refs[half + n], refs[-1].at[n]).start()
    for n in range(half):
        pltpu.make_async_copy(refs[n], refs[half + n], refs[-1].at[n]).wait()


def second_kernel(post, cotangent, cell, odd_x, even_x, to_odd, to_even):
    sources = {"post": post, "adjoint": cotangent, "cell": cell}

    def own(name, i, plane, first, rows):
        return sources[name][i, plane, first : first + rows]

    send_y(FIRST, own, odd_x, even_x, to_odd, to_even)


def start_copies(sems, *pairs):
    copies = [pltpu.make_async_copy(a, b, sems.at[n]) for n, (a, b) in enumerate(pairs)]
    for copy in copies:
        copy.start()

    def wait():
        for copy in copies:
            copy.wait()

    return wait


def put_block(wide, block, members):
    for i in range(members):
        wide[i, HALO : HALO + NX, NY : 2 * NY] = block[i]


def third_early_kernel(
    rates_hbm, start_hbm, post, cotangent, cell, odd_x, even_x,
    post_zero, post_one, post_two, wide_adjoint, wide_cell, speed_one, speed_two,
    rates, start, sems,
):
    wait = start_copies(sems, (rates_hbm, rates), (start_hbm, start))
    put_block(post_zero, post, 27)
    put_block(wide_adjoint, cotangent, 27)
    put_block(wide_cell, cell, 2)
    wide = {"post": post_zero, "strip": post_zero, "next": post_one, "adjoint": wide_adjoint, "cell": wide_cell}
    receive_x(FIRST, wide, odd_x, even_x)
    wait()
    forward(OWN, post_zero, post_one, wide_cell, speed_one, rates, inlet_speed(start, 1))
    forward(OWN, post_one, post_two, wide_cell, speed_two, rates, inlet_speed(start, 2))


def third_late_kernel(
    rates_hbm, start_hbm, _0, _1, _2, _3, _4, _5, _6, odd_y, even_y,
    post_zero, post_one, post_two, wide_adjoint, wide_cell, speed_one, speed_two,
    last_post, adjoint, gain, to_odd, to_even,
    rates, start, inner, ahead, sems,
):
    wait = start_copies(sems, (rates_hbm, rates), (start_hbm, start))
    wide = {"post": post_zero, "strip": post_zero, "next": post_one, "adjoint": wide_adjoint, "cell": wide_cell}
    receive_y(FIRST, wide, odd_y, even_y)
    wait()
    inlet = inlet_speed(start, 1)
    forward(NARROW_EDGE, post_zero, post_one, wide_cell, speed_one, rates, inlet, True)
    forward(EDGE, post_zero, post_one, wide_cell, speed_one, rates, inlet)
    forward(EDGE, post_one, post_two, wide_cell, speed_two, rates, inlet_speed(start, 2))
    inlet = inlet_speed(start, 3)

    def load(n):
        plane = n + HALO
        return (
            pulled(post_two, plane, own_rows, 1), pulled(wide_adjoint, plane, own_rows, -1),
            own_rows(wide_cell, (0, plane)), own_rows(wide_cell, (1, plane)),
        )

    def work(f, h, kappa, kind):
        out, values = collide(f, kappa, kind, rates, inlet)
        return out, collide_back(h, kappa, kind, rates, values[:4], values[4])

    def store(n, result):
        out, (back, grad) = result
        for i in range(27):
            last_post[i, n] = out[i]
            adjoint[i, n] = back[i]
            inner[i, n, NY : 2 * NY] = back[i]
        gain[n] = grad

    planes_loop(0, NX, load, work, store)

    def load_inner(n):
        plane = n + HALO
        values = [own_rows(speed_two, (i, plane)) for i in range(4)]
        return (
            pulled(inner, n, own_rows, -1), own_rows(wide_cell, (0, plane)), own_rows(wide_cell, (1, plane)), values
        )

    def work_inner(h, kappa, kind, values):
        return collide_back(h, kappa, kind, rates, values)[0]

    put_inner(ahead, -1, load_inner, work_inner)

    def read(name, i, plane):
        if name == "speed":
            return speed_two[i, plane + HALO, NY : 2 * NY]
        if name == "next":
            return ahead[plane - 1, i]
        return {"post": last_post, "adjoint": adjoint, "strip": adjoint}[name][i, plane]

    send_x(SECOND, read, to_odd, to_even)


def fourth_kernel(post, adjoint, speed, odd_x, even_x, to_odd, to_even):
    def own(name, i, plane, first, rows):
        if name == "speed":
            return speed[i, plane + HALO, NY + first : NY + first + rows]
        return {"post": post, "adjoint": adjoint}[name][i, plane, first : first + rows]

    send_y(SECOND, own, odd_x, even_x, to_odd, to_even)


def fifth_early_kernel(
    rates_hbm, post, adjoint, wide_cell, speed_one, _0, odd_x, even_x,
    speed_two, adjoint_three, adjoint_two, adjoint_one, wide_post, gain_two, gain_one,
    rates, sems,
):
    wait = start_copies(sems, (rates_hbm, rates))
    put_block(wide_post, post, 27)
    put_block(adjoint_three, adjoint, 27)
    wide = {
        "post": wide_post, "adjoint": adjoint_three, "strip": adjoint_three, "next": adjoint_two, "speed": speed_two
    }
    receive_x(SECOND, wide, odd_x, even_x)
    wait()
    backward(OWN, adjoint_three, adjoint_two, wide_cell, speed_two, gain_two, rates)
    backward(OWN, adjoint_two, adjoint_one, wide_cell, speed_one, gain_one, rates)


def fifth_late_kernel(
    rates_hbm, wide_cell, speed_zero, speed_one, gain, porosity, odd_y, even_y, _0, _1, _2, _3, _4, _5, _6,
    flow, first_adjoint, sensitivity,
    speed_two, adjoint_three, adjoint_two, adjoint_one, wide_post, gain_two, gain_one,
    rates, flow_here, adjoint_here, sensitivity_here, sems,
):
    wait = start_copies(sems, (rates_hbm, rates))
    wide = {
        "post": wide_post, "adjoint": adjoint_three, "strip": adjoint_three, "next": adjoint_two, "speed": speed_two
    }
    receive_y(SECOND, wide, odd_y, even_y)

    def run(n, carry):
        tiles = pulled(wide_post, n + HALO, own_rows, 1)
        for i in range(27):
            flow_here[i, n] = tiles[i]
        return carry

    lax.fori_loop(0, NX, run, 0)
    wait()
    wait = start_copies(sems, (flow_here, flow))
    backward(NARROW_EDGE, adjoint_three, adjoint_two, wide_cell, speed_two, gain_two, rates, True)
    backward(EDGE, adjoint_three, adjoint_two, wide_cell, speed_two, gain_two, rates)
    backward(EDGE, adjoint_two, adjoint_one, wide_cell, speed_one, gain_one, rates)

    def load(n):
        plane = n + HALO
        total = (gain[n] + own_rows(gain_two, (plane,))) + own_rows(gain_one, (plane,))
        ramp = RAMP_Q * (1.0 + DRAG_MAX) + (1.0 - DRAG_MAX * RAMP_Q) * porosity[n]
        slope = (DRAG_MAX * RAMP_Q * (1.0 + RAMP_Q)) / (ramp * ramp)
        kappa, kind = own_rows(wide_cell, (0, plane)), own_rows(wide_cell, (1, plane))
        values = [speed_zero[i, n] for i in range(5)]
        return pulled(adjoint_one, plane, own_rows, -1), kappa, kind, values, total, slope

    def work(h, kappa, kind, values, total, slope):
        out, grad = collide_back(h, kappa, kind, rates, values[:4], values[4])
        return out, jnp.where(kind < 0.5, slope * (total + grad), 0.0)

    def store(n, result):
        out, gradient = result
        for i in range(27):
            adjoint_here[i, n] = out[i]
        sensitivity_here[n] = gradient

    planes_loop(0, NX, load, work, store)
    last = start_copies(sems.at[1:3], (adjoint_here, first_adjoint), (sensitivity_here, sensitivity))
    wait()
    last()


def f32(*shape):
    return jax.ShapeDtypeStruct(shape, jnp.float32)


def call(kernel, far, arrays, outs, scratch=(), limit=VMEM_LIMIT, aliases=None, far_outs=0):
    hbm = pl.BlockSpec(memory_space=pltpu.HBM)
    vmem = pl.BlockSpec(memory_space=pltpu.VMEM)
    return pl.pallas_call(
        kernel,
        out_shape=tuple(f32(*s) for s in outs),
        in_specs=[hbm] * len(far) + [vmem] * len(arrays),
        out_specs=(hbm,) * far_outs + (vmem,) * (len(outs) - far_outs),
        scratch_shapes=[pltpu.VMEM(s, jnp.float32) if isinstance(s, tuple) else s for s in scratch],
        compiler_params=pltpu.CompilerParams(vmem_limit_bytes=limit),
        input_output_aliases=aliases or {},
        name=kernel.__name__,
    )(*far, *arrays)


def partners(axis, first):
    count = lax.axis_size(axis)
    return [[i % count, (i + 1) % count] for i in range(first, count + first, 2)]


def swap(value, axis, first):
    pairs = partners(axis, first)
    return lax.ppermute(value, axis, [(a, b) for a, b in pairs] + [(b, a) for a, b in pairs])


def exchange_x(to_odd, to_even):
    return swap(to_odd, "gx", 1), swap(to_even, "gx", 0)


def exchange_y(to_odd, to_even):
    from_odd = swap(to_odd, "gy", 1)
    return from_odd, lax.all_gather(to_even, "gy", axis_index_groups=partners("gy", 0))


def body(populations, cotangent, porosity, cell_type, rates, start_step):
    block = (27, NX, NY, LANES)
    wide = (27, PLANES, ROWS, LANES)
    inner, ahead = (27, NX, ROWS, LANES), (2, 27, NY, LANES)
    tiles = (PLAN_X[FIRST, 1][1], NY, LANES), (PLAN_X[FIRST, -1][1], NY, LANES)
    rows = (PLAN_Y[FIRST, 1][1], LANES), (PLAN_Y[FIRST, -1][1], LANES)
    rates_here, start_here = pltpu.SMEM((27,), jnp.float32), pltpu.SMEM((1,), jnp.int32)
    post, cell, speed_zero, to_odd, to_even = call(
        first_kernel, (rates, start_step, populations, cotangent, porosity, cell_type), (),
        (block, (2, NX, NY, LANES), (5, NX, NY, LANES)) + tiles,
        (
            rates_here, start_here, block, (NX, NY, LANES), pltpu.VMEM((NX, NY, LANES), jnp.int32),
            (2, 9, NY, LANES), inner, (2, NX, NY, LANES), (5, NX, NY, LANES), *tiles, ahead,
            pltpu.SemaphoreType.DMA((8,)),
        ),
        FIRST_LIMIT,
        far_outs=5,
    )
    kept = (post, cotangent, cell)
    post, held, cell = call(
        holding_kernel, kept, (), tuple(a.shape for a in kept), (pltpu.SemaphoreType.DMA((len(kept),)),)
    )
    x_halos = exchange_x(to_odd, to_even)
    to_odd, to_even = call(second_kernel, (), (post, held, cell) + x_halos, rows)
    y_halos = exchange_y(to_odd, to_even)
    wide_values = (5, PLANES, ROWS, LANES)
    wides = (wide, wide, wide, wide, (2, PLANES, ROWS, LANES), wide_values, wide_values)
    scalars = (rates_here, start_here, pltpu.SemaphoreType.DMA((2,)))
    wides = call(
        third_early_kernel, (rates, start_step), (post, held, cell) + x_halos, wides, scalars
    )
    tiles = (PLAN_X[SECOND, 1][1], NY, LANES), (PLAN_X[SECOND, -1][1], NY, LANES)
    rows = (PLAN_Y[SECOND, 1][1], LANES), (PLAN_Y[SECOND, -1][1], LANES)
    *wides, post, adjoint, gain, to_odd, to_even = call(
        third_late_kernel, (rates, start_step), tuple(wides) + y_halos,
        tuple(a.shape for a in wides) + (block, block, (NX, NY, LANES)) + tiles,
        scalars[:2] + (inner, ahead) + scalars[2:], aliases={2 + n: n for n in range(len(wides))},
    )
    wide_cell, speed_one, speed_two = wides[4:]
    x_halos = exchange_x(to_odd, to_even)
    to_odd, to_even = call(fourth_kernel, (), (post, adjoint, speed_two) + x_halos, rows)
    y_halos = exchange_y(to_odd, to_even)
    scalars = (rates_here, pltpu.SemaphoreType.DMA((1,)))
    wide_gain = (PLANES, ROWS, LANES)
    wides = call(
        fifth_early_kernel, (rates,), (post, adjoint, wide_cell, speed_one, speed_two) + x_halos,
        (wide_values, wide, wide, wide, wide, wide_gain, wide_gain), scalars, aliases={5: 0},
    )
    return call(
        fifth_late_kernel, (rates,),
        (wide_cell, speed_zero, speed_one, gain, porosity) + y_halos + tuple(wides),
        (block, block, (NX, NY, LANES)) + tuple(a.shape for a in wides),
        (rates_here, block, block, (NX, NY, LANES), pltpu.SemaphoreType.DMA((3,))),
        aliases={8 + n: 3 + n for n in range(len(wides))}, far_outs=3,
    )[:3]


def solution(mesh):
    return jax.shard_map(
        body,
        mesh=mesh,
        in_specs=(
            P(None, "gx", "gy", None),
            P(None, "gx", "gy", None),
            P("gx", "gy", None),
            P("gx", "gy", None),
            P(),
            P(),
        ),
        out_specs=(P(None, "gx", "gy", None), P(None, "gx", "gy", None), P("gx", "gy", None)),
        check_vma=False,
    )
```

```python
import jax
import jax.numpy as jnp
import numpy as np
from jax import lax
from jax.experimental import pallas as pl
from jax.experimental.pallas import tpu as pltpu
from jax.sharding import PartitionSpec as P

DRAG_MAX = 1.0
RAMP_Q = 0.1
INLET_SPEED = 0.3
PULSE_PERIOD = 64

NX, NY, LANES = 4, 8, 128
HALO = 3
PLANES = NX + 2 * HALO
ROWS = 3 * NY
VMEM_LIMIT = 16 * 1024 * 1024
FIRST_LIMIT = 64 * 1024 * 1024

SCALE = [
    float(s)
    for s in np.kron(np.kron([1 / 3, 1 / 2, 1 / 6], [1 / 3, 1 / 2, 1 / 6]), [1 / 3, 1 / 2, 1 / 6])
]
VEL = [(a - 1, b - 1, d - 1) for a in range(3) for b in range(3) for d in range(3)]
ODD = [(c[0] == 0) ^ (c[1] == 0) ^ (c[2] == 0) for c in VEL]


def reach(component, side, width, direction):
    inward = -side * direction
    return max(0, width - (0 if component == inward else 1 if component == 0 else 2))


def layers_x(field, i, side):
    _, _, kind, width, _, direction = field
    if kind == "stream":
        return 1, reach(VEL[i][0], side, width, direction)
    if kind == "strip":
        return (reach(VEL[i][0], side, width, direction),) * 2
    if kind == "next":
        return width, width if VEL[i][0] == -side * direction else 0
    return (width if kind == "corner" else 1), 0 if kind == "ring" else width


def layers_y(field, i, side, plane):
    _, _, kind, _, width, direction = field
    if kind in ("stream", "strip"):
        return 0, reach(VEL[i][1], side, width, direction)
    if kind == "next":
        return width - 1, width if VEL[i][1] == -side * direction else 0
    return (width - 1 if kind == "ring" else 0), width


def strip_rows(field, i):
    return {1: (NY - 2, NY - 1), 0: (0, NY - 1), -1: (0, 1)}[VEL[i][1] * field[5]]


def plan_x(fields, side):
    places, strips, tile = {}, [], 0
    for field in fields:
        for layer in range(1, NX):
            for i in range(field[1]):
                first, last = layers_x(field, i, side)
                if not first <= layer <= last:
                    continue
                if field[2] in ("strip", "corner"):
                    strips.append((field, i, layer))
                else:
                    places[field, i, layer] = tile, 0
                    tile += 1
    for n, key in enumerate(strips):
        places[key] = tile + n // (NY // 2), n % (NY // 2) * 2
    return places, tile - (-len(strips) // (NY // 2))


def plan_y(fields, side):
    entries, start = [], 0
    for field in fields:
        for plane in range(1 - NX, 2 * NX - 1):
            for i in range(field[1]):
                if plane < 0 or plane >= NX:
                    first, last = layers_x(field, i, -1 if plane < 0 else 1)
                    inner = field[2] == "ring" and -field[3] < plane < NX + field[3] - 1
                    if not inner and not first <= (-plane if plane < 0 else plane - NX + 1) <= last:
                        continue
                elif field[2] in ("strip", "next", "corner"):
                    continue
                skip, last = layers_y(field, i, side, plane)
                if last > skip:
                    entries.append((field, i, plane, start, skip, last - skip))
                    start += last - skip
    return entries, -(-start // 8) * 8


FIRST = (
    ("post", 27, "stream", 2, 3, 1), ("strip", 27, "strip", 3, 2, 1), ("next", 27, "next", 2, 2, 1),
    ("adjoint", 27, "stream", 1, 1, -1), ("cell", 2, "plain", 1, 2, 0), ("corner", 2, "corner", 2, 1, 0),
)
SECOND = (
    ("adjoint", 27, "stream", 2, 3, -1), ("strip", 27, "strip", 3, 2, -1), ("next", 27, "next", 2, 2, -1),
    ("post", 27, "stream", 1, 1, 1), ("speed", 4, "ring", 2, 2, 0), ("corner", 4, "corner", 2, 1, 0),
)
PLAN_X = {(f, s): plan_x(f, s) for f in (FIRST, SECOND) for s in (-1, 1)}
PLAN_Y = {(f, s): plan_y(f, s) for f in (FIRST, SECOND) for s in (-1, 1)}


def pack_x(fields, side, read, out):
    for (field, i, layer), (tile, row) in PLAN_X[fields, side][0].items():
        value = read(field[0], i, layer - 1 if side > 0 else NX - layer)
        if field[2] in ("strip", "corner"):
            low, high = strip_rows(field, i)
            out[tile, row : row + 1] = value[low : low + 1]
            out[tile, row + 1 : row + 2] = value[high : high + 1]
        else:
            out[tile] = value


def halo_rows(fields, from_low, from_high, field, i, plane, first, rows):
    ref, side, layer = (from_low, -1, -plane) if plane < 0 else (from_high, 1, plane - NX + 1)
    tile, row = PLAN_X[fields, side][0][field, i, layer]
    if field[2] in ("strip", "corner"):
        first = strip_rows(field, i).index(first)
    return ref[tile, row + first : row + first + rows]


def pack_y(fields, side, own, from_low, from_high, out):
    for field, i, plane, start, skip, rows in PLAN_Y[fields, side][0]:
        first = skip if side > 0 else NY - skip - rows
        if 0 <= plane < NX or (field[2] == "ring" and -field[3] < plane < NX + field[3] - 1):
            out[start : start + rows] = own(field[0], i, plane, first, rows)
        else:
            out[start : start + rows] = halo_rows(fields, from_low, from_high, field, i, plane, first, rows)


def by_parity(axis, run, from_odd, from_even):
    parity = lax.axis_index(axis) % 2

    @pl.when(parity == 0)
    def _():
        run(from_odd, from_even)

    @pl.when(parity == 1)
    def _():
        run(from_even, from_odd)


def unpack_x(fields, wide, *from_x):
    for side, ref in zip((-1, 1), from_x):
        for (field, i, layer), (tile, row) in PLAN_X[fields, side][0].items():
            plane = (NX - 1 + layer if side > 0 else -layer) + HALO
            if field[2] in ("strip", "corner"):
                for n, at in enumerate(strip_rows(field, i)):
                    wide[field[0]][i, plane, NY + at : NY + at + 1] = ref[tile, row + n : row + n + 1]
            else:
                wide[field[0]][i, plane, NY : 2 * NY] = ref[tile]


def unpack_y(fields, wide, side, ref):
    for field, i, plane, start, skip, rows in PLAN_Y[fields, side][0]:
        first = 2 * NY + skip if side > 0 else NY - skip - rows
        wide[field[0]][i, plane + HALO, first : first + rows] = ref[start : start + rows]


def receive_x(fields, wide, odd_x, even_x):
    by_parity("gx", lambda low, high: unpack_x(fields, wide, low, high), odd_x, even_x)


def receive_y(fields, wide, from_partner, even):
    parity = lax.axis_index("gy") % 2
    ref = from_partner.at[1 - parity] if even else from_partner

    @pl.when(parity == 0)
    def _():
        unpack_y(fields, wide, 1 if even else -1, ref)

    @pl.when(parity == 1)
    def _():
        unpack_y(fields, wide, -1 if even else 1, ref)


def send_x(fields, read, to_odd, to_even):
    def run(to_low, to_high):
        pack_x(fields, 1, read, to_low)
        pack_x(fields, -1, read, to_high)

    by_parity("gx", run, to_odd, to_even)


def send_y(fields, own, odd_x, even_x, to_odd, to_even):
    def with_halo(from_low, from_high):
        def run(to_low, to_high):
            pack_y(fields, 1, own, from_low, from_high, to_low)
            pack_y(fields, -1, own, from_low, from_high, to_high)

        by_parity("gy", run, to_odd, to_even)

    by_parity("gx", with_halo, odd_x, even_x)


def moments(f):
    v = list(f)
    for stride in (9, 3, 1):
        for i in range(27):
            if (i // stride) % 3 == 0:
                a, b, c = v[i], v[i + stride], v[i + 2 * stride]
                s = (a + c) + b
                v[i], v[i + stride], v[i + 2 * stride] = s, c - a, s - 3.0 * b
    return v


def moments_transposed(m):
    v = list(m)
    for stride in (9, 3, 1):
        for i in range(27):
            if (i // stride) % 3 == 0:
                s, d, q = v[i], v[i + stride], v[i + 2 * stride]
                t = s + q
                v[i], v[i + stride], v[i + 2 * stride] = t - d, s - (q + q), t + d
    return v


def rate_of(rates, i, relaxing, even, odd):
    return jnp.where(relaxing, rates[i], odd if ODD[i] else even)


def kinds_of(kind):
    relaxing = kind < 1.5
    even = jnp.where((kind > 1.5) & (kind < 3.5), 1.0, 0.0)
    odd = jnp.where(kind > 3.5, 2.0, even)
    return relaxing, even, odd


def collide(f, kappa, kind, rates, inlet):
    m = moments(f)
    relaxing, even, odd = kinds_of(kind)
    rho = m[0]
    inverse = 1.0 / rho
    ux, uy, uz = m[9] * inverse, m[3] * inverse, m[1] * inverse
    vx, vy = kappa * ux, kappa * uy
    vz = jnp.where((kind > 1.5) & (kind < 2.5), inlet, kappa * uz)
    den = jnp.where(relaxing, rho, 1.0)
    jx, jy, jz = den * vx, den * vy, den * vz
    xy, xz, yz = jx * vy, jx * vz, jy * vz
    xx, yy, zz = 3.0 * (jx * vx), 3.0 * (jy * vy), 3.0 * (jz * vz)
    x2, y2, z2 = xx - den, yy - den, zz - den
    e = [None] * 27
    e[0] = den
    e[18], e[6], e[2] = x2, y2, z2
    e[24], e[20], e[8] = -(x2 + yy), -(x2 + zz), -(y2 + zz)
    e[26] = (x2 + yy) + zz
    e[9], e[15], e[11], e[17] = jx, -jx, -jx, jx
    e[3], e[21], e[5], e[23] = jy, -jy, -jy, jy
    e[1], e[19], e[7], e[25] = jz, -jz, -jz, jz
    e[12], e[14] = xy, -xy
    e[10], e[16] = xz, -xz
    e[4], e[22] = yz, -yz
    out = []
    for i in range(27):
        rate = rate_of(rates, i, relaxing, even, odd)
        gap = -m[i] if e[i] is None else e[i] - m[i]
        out.append(SCALE[i] * (m[i] + rate * gap))
    return moments_transposed(out), (ux, uy, uz, inverse, rho)


def collide_back(h, kappa, kind, rates, speed, rho=None):
    y = moments(h)
    relaxing, even, odd = kinds_of(kind)
    ux, uy, uz, inverse = speed
    w, z = [], []
    for i in range(27):
        yi = SCALE[i] * y[i]
        wi = rate_of(rates, i, relaxing, even, odd) * yi
        w.append(wi)
        z.append(yi - wi)
    vx, vy, vz = kappa * ux, kappa * uy, kappa * uz
    w222 = w[26]
    a_x = (w[18] - w[24]) - (w[20] - w222)
    a_y = (w[6] - w[24]) - (w[8] - w222)
    a_z = (w[2] - w[20]) - (w[8] - w222)
    b_x = (w[9] - w[15]) - (w[11] - w[17])
    b_y = (w[3] - w[21]) - (w[5] - w[23])
    b_z = (w[1] - w[19]) - (w[7] - w[25])
    c_xy, c_xz, c_yz = w[12] - w[14], w[10] - w[16], w[4] - w[22]
    base = ((w[0] - w[18]) - (w[6] + w[2])) + ((w[24] + w[20]) + (w[8] - w222))
    p_x, p_y, p_z = 3.0 * (a_x * vx), 3.0 * (a_y * vy), 3.0 * (a_z * vz)
    q_x, q_y, q_z = c_xy * vy + c_xz * vz, c_xy * vx + c_yz * vz, c_xz * vx + c_yz * vy
    r_x, r_y, r_z = b_x + p_x, b_y + p_y, b_z + p_z
    value = base + vx * (r_x + 0.5 * q_x) + vy * (r_y + 0.5 * q_y) + vz * (r_z + 0.5 * q_z)
    g_x, g_y, g_z = r_x + p_x + q_x, r_y + p_y + q_y, r_z + p_z + q_z
    factor = jnp.where(relaxing, kappa, kappa * inverse)
    along = ux * g_x + uy * g_y + uz * g_z
    z[0] = z[0] + (jnp.where(relaxing, value, 0.0) - factor * along)
    z[9] = z[9] + factor * g_x
    z[3] = z[3] + factor * g_y
    z[1] = z[1] + factor * g_z
    return moments_transposed(z), None if rho is None else rho * along


def turned(value, shift):
    return value if shift == 0 else pltpu.roll(value, shift % LANES, axis=1)


class Own:
    items = tuple(range(HALO - 1, HALO + NX + 1))

    def get(self, ref, place, shift=0):
        return ref[place + (slice(NY + shift, 2 * NY + shift),)]

    def put(self, ref, place, value, halves=(True, True)):
        ref[place + (slice(NY, 2 * NY),)] = value


class Edge:
    items = tuple((plane, plane + 1) for plane in range(HALO - 1, HALO + NX + 1, 2))

    def __init__(self, high, narrow=False):
        self.first = NY - 2 + NY * high
        self.skip = 1 if narrow else 0
        if narrow:
            self.items = ((HALO - 2, HALO + NX + 1),)

    def get(self, ref, place, shift=0):
        upper, lower = (
            ref[place[:-1] + (plane, pl.ds(self.first + shift - half * (NY // 2), NY))]
            for half, plane in enumerate(place[-1])
        )
        return jnp.where(lax.broadcasted_iota(jnp.int32, (NY, LANES), 0) < NY // 2, upper, lower)

    def put(self, ref, place, value, halves=(True, True)):
        rows = NY // 2 - 2 * self.skip
        for half, plane in enumerate(place[-1]):
            if halves[half]:
                start = half * (NY // 2) + self.skip
                ref[place[:-1] + (plane, pl.ds(self.first + self.skip, rows))] = value[start : start + rows]


OWN = Own()


def edges(even):
    parity = lax.axis_index("gy") % 2
    high = 1 - parity if even else parity
    return Edge(high), Edge(high, True)


def pulled(wide, plane, rows, direction):
    tiles = []
    for i, (cx, cy, cz) in enumerate(VEL):
        moved = (
            tuple(p - direction * cx for p in plane) if isinstance(plane, tuple) else plane - direction * cx
        )
        tiles.append(turned(rows.get(wide, (i, moved), -direction * cy), direction * cz))
    return tiles


def planes_loop(items, load, work, store):
    together = 3 if len(items) == 6 else len(items)

    def body(n, carry):
        planes = items if together == len(items) else [items[0] + together * n + k for k in range(together)]
        results = [work(*values) for values in [load(plane) for plane in planes]]
        for plane, result in zip(planes, results):
            store(plane, result)
        return carry

    if together == len(items):
        body(0, 0)
    else:
        lax.fori_loop(0, len(items) // together, body, 0)


def put_inner(ahead, direction, load, work):
    results = [work(*values) for values in [load(1), load(NX - 2)]]
    for n, out in enumerate(results):
        for i in range(27):
            if VEL[i][0] == (direction if n else -direction):
                ahead[n, i] = out[i]


def put_all(rows, target, plane, out, direction, outer):
    for i in range(27):
        halves = (VEL[i][0] == direction, VEL[i][0] == -direction) if outer else (True, True)
        rows.put(target, (i, plane), out[i], halves)


def forward(rows, source, target, cell, speed, rates, inlet, outer=False):
    def load(plane):
        return pulled(source, plane, rows, 1), rows.get(cell, (0, plane)), rows.get(cell, (1, plane))

    def work(f, kappa, kind):
        return collide(f, kappa, kind, rates, inlet)

    def store(plane, result):
        out, values = result
        put_all(rows, target, plane, out, 1, outer)
        if not outer:
            for i in range(5):
                rows.put(speed, (i, plane), values[i])

    planes_loop(rows.items, load, work, store)


def backward(rows, source, target, cell, speed, gain, rates, outer=False):
    def load(plane):
        values = [rows.get(speed, (i, plane)) for i in range(5)]
        h = pulled(source, plane, rows, -1)
        return h, rows.get(cell, (0, plane)), rows.get(cell, (1, plane)), values

    def work(h, kappa, kind, values):
        return collide_back(h, kappa, kind, rates, values[:4], values[4])

    def store(plane, result):
        out, grad = result
        put_all(rows, target, plane, out, -1, outer)
        if not outer:
            rows.put(gain, (plane,), grad)

    planes_loop(rows.items, load, work, store)


def inlet_speed(start, step):
    time = jnp.full((NY, LANES), (start[0] + step) % PULSE_PERIOD, jnp.int32).astype(jnp.float32)
    return INLET_SPEED * jnp.sin(time * (2.0 * np.pi / PULSE_PERIOD))


def kappa_of(porosity, kind):
    damping = (RAMP_Q + porosity) / (
        RAMP_Q * (1.0 + DRAG_MAX) + (1.0 - DRAG_MAX * RAMP_Q) * porosity
    )
    return jnp.where(kind < 0.5, damping, jnp.where((kind > 2.5) & (kind < 3.5), 1.0, 0.0))


def first_kernel(
    rates_hbm, start_hbm, populations, cotangent, porosity, cell_type,
    post_hbm, cell_hbm, speed_hbm, to_odd_hbm, to_even_hbm,
    rates, start, f, gamma, kinds, ends, post, cell, speed, to_odd, to_even, ahead, sems,
):
    small = start_copies(
        sems, (rates_hbm, rates), (start_hbm, start), (porosity, gamma), (cell_type, kinds)
    )
    halves = [
        start_copies(sems.at[4 + n : 5 + n], (populations.at[:, 2 * n : 2 * n + 2], f.at[:, 2 * n : 2 * n + 2]))
        for n in range(NX // 2)
    ]
    tail = start_copies(
        sems.at[6:8], (cotangent.at[18:27, 0], ends.at[0]), (cotangent.at[0:9, NX - 1], ends.at[1])
    )
    small()
    inlet = inlet_speed(start, 0)
    done = []
    for n, arrived in enumerate(halves):
        arrived()
        planes = range(2 * n, 2 * n + 2)
        results = []
        for plane in planes:
            kind = kinds[plane].astype(jnp.float32)
            kappa = kappa_of(gamma[plane], kind)
            cell[0, plane] = kappa
            cell[1, plane] = kind
            results.append(collide([f[i, plane] for i in range(27)], kappa, kind, rates, inlet))
        for plane, (out, values) in zip(planes, results):
            for i in range(27):
                post[i, plane, NY : 2 * NY] = out[i]
            for i in range(5):
                speed[i, plane] = values[i]
        part = slice(2 * n, 2 * n + 2)
        done.append(start_copies(sems.at[4 + n : 5 + n], (post.at[:, part, NY : 2 * NY], post_hbm.at[:, part])))
    done.append(start_copies(sems, (cell, cell_hbm), (speed, speed_hbm)))
    later = inlet_speed(start, 1)
    put_inner(
        ahead, 1,
        lambda plane: (pulled(post, plane, OWN, 1), cell[0, plane], cell[1, plane]),
        lambda f, kappa, kind: collide(f, kappa, kind, rates, later)[0],
    )
    tail()

    def read(name, i, plane):
        if name == "adjoint":
            return ends[0, i - 18] if plane == 0 else ends[1, i]
        if name == "next":
            return ahead[plane - 1, i]
        return cell[i, plane] if name in ("cell", "corner") else post[i, plane, NY : 2 * NY]

    send_x(FIRST, read, to_odd, to_even)
    done.append(start_copies(sems.at[6:8], (to_odd, to_odd_hbm), (to_even, to_even_hbm)))
    for wait in done:
        wait()


def holding_kernel(*refs):
    half = len(refs) // 2
    for n in range(half):
        pltpu.make_async_copy(refs[n], refs[half + n], refs[-1].at[n]).start()
    for n in range(half):
        pltpu.make_async_copy(refs[n], refs[half + n], refs[-1].at[n]).wait()


def second_kernel(post, cotangent, cell, odd_x, even_x, to_odd, to_even):
    sources = {"post": post, "adjoint": cotangent, "cell": cell}

    def own(name, i, plane, first, rows):
        return sources[name][i, plane, first : first + rows]

    send_y(FIRST, own, odd_x, even_x, to_odd, to_even)


def start_copies(sems, *pairs):
    copies = [pltpu.make_async_copy(a, b, sems.at[n]) for n, (a, b) in enumerate(pairs)]
    for copy in copies:
        copy.start()

    def wait():
        for copy in copies:
            copy.wait()

    return wait


def put_block(wide, block, members):
    for i in range(members):
        wide[i, HALO : HALO + NX, NY : 2 * NY] = block[i]


def third_early_kernel(
    rates_hbm, start_hbm, post, cotangent, cell, odd_x, even_x,
    post_zero, post_one, post_two, wide_adjoint, wide_cell, speed_one, speed_two,
    rates, start, sems,
):
    wait = start_copies(sems, (rates_hbm, rates), (start_hbm, start))
    put_block(post_zero, post, 27)
    put_block(wide_adjoint, cotangent, 27)
    put_block(wide_cell, cell, 2)
    wide = {
        "post": post_zero, "strip": post_zero, "next": post_one, "adjoint": wide_adjoint, "cell": wide_cell,
        "corner": wide_cell,
    }
    receive_x(FIRST, wide, odd_x, even_x)
    wait()
    forward(OWN, post_zero, post_one, wide_cell, speed_one, rates, inlet_speed(start, 1))
    forward(OWN, post_one, post_two, wide_cell, speed_two, rates, inlet_speed(start, 2))


def third_edges(
    rates_hbm, start_hbm, from_partner, even,
    post_zero, post_one, post_two, wide_adjoint, wide_cell, speed_one, speed_two,
    rates, start, sems,
):
    wait = start_copies(sems, (rates_hbm, rates), (start_hbm, start))
    wide = {
        "post": post_zero, "strip": post_zero, "next": post_one, "adjoint": wide_adjoint, "cell": wide_cell,
        "corner": wide_cell,
    }
    receive_y(FIRST, wide, from_partner, even)
    wait()
    rows, narrow = edges(even)
    inlet = inlet_speed(start, 1)
    forward(narrow, post_zero, post_one, wide_cell, speed_one, rates, inlet, True)
    forward(rows, post_zero, post_one, wide_cell, speed_one, rates, inlet)
    forward(rows, post_one, post_two, wide_cell, speed_two, rates, inlet_speed(start, 2))


def third_middle_kernel(rates_hbm, start_hbm, _0, _1, _2, _3, _4, _5, _6, even_y, *refs):
    third_edges(rates_hbm, start_hbm, even_y, True, *refs)


def third_late_kernel(
    rates_hbm, start_hbm, _0, _1, _2, _3, _4, _5, _6, odd_y,
    post_zero, post_one, post_two, wide_adjoint, wide_cell, speed_one, speed_two,
    last_post, adjoint, gain, to_odd, to_even,
    rates, start, inner, ahead, sems,
):
    third_edges(
        rates_hbm, start_hbm, odd_y, False, post_zero, post_one, post_two, wide_adjoint, wide_cell, speed_one,
        speed_two, rates, start, sems,
    )
    inlet = inlet_speed(start, 3)

    def load(n):
        plane = n + HALO
        return (
            pulled(post_two, plane, OWN, 1), pulled(wide_adjoint, plane, OWN, -1),
            OWN.get(wide_cell, (0, plane)), OWN.get(wide_cell, (1, plane)),
        )

    def work(f, h, kappa, kind):
        out, values = collide(f, kappa, kind, rates, inlet)
        return out, collide_back(h, kappa, kind, rates, values[:4], values[4])

    def store(n, result):
        out, (back, grad) = result
        for i in range(27):
            last_post[i, n] = out[i]
            adjoint[i, n] = back[i]
            inner[i, n, NY : 2 * NY] = back[i]
        gain[n] = grad

    planes_loop(range(NX), load, work, store)

    def load_inner(n):
        plane = n + HALO
        values = [OWN.get(speed_two, (i, plane)) for i in range(4)]
        return (
            pulled(inner, n, OWN, -1), OWN.get(wide_cell, (0, plane)), OWN.get(wide_cell, (1, plane)), values
        )

    def work_inner(h, kappa, kind, values):
        return collide_back(h, kappa, kind, rates, values)[0]

    put_inner(ahead, -1, load_inner, work_inner)

    def read(name, i, plane):
        if name == "corner":
            return speed_two[i, plane + HALO, NY : 2 * NY]
        if name == "next":
            return ahead[plane - 1, i]
        return {"post": last_post, "adjoint": adjoint, "strip": adjoint}[name][i, plane]

    send_x(SECOND, read, to_odd, to_even)


def fourth_kernel(post, adjoint, speed, odd_x, even_x, to_odd, to_even):
    def own(name, i, plane, first, rows):
        if name == "speed":
            return speed[i, plane + HALO, NY + first : NY + first + rows]
        return {"post": post, "adjoint": adjoint}[name][i, plane, first : first + rows]

    send_y(SECOND, own, odd_x, even_x, to_odd, to_even)


def fifth_early_kernel(
    rates_hbm, post, adjoint, wide_cell, speed_one, _0, odd_x, even_x,
    speed_two, adjoint_three, adjoint_two, adjoint_one, wide_post, gain_two, gain_one,
    rates, sems,
):
    wait = start_copies(sems, (rates_hbm, rates))
    put_block(wide_post, post, 27)
    put_block(adjoint_three, adjoint, 27)
    wide = {
        "post": wide_post, "adjoint": adjoint_three, "strip": adjoint_three, "next": adjoint_two, "speed": speed_two,
        "corner": speed_two,
    }
    receive_x(SECOND, wide, odd_x, even_x)
    wait()
    backward(OWN, adjoint_three, adjoint_two, wide_cell, speed_two, gain_two, rates)
    backward(OWN, adjoint_two, adjoint_one, wide_cell, speed_one, gain_one, rates)


def fifth_edges(
    rates_hbm, wide_cell, speed_one, from_partner, even,
    speed_two, adjoint_three, adjoint_two, adjoint_one, wide_post, gain_two, gain_one,
    rates, sems,
):
    wait = start_copies(sems, (rates_hbm, rates))
    wide = {
        "post": wide_post, "adjoint": adjoint_three, "strip": adjoint_three, "next": adjoint_two, "speed": speed_two,
        "corner": speed_two,
    }
    receive_y(SECOND, wide, from_partner, even)
    wait()
    rows, narrow = edges(even)
    backward(narrow, adjoint_three, adjoint_two, wide_cell, speed_two, gain_two, rates, True)
    backward(rows, adjoint_three, adjoint_two, wide_cell, speed_two, gain_two, rates)
    backward(rows, adjoint_two, adjoint_one, wide_cell, speed_one, gain_one, rates)


def fifth_middle_kernel(rates_hbm, wide_cell, speed_one, even_y, _0, _1, _2, _3, _4, _5, _6, *refs):
    fifth_edges(rates_hbm, wide_cell, speed_one, even_y, True, *refs)


def fifth_late_kernel(
    rates_hbm, wide_cell, speed_zero, speed_one, gain, porosity, odd_y, _0, _1, _2, _3, _4, _5, _6,
    flow, first_adjoint, sensitivity,
    speed_two, adjoint_three, adjoint_two, adjoint_one, wide_post, gain_two, gain_one,
    rates, flow_here, adjoint_here, sensitivity_here, sems,
):
    fifth_edges(
        rates_hbm, wide_cell, speed_one, odd_y, False, speed_two, adjoint_three, adjoint_two, adjoint_one, wide_post,
        gain_two, gain_one, rates, sems,
    )

    def run(n, carry):
        tiles = pulled(wide_post, n + HALO, OWN, 1)
        for i in range(27):
            flow_here[i, n] = tiles[i]
        return carry

    lax.fori_loop(0, NX, run, 0)
    wait = start_copies(sems, (flow_here, flow))
    def load(n):
        plane = n + HALO
        total = (gain[n] + OWN.get(gain_two, (plane,))) + OWN.get(gain_one, (plane,))
        ramp = RAMP_Q * (1.0 + DRAG_MAX) + (1.0 - DRAG_MAX * RAMP_Q) * porosity[n]
        slope = (DRAG_MAX * RAMP_Q * (1.0 + RAMP_Q)) / (ramp * ramp)
        kappa, kind = OWN.get(wide_cell, (0, plane)), OWN.get(wide_cell, (1, plane))
        values = [speed_zero[i, n] for i in range(5)]
        return pulled(adjoint_one, plane, OWN, -1), kappa, kind, values, total, slope

    def work(h, kappa, kind, values, total, slope):
        out, grad = collide_back(h, kappa, kind, rates, values[:4], values[4])
        return out, jnp.where(kind < 0.5, slope * (total + grad), 0.0)

    def store(n, result):
        out, gradient = result
        for i in range(27):
            adjoint_here[i, n] = out[i]
        sensitivity_here[n] = gradient

    planes_loop(range(NX), load, work, store)
    last = start_copies(sems.at[1:3], (adjoint_here, first_adjoint), (sensitivity_here, sensitivity))
    wait()
    last()


def f32(*shape):
    return jax.ShapeDtypeStruct(shape, jnp.float32)


def call(kernel, far, arrays, outs, scratch=(), limit=VMEM_LIMIT, aliases=None, far_outs=0):
    hbm = pl.BlockSpec(memory_space=pltpu.HBM)
    vmem = pl.BlockSpec(memory_space=pltpu.VMEM)
    return pl.pallas_call(
        kernel,
        out_shape=tuple(f32(*s) for s in outs),
        in_specs=[hbm] * len(far) + [vmem] * len(arrays),
        out_specs=(hbm,) * far_outs + (vmem,) * (len(outs) - far_outs),
        scratch_shapes=[pltpu.VMEM(s, jnp.float32) if isinstance(s, tuple) else s for s in scratch],
        compiler_params=pltpu.CompilerParams(vmem_limit_bytes=limit),
        input_output_aliases=aliases or {},
        name=kernel.__name__,
    )(*far, *arrays)


def partners(axis, first):
    count = lax.axis_size(axis)
    return [[i % count, (i + 1) % count] for i in range(first, count + first, 2)]


def swap(value, axis, first):
    pairs = partners(axis, first)
    return lax.ppermute(value, axis, [(a, b) for a, b in pairs] + [(b, a) for a, b in pairs])


def exchange_x(to_odd, to_even):
    return swap(to_odd, "gx", 1), swap(to_even, "gx", 0)


def exchange_y(to_odd, to_even):
    from_odd = swap(to_odd, "gy", 1)
    return from_odd, lax.all_gather(to_even, "gy", axis_index_groups=partners("gy", 0))


def body(populations, cotangent, porosity, cell_type, rates, start_step):
    block = (27, NX, NY, LANES)
    wide = (27, PLANES, ROWS, LANES)
    inner, ahead = (27, NX, ROWS, LANES), (2, 27, NY, LANES)
    tiles = (PLAN_X[FIRST, 1][1], NY, LANES), (PLAN_X[FIRST, -1][1], NY, LANES)
    rows = (PLAN_Y[FIRST, 1][1], LANES), (PLAN_Y[FIRST, -1][1], LANES)
    rates_here, start_here = pltpu.SMEM((27,), jnp.float32), pltpu.SMEM((1,), jnp.int32)
    post, cell, speed_zero, to_odd, to_even = call(
        first_kernel, (rates, start_step, populations, cotangent, porosity, cell_type), (),
        (block, (2, NX, NY, LANES), (5, NX, NY, LANES)) + tiles,
        (
            rates_here, start_here, block, (NX, NY, LANES), pltpu.VMEM((NX, NY, LANES), jnp.int32),
            (2, 9, NY, LANES), inner, (2, NX, NY, LANES), (5, NX, NY, LANES), *tiles, ahead,
            pltpu.SemaphoreType.DMA((8,)),
        ),
        FIRST_LIMIT,
        far_outs=5,
    )
    kept = (post, cotangent, cell)
    post, held, cell = call(
        holding_kernel, kept, (), tuple(a.shape for a in kept), (pltpu.SemaphoreType.DMA((len(kept),)),)
    )
    x_halos = exchange_x(to_odd, to_even)
    to_odd, to_even = call(second_kernel, (), (post, held, cell) + x_halos, rows)
    y_halos = exchange_y(to_odd, to_even)
    wide_values = (5, PLANES, ROWS, LANES)
    wides = (wide, wide, wide, wide, (2, PLANES, ROWS, LANES), wide_values, wide_values)
    scalars = (rates_here, start_here, pltpu.SemaphoreType.DMA((2,)))
    wides = call(
        third_early_kernel, (rates, start_step), (post, held, cell) + x_halos, wides, scalars
    )
    odd_y, even_y = y_halos
    kept = tuple(a.shape for a in wides)
    wides = call(
        third_middle_kernel, (rates, start_step), tuple(wides) + (even_y,), kept, scalars,
        aliases={2 + n: n for n in range(len(wides))},
    )
    tiles = (PLAN_X[SECOND, 1][1], NY, LANES), (PLAN_X[SECOND, -1][1], NY, LANES)
    rows = (PLAN_Y[SECOND, 1][1], LANES), (PLAN_Y[SECOND, -1][1], LANES)
    *wides, post, adjoint, gain, to_odd, to_even = call(
        third_late_kernel, (rates, start_step), tuple(wides) + (odd_y,),
        kept + (block, block, (NX, NY, LANES)) + tiles,
        scalars[:2] + (inner, ahead) + scalars[2:], aliases={2 + n: n for n in range(len(wides))},
    )
    wide_cell, speed_one, speed_two = wides[4:]
    x_halos = exchange_x(to_odd, to_even)
    to_odd, to_even = call(fourth_kernel, (), (post, adjoint, speed_two) + x_halos, rows)
    y_halos = exchange_y(to_odd, to_even)
    scalars = (rates_here, pltpu.SemaphoreType.DMA((1,)))
    wide_gain = (PLANES, ROWS, LANES)
    wides = call(
        fifth_early_kernel, (rates,), (post, adjoint, wide_cell, speed_one, speed_two) + x_halos,
        (wide_values, wide, wide, wide, wide, wide_gain, wide_gain), scalars, aliases={5: 0},
    )
    odd_y, even_y = y_halos
    kept = tuple(a.shape for a in wides)
    wides = call(
        fifth_middle_kernel, (rates,), (wide_cell, speed_one, even_y) + tuple(wides), kept, scalars,
        aliases={4 + n: n for n in range(len(wides))},
    )
    return call(
        fifth_late_kernel, (rates,),
        (wide_cell, speed_zero, speed_one, gain, porosity, odd_y) + tuple(wides),
        (block, block, (NX, NY, LANES)) + kept,
        (rates_here, block, block, (NX, NY, LANES), pltpu.SemaphoreType.DMA((3,))),
        aliases={7 + n: 3 + n for n in range(len(wides))}, far_outs=3,
    )[:3]


def solution(mesh):
    return jax.shard_map(
        body,
        mesh=mesh,
        in_specs=(
            P(None, "gx", "gy", None),
            P(None, "gx", "gy", None),
            P("gx", "gy", None),
            P("gx", "gy", None),
            P(),
            P(),
        ),
        out_specs=(P(None, "gx", "gy", None), P(None, "gx", "gy", None), P("gx", "gy", None)),
        check_vma=False,
    )
```

```python
import jax
import jax.numpy as jnp
import numpy as np
from jax import lax
from jax.experimental import pallas as pl
from jax.experimental.pallas import tpu as pltpu
from jax.sharding import PartitionSpec as P

DRAG_MAX = 1.0
RAMP_Q = 0.1
INLET_SPEED = 0.3
PULSE_PERIOD = 64

NX, NY, LANES = 4, 8, 128
HALO = 3
PLANES = NX + 2 * HALO
ROWS = 3 * NY
VMEM_LIMIT = 16 * 1024 * 1024
FIRST_LIMIT = 64 * 1024 * 1024

SCALE = [
    float(s)
    for s in np.kron(np.kron([1 / 3, 1 / 2, 1 / 6], [1 / 3, 1 / 2, 1 / 6]), [1 / 3, 1 / 2, 1 / 6])
]
VEL = [(a - 1, b - 1, d - 1) for a in range(3) for b in range(3) for d in range(3)]
ODD = [(c[0] == 0) ^ (c[1] == 0) ^ (c[2] == 0) for c in VEL]


def reach(component, side, width, direction):
    inward = -side * direction
    return max(0, width - (0 if component == inward else 1 if component == 0 else 2))


def layers_x(field, i, side):
    _, _, kind, width, _, direction = field
    if kind == "stream":
        return 1, reach(VEL[i][0], side, width, direction)
    if kind == "strip":
        return (reach(VEL[i][0], side, width, direction),) * 2
    if kind == "next":
        return width, width if VEL[i][0] == -side * direction else 0
    return (width if kind == "corner" else 1), 0 if kind == "ring" else width


def layers_y(field, i, side, plane):
    _, _, kind, _, width, direction = field
    if kind in ("stream", "strip"):
        return 0, reach(VEL[i][1], side, width, direction)
    if kind == "next":
        return width - 1, width if VEL[i][1] == -side * direction else 0
    return (width - 1 if kind == "ring" else 0), width


def strip_rows(field, i):
    return {1: (NY - 2, NY - 1), 0: (0, NY - 1), -1: (0, 1)}[VEL[i][1] * field[5]]


def plan_x(fields, side):
    places, strips, tile = {}, [], 0
    for field in fields:
        for layer in range(1, NX):
            for i in range(field[1]):
                first, last = layers_x(field, i, side)
                if not first <= layer <= last:
                    continue
                if field[2] in ("strip", "corner"):
                    strips.append((field, i, layer))
                else:
                    places[field, i, layer] = tile, 0
                    tile += 1
    for n, key in enumerate(strips):
        places[key] = tile + n // (NY // 2), n % (NY // 2) * 2
    return places, tile - (-len(strips) // (NY // 2))


def plan_y(fields, side):
    entries, start = [], 0
    for field in fields:
        for plane in range(1 - NX, 2 * NX - 1):
            for i in range(field[1]):
                if plane < 0 or plane >= NX:
                    first, last = layers_x(field, i, -1 if plane < 0 else 1)
                    inner = field[2] == "ring" and -field[3] < plane < NX + field[3] - 1
                    if not inner and not first <= (-plane if plane < 0 else plane - NX + 1) <= last:
                        continue
                elif field[2] in ("strip", "next", "corner"):
                    continue
                skip, last = layers_y(field, i, side, plane)
                if last > skip:
                    entries.append((field, i, plane, start, skip, last - skip))
                    start += last - skip
    return entries, -(-start // 8) * 8


FIRST = (
    ("post", 27, "stream", 2, 3, 1), ("strip", 27, "strip", 3, 2, 1), ("next", 27, "next", 2, 2, 1),
    ("adjoint", 27, "stream", 1, 1, -1), ("cell", 2, "plain", 1, 2, 0), ("corner", 2, "corner", 2, 1, 0),
)
SECOND = (
    ("adjoint", 27, "stream", 2, 3, -1), ("strip", 27, "strip", 3, 2, -1), ("next", 27, "next", 2, 2, -1),
    ("post", 27, "stream", 1, 1, 1), ("speed", 4, "ring", 2, 2, 0), ("corner", 4, "corner", 2, 1, 0),
)
PLAN_X = {(f, s): plan_x(f, s) for f in (FIRST, SECOND) for s in (-1, 1)}
PLAN_Y = {(f, s): plan_y(f, s) for f in (FIRST, SECOND) for s in (-1, 1)}


def pack_x(fields, side, read, out):
    for (field, i, layer), (tile, row) in PLAN_X[fields, side][0].items():
        value = read(field[0], i, layer - 1 if side > 0 else NX - layer)
        if field[2] in ("strip", "corner"):
            low, high = strip_rows(field, i)
            out[tile, row : row + 1] = value[low : low + 1]
            out[tile, row + 1 : row + 2] = value[high : high + 1]
        else:
            out[tile] = value


def halo_rows(fields, from_low, from_high, field, i, plane, first, rows):
    ref, side, layer = (from_low, -1, -plane) if plane < 0 else (from_high, 1, plane - NX + 1)
    tile, row = PLAN_X[fields, side][0][field, i, layer]
    if field[2] in ("strip", "corner"):
        first = strip_rows(field, i).index(first)
    return ref[tile, row + first : row + first + rows]


def pack_y(fields, side, own, from_low, from_high, out):
    for field, i, plane, start, skip, rows in PLAN_Y[fields, side][0]:
        first = skip if side > 0 else NY - skip - rows
        if 0 <= plane < NX or (field[2] == "ring" and -field[3] < plane < NX + field[3] - 1):
            out[start : start + rows] = own(field[0], i, plane, first, rows)
        else:
            out[start : start + rows] = halo_rows(fields, from_low, from_high, field, i, plane, first, rows)


def by_parity(axis, run, from_odd, from_even):
    parity = lax.axis_index(axis) % 2

    @pl.when(parity == 0)
    def _():
        run(from_odd, from_even)

    @pl.when(parity == 1)
    def _():
        run(from_even, from_odd)


def unpack_x(fields, wide, *from_x):
    for side, ref in zip((-1, 1), from_x):
        for (field, i, layer), (tile, row) in PLAN_X[fields, side][0].items():
            plane = (NX - 1 + layer if side > 0 else -layer) + HALO
            if field[2] in ("strip", "corner"):
                for n, at in enumerate(strip_rows(field, i)):
                    wide[field[0]][i, plane, NY + at : NY + at + 1] = ref[tile, row + n : row + n + 1]
            else:
                wide[field[0]][i, plane, NY : 2 * NY] = ref[tile]


def unpack_y(fields, wide, side, ref):
    for field, i, plane, start, skip, rows in PLAN_Y[fields, side][0]:
        first = 2 * NY + skip if side > 0 else NY - skip - rows
        wide[field[0]][i, plane + HALO, first : first + rows] = ref[start : start + rows]


def receive_x(fields, wide, odd_x, even_x):
    by_parity("gx", lambda low, high: unpack_x(fields, wide, low, high), odd_x, even_x)


def receive_y(fields, wide, from_partner, even):
    parity = lax.axis_index("gy") % 2
    ref = from_partner.at[1 - parity] if even else from_partner

    @pl.when(parity == 0)
    def _():
        unpack_y(fields, wide, 1 if even else -1, ref)

    @pl.when(parity == 1)
    def _():
        unpack_y(fields, wide, -1 if even else 1, ref)


def send_x(fields, read, to_odd, to_even):
    def run(to_low, to_high):
        pack_x(fields, 1, read, to_low)
        pack_x(fields, -1, read, to_high)

    by_parity("gx", run, to_odd, to_even)


def send_y(fields, own, odd_x, even_x, to_odd, to_even):
    def with_halo(from_low, from_high):
        def run(to_low, to_high):
            pack_y(fields, 1, own, from_low, from_high, to_low)
            pack_y(fields, -1, own, from_low, from_high, to_high)

        by_parity("gy", run, to_odd, to_even)

    by_parity("gx", with_halo, odd_x, even_x)


def moments(f):
    v = list(f)
    for stride in (9, 3, 1):
        for i in range(27):
            if (i // stride) % 3 == 0:
                a, b, c = v[i], v[i + stride], v[i + 2 * stride]
                s = (a + c) + b
                v[i], v[i + stride], v[i + 2 * stride] = s, c - a, s - 3.0 * b
    return v


def moments_transposed(m):
    v = list(m)
    for stride in (9, 3, 1):
        for i in range(27):
            if (i // stride) % 3 == 0:
                s, d, q = v[i], v[i + stride], v[i + 2 * stride]
                t = s + q
                v[i], v[i + stride], v[i + 2 * stride] = t - d, s - (q + q), t + d
    return v


def rate_of(rates, i, relaxing, even, odd):
    return jnp.where(relaxing, rates[i], odd if ODD[i] else even)


def kinds_of(kind):
    relaxing = kind < 1.5
    even = jnp.where((kind > 1.5) & (kind < 3.5), 1.0, 0.0)
    odd = jnp.where(kind > 3.5, 2.0, even)
    return relaxing, even, odd


def collide(f, kappa, kind, rates, inlet):
    m = moments(f)
    relaxing, even, odd = kinds_of(kind)
    rho = m[0]
    inverse = 1.0 / rho
    ux, uy, uz = m[9] * inverse, m[3] * inverse, m[1] * inverse
    vx, vy = kappa * ux, kappa * uy
    vz = jnp.where((kind > 1.5) & (kind < 2.5), inlet, kappa * uz)
    den = jnp.where(relaxing, rho, 1.0)
    jx, jy, jz = den * vx, den * vy, den * vz
    xy, xz, yz = jx * vy, jx * vz, jy * vz
    xx, yy, zz = 3.0 * (jx * vx), 3.0 * (jy * vy), 3.0 * (jz * vz)
    x2, y2, z2 = xx - den, yy - den, zz - den
    e = [None] * 27
    e[0] = den
    e[18], e[6], e[2] = x2, y2, z2
    e[24], e[20], e[8] = -(x2 + yy), -(x2 + zz), -(y2 + zz)
    e[26] = (x2 + yy) + zz
    e[9], e[15], e[11], e[17] = jx, -jx, -jx, jx
    e[3], e[21], e[5], e[23] = jy, -jy, -jy, jy
    e[1], e[19], e[7], e[25] = jz, -jz, -jz, jz
    e[12], e[14] = xy, -xy
    e[10], e[16] = xz, -xz
    e[4], e[22] = yz, -yz
    out = []
    for i in range(27):
        rate = rate_of(rates, i, relaxing, even, odd)
        gap = -m[i] if e[i] is None else e[i] - m[i]
        out.append(SCALE[i] * (m[i] + rate * gap))
    return moments_transposed(out), (ux, uy, uz, inverse, rho)


def collide_back(h, kappa, kind, rates, speed, rho=None):
    y = moments(h)
    relaxing, even, odd = kinds_of(kind)
    ux, uy, uz, inverse = speed
    w, z = [], []
    for i in range(27):
        yi = SCALE[i] * y[i]
        wi = rate_of(rates, i, relaxing, even, odd) * yi
        w.append(wi)
        z.append(yi - wi)
    vx, vy, vz = kappa * ux, kappa * uy, kappa * uz
    w222 = w[26]
    a_x = (w[18] - w[24]) - (w[20] - w222)
    a_y = (w[6] - w[24]) - (w[8] - w222)
    a_z = (w[2] - w[20]) - (w[8] - w222)
    b_x = (w[9] - w[15]) - (w[11] - w[17])
    b_y = (w[3] - w[21]) - (w[5] - w[23])
    b_z = (w[1] - w[19]) - (w[7] - w[25])
    c_xy, c_xz, c_yz = w[12] - w[14], w[10] - w[16], w[4] - w[22]
    base = ((w[0] - w[18]) - (w[6] + w[2])) + ((w[24] + w[20]) + (w[8] - w222))
    p_x, p_y, p_z = 3.0 * (a_x * vx), 3.0 * (a_y * vy), 3.0 * (a_z * vz)
    q_x, q_y, q_z = c_xy * vy + c_xz * vz, c_xy * vx + c_yz * vz, c_xz * vx + c_yz * vy
    r_x, r_y, r_z = b_x + p_x, b_y + p_y, b_z + p_z
    value = base + vx * (r_x + 0.5 * q_x) + vy * (r_y + 0.5 * q_y) + vz * (r_z + 0.5 * q_z)
    g_x, g_y, g_z = r_x + p_x + q_x, r_y + p_y + q_y, r_z + p_z + q_z
    factor = jnp.where(relaxing, kappa, kappa * inverse)
    along = ux * g_x + uy * g_y + uz * g_z
    z[0] = z[0] + (jnp.where(relaxing, value, 0.0) - factor * along)
    z[9] = z[9] + factor * g_x
    z[3] = z[3] + factor * g_y
    z[1] = z[1] + factor * g_z
    return moments_transposed(z), None if rho is None else rho * along


def turned(value, shift):
    return value if shift == 0 else pltpu.roll(value, shift % LANES, axis=1)


class Own:
    items = tuple(range(HALO - 1, HALO + NX + 1))

    def get(self, ref, place, shift=0):
        return ref[place + (slice(NY + shift, 2 * NY + shift),)]

    def put(self, ref, place, value, halves=(True, True)):
        ref[place + (slice(NY, 2 * NY),)] = value


class Edge:
    items = tuple((plane, plane + 1) for plane in range(HALO - 1, HALO + NX + 1, 2))

    def __init__(self, high, narrow=False):
        self.first = NY - 2 + NY * high
        self.skip = 1 if narrow else 0
        if narrow:
            self.items = ((HALO - 2, HALO + NX + 1),)

    def get(self, ref, place, shift=0):
        upper, lower = (
            ref[place[:-1] + (plane, pl.ds(self.first + shift - half * (NY // 2), NY))]
            for half, plane in enumerate(place[-1])
        )
        return jnp.where(lax.broadcasted_iota(jnp.int32, (NY, LANES), 0) < NY // 2, upper, lower)

    def put(self, ref, place, value, halves=(True, True)):
        rows = NY // 2 - 2 * self.skip
        for half, plane in enumerate(place[-1]):
            if halves[half]:
                start = half * (NY // 2) + self.skip
                ref[place[:-1] + (plane, pl.ds(self.first + self.skip, rows))] = value[start : start + rows]


OWN = Own()


def edges(even):
    parity = lax.axis_index("gy") % 2
    high = 1 - parity if even else parity
    return Edge(high), Edge(high, True)


def pulled(wide, plane, rows, direction):
    tiles = []
    for i, (cx, cy, cz) in enumerate(VEL):
        moved = (
            tuple(p - direction * cx for p in plane) if isinstance(plane, tuple) else plane - direction * cx
        )
        tiles.append(turned(rows.get(wide, (i, moved), -direction * cy), direction * cz))
    return tiles


def planes_loop(items, load, work, store):
    together = 3 if len(items) == 6 else len(items)

    def body(n, carry):
        planes = items if together == len(items) else [items[0] + together * n + k for k in range(together)]
        results = [work(*values) for values in [load(plane) for plane in planes]]
        for plane, result in zip(planes, results):
            store(plane, result)
        return carry

    if together == len(items):
        body(0, 0)
    else:
        lax.fori_loop(0, len(items) // together, body, 0)


def put_inner(ahead, direction, load, work):
    results = [work(*values) for values in [load(1), load(NX - 2)]]
    for n, out in enumerate(results):
        for i in range(27):
            if VEL[i][0] == (direction if n else -direction):
                ahead[n, i] = out[i]


def put_all(rows, target, plane, out, direction, outer):
    for i in range(27):
        halves = (VEL[i][0] == direction, VEL[i][0] == -direction) if outer else (True, True)
        rows.put(target, (i, plane), out[i], halves)


def forward(rows, source, target, cell, speed, rates, inlet, outer=False):
    def load(plane):
        return pulled(source, plane, rows, 1), rows.get(cell, (0, plane)), rows.get(cell, (1, plane))

    def work(f, kappa, kind):
        return collide(f, kappa, kind, rates, inlet)

    def store(plane, result):
        out, values = result
        put_all(rows, target, plane, out, 1, outer)
        if not outer:
            for i in range(5):
                rows.put(speed, (i, plane), values[i])

    planes_loop(rows.items, load, work, store)


def backward(rows, source, target, cell, speed, gain, rates, outer=False):
    def load(plane):
        values = [rows.get(speed, (i, plane)) for i in range(5)]
        h = pulled(source, plane, rows, -1)
        return h, rows.get(cell, (0, plane)), rows.get(cell, (1, plane)), values

    def work(h, kappa, kind, values):
        return collide_back(h, kappa, kind, rates, values[:4], values[4])

    def store(plane, result):
        out, grad = result
        put_all(rows, target, plane, out, -1, outer)
        if not outer:
            rows.put(gain, (plane,), grad)

    planes_loop(rows.items, load, work, store)


def inlet_speed(start, step):
    time = jnp.full((NY, LANES), (start[0] + step) % PULSE_PERIOD, jnp.int32).astype(jnp.float32)
    return INLET_SPEED * jnp.sin(time * (2.0 * np.pi / PULSE_PERIOD))


def kappa_of(porosity, kind):
    damping = (RAMP_Q + porosity) / (
        RAMP_Q * (1.0 + DRAG_MAX) + (1.0 - DRAG_MAX * RAMP_Q) * porosity
    )
    return jnp.where(kind < 0.5, damping, jnp.where((kind > 2.5) & (kind < 3.5), 1.0, 0.0))


def first_kernel(
    rates_hbm, start_hbm, populations, cotangent, porosity, cell_type,
    post_hbm, cell_hbm, speed_hbm, to_odd_hbm, to_even_hbm,
    rates, start, f, gamma, kinds, ends, post, cell, speed, to_odd, to_even, ahead, sems,
):
    small = start_copies(
        sems, (rates_hbm, rates), (start_hbm, start), (porosity, gamma), (cell_type, kinds)
    )
    halves = [
        start_copies(sems.at[4 + n : 5 + n], (populations.at[:, 2 * n : 2 * n + 2], f.at[:, 2 * n : 2 * n + 2]))
        for n in range(NX // 2)
    ]
    tail = start_copies(
        sems.at[6:8], (cotangent.at[18:27, 0], ends.at[0]), (cotangent.at[0:9, NX - 1], ends.at[1])
    )
    small()
    inlet = inlet_speed(start, 0)
    done = []
    for n, arrived in enumerate(halves):
        arrived()
        planes = range(2 * n, 2 * n + 2)
        results = []
        for plane in planes:
            kind = kinds[plane].astype(jnp.float32)
            kappa = kappa_of(gamma[plane], kind)
            cell[0, plane] = kappa
            cell[1, plane] = kind
            results.append(collide([f[i, plane] for i in range(27)], kappa, kind, rates, inlet))
        for plane, (out, values) in zip(planes, results):
            for i in range(27):
                post[i, plane, NY : 2 * NY] = out[i]
            for i in range(5):
                speed[i, plane] = values[i]
        part = slice(2 * n, 2 * n + 2)
        done.append(start_copies(sems.at[4 + n : 5 + n], (post.at[:, part, NY : 2 * NY], post_hbm.at[:, part])))
    done.append(start_copies(sems, (cell, cell_hbm), (speed, speed_hbm)))
    later = inlet_speed(start, 1)
    put_inner(
        ahead, 1,
        lambda plane: (pulled(post, plane, OWN, 1), cell[0, plane], cell[1, plane]),
        lambda f, kappa, kind: collide(f, kappa, kind, rates, later)[0],
    )
    tail()

    def read(name, i, plane):
        if name == "adjoint":
            return ends[0, i - 18] if plane == 0 else ends[1, i]
        if name == "next":
            return ahead[plane - 1, i]
        return cell[i, plane] if name in ("cell", "corner") else post[i, plane, NY : 2 * NY]

    send_x(FIRST, read, to_odd, to_even)
    done.append(start_copies(sems.at[6:8], (to_odd, to_odd_hbm), (to_even, to_even_hbm)))
    for wait in done:
        wait()


def holding_kernel(*refs):
    half = len(refs) // 2
    for n in range(half):
        pltpu.make_async_copy(refs[n], refs[half + n], refs[-1].at[n]).start()
    for n in range(half):
        pltpu.make_async_copy(refs[n], refs[half + n], refs[-1].at[n]).wait()


def second_kernel(post, cotangent, cell, odd_x, even_x, to_odd, to_even):
    sources = {"post": post, "adjoint": cotangent, "cell": cell}

    def own(name, i, plane, first, rows):
        return sources[name][i, plane, first : first + rows]

    send_y(FIRST, own, odd_x, even_x, to_odd, to_even)


def start_copies(sems, *pairs):
    copies = [pltpu.make_async_copy(a, b, sems.at[n]) for n, (a, b) in enumerate(pairs)]
    for copy in copies:
        copy.start()

    def wait():
        for copy in copies:
            copy.wait()

    return wait


def put_block(wide, block, members):
    for i in range(members):
        wide[i, HALO : HALO + NX, NY : 2 * NY] = block[i]


def third_early_kernel(
    rates_hbm, start_hbm, post, cotangent, cell, odd_x, even_x,
    post_zero, post_one, post_two, wide_adjoint, wide_cell, speed_one, speed_two,
    rates, start, sems,
):
    wait = start_copies(sems, (rates_hbm, rates), (start_hbm, start))
    put_block(post_zero, post, 27)
    put_block(wide_adjoint, cotangent, 27)
    put_block(wide_cell, cell, 2)
    wide = {
        "post": post_zero, "strip": post_zero, "next": post_one, "adjoint": wide_adjoint, "cell": wide_cell,
        "corner": wide_cell,
    }
    receive_x(FIRST, wide, odd_x, even_x)
    wait()
    forward(OWN, post_zero, post_one, wide_cell, speed_one, rates, inlet_speed(start, 1))
    forward(OWN, post_one, post_two, wide_cell, speed_two, rates, inlet_speed(start, 2))


def third_edges(
    rates_hbm, start_hbm, from_partner, even,
    post_zero, post_one, post_two, wide_adjoint, wide_cell, speed_one, speed_two,
    rates, start, sems,
):
    wait = start_copies(sems, (rates_hbm, rates), (start_hbm, start))
    wide = {
        "post": post_zero, "strip": post_zero, "next": post_one, "adjoint": wide_adjoint, "cell": wide_cell,
        "corner": wide_cell,
    }
    receive_y(FIRST, wide, from_partner, even)
    wait()
    rows, narrow = edges(even)
    inlet = inlet_speed(start, 1)
    forward(narrow, post_zero, post_one, wide_cell, speed_one, rates, inlet, True)
    forward(rows, post_zero, post_one, wide_cell, speed_one, rates, inlet)
    forward(rows, post_one, post_two, wide_cell, speed_two, rates, inlet_speed(start, 2))


def third_middle_kernel(rates_hbm, start_hbm, _0, _1, _2, _3, _4, _5, _6, even_y, *refs):
    third_edges(rates_hbm, start_hbm, even_y, True, *refs)


def third_late_kernel(
    rates_hbm, start_hbm, _0, _1, _2, _3, _4, _5, _6, odd_y,
    post_zero, post_one, post_two, wide_adjoint, wide_cell, speed_one, speed_two,
    last_post, adjoint, gain, to_odd, to_even,
    rates, start, inner, ahead, sems,
):
    third_edges(
        rates_hbm, start_hbm, odd_y, False, post_zero, post_one, post_two, wide_adjoint, wide_cell, speed_one,
        speed_two, rates, start, sems,
    )
    inlet = inlet_speed(start, 3)

    def load(n):
        plane = n + HALO
        return (
            plane, pulled(post_two, plane, OWN, 1),
            OWN.get(wide_cell, (0, plane)), OWN.get(wide_cell, (1, plane)),
        )

    def work(plane, f, kappa, kind):
        out, values = collide(f, kappa, kind, rates, inlet)
        h = pulled(wide_adjoint, plane, OWN, -1)
        return out, collide_back(h, kappa, kind, rates, values[:4], values[4])

    def store(n, result):
        out, (back, grad) = result
        for i in range(27):
            last_post[i, n] = out[i]
            adjoint[i, n] = back[i]
            inner[i, n, NY : 2 * NY] = back[i]
        gain[n] = grad

    planes_loop(range(NX), load, work, store)

    def load_inner(n):
        plane = n + HALO
        values = [OWN.get(speed_two, (i, plane)) for i in range(4)]
        return (
            pulled(inner, n, OWN, -1), OWN.get(wide_cell, (0, plane)), OWN.get(wide_cell, (1, plane)), values
        )

    def work_inner(h, kappa, kind, values):
        return collide_back(h, kappa, kind, rates, values)[0]

    put_inner(ahead, -1, load_inner, work_inner)

    def read(name, i, plane):
        if name == "corner":
            return speed_two[i, plane + HALO, NY : 2 * NY]
        if name == "next":
            return ahead[plane - 1, i]
        return {"post": last_post, "adjoint": adjoint, "strip": adjoint}[name][i, plane]

    send_x(SECOND, read, to_odd, to_even)


def fourth_kernel(post, adjoint, speed, odd_x, even_x, to_odd, to_even):
    def own(name, i, plane, first, rows):
        if name == "speed":
            return speed[i, plane + HALO, NY + first : NY + first + rows]
        return {"post": post, "adjoint": adjoint}[name][i, plane, first : first + rows]

    send_y(SECOND, own, odd_x, even_x, to_odd, to_even)


def fifth_early_kernel(
    rates_hbm, post, adjoint, wide_cell, speed_one, _0, odd_x, even_x,
    speed_two, adjoint_three, adjoint_two, adjoint_one, wide_post, gain_two, gain_one,
    rates, sems,
):
    wait = start_copies(sems, (rates_hbm, rates))
    put_block(wide_post, post, 27)
    put_block(adjoint_three, adjoint, 27)
    wide = {
        "post": wide_post, "adjoint": adjoint_three, "strip": adjoint_three, "next": adjoint_two, "speed": speed_two,
        "corner": speed_two,
    }
    receive_x(SECOND, wide, odd_x, even_x)
    wait()
    backward(OWN, adjoint_three, adjoint_two, wide_cell, speed_two, gain_two, rates)
    backward(OWN, adjoint_two, adjoint_one, wide_cell, speed_one, gain_one, rates)


def fifth_edges(
    rates_hbm, wide_cell, speed_one, from_partner, even,
    speed_two, adjoint_three, adjoint_two, adjoint_one, wide_post, gain_two, gain_one,
    rates, sems,
):
    wait = start_copies(sems, (rates_hbm, rates))
    wide = {
        "post": wide_post, "adjoint": adjoint_three, "strip": adjoint_three, "next": adjoint_two, "speed": speed_two,
        "corner": speed_two,
    }
    receive_y(SECOND, wide, from_partner, even)
    wait()
    rows, narrow = edges(even)
    backward(narrow, adjoint_three, adjoint_two, wide_cell, speed_two, gain_two, rates, True)
    backward(rows, adjoint_three, adjoint_two, wide_cell, speed_two, gain_two, rates)
    backward(rows, adjoint_two, adjoint_one, wide_cell, speed_one, gain_one, rates)


def fifth_middle_kernel(rates_hbm, wide_cell, speed_one, even_y, _0, _1, _2, _3, _4, _5, _6, *refs):
    fifth_edges(rates_hbm, wide_cell, speed_one, even_y, True, *refs)


def fifth_late_kernel(
    rates_hbm, wide_cell, speed_zero, speed_one, gain, porosity, odd_y, _0, _1, _2, _3, _4, _5, _6,
    flow, first_adjoint, sensitivity,
    speed_two, adjoint_three, adjoint_two, adjoint_one, wide_post, gain_two, gain_one,
    rates, flow_here, adjoint_here, sensitivity_here, sems,
):
    fifth_edges(
        rates_hbm, wide_cell, speed_one, odd_y, False, speed_two, adjoint_three, adjoint_two, adjoint_one, wide_post,
        gain_two, gain_one, rates, sems,
    )

    def run(n, carry):
        tiles = pulled(wide_post, n + HALO, OWN, 1)
        for i in range(27):
            flow_here[i, n] = tiles[i]
        return carry

    lax.fori_loop(0, NX, run, 0)
    wait = start_copies(sems, (flow_here, flow))
    def load(n):
        plane = n + HALO
        total = (gain[n] + OWN.get(gain_two, (plane,))) + OWN.get(gain_one, (plane,))
        ramp = RAMP_Q * (1.0 + DRAG_MAX) + (1.0 - DRAG_MAX * RAMP_Q) * porosity[n]
        slope = (DRAG_MAX * RAMP_Q * (1.0 + RAMP_Q)) / (ramp * ramp)
        kappa, kind = OWN.get(wide_cell, (0, plane)), OWN.get(wide_cell, (1, plane))
        values = [speed_zero[i, n] for i in range(5)]
        return pulled(adjoint_one, plane, OWN, -1), kappa, kind, values, total, slope

    def work(h, kappa, kind, values, total, slope):
        out, grad = collide_back(h, kappa, kind, rates, values[:4], values[4])
        return out, jnp.where(kind < 0.5, slope * (total + grad), 0.0)

    def store(n, result):
        out, gradient = result
        for i in range(27):
            adjoint_here[i, n] = out[i]
        sensitivity_here[n] = gradient

    planes_loop(range(NX), load, work, store)
    last = start_copies(sems.at[1:3], (adjoint_here, first_adjoint), (sensitivity_here, sensitivity))
    wait()
    last()


def f32(*shape):
    return jax.ShapeDtypeStruct(shape, jnp.float32)


def call(kernel, far, arrays, outs, scratch=(), limit=VMEM_LIMIT, aliases=None, far_outs=0):
    hbm = pl.BlockSpec(memory_space=pltpu.HBM)
    vmem = pl.BlockSpec(memory_space=pltpu.VMEM)
    return pl.pallas_call(
        kernel,
        out_shape=tuple(f32(*s) for s in outs),
        in_specs=[hbm] * len(far) + [vmem] * len(arrays),
        out_specs=(hbm,) * far_outs + (vmem,) * (len(outs) - far_outs),
        scratch_shapes=[pltpu.VMEM(s, jnp.float32) if isinstance(s, tuple) else s for s in scratch],
        compiler_params=pltpu.CompilerParams(vmem_limit_bytes=limit),
        input_output_aliases=aliases or {},
        name=kernel.__name__,
    )(*far, *arrays)


def partners(axis, first):
    count = lax.axis_size(axis)
    return [[i % count, (i + 1) % count] for i in range(first, count + first, 2)]


def swap(value, axis, first):
    pairs = partners(axis, first)
    return lax.ppermute(value, axis, [(a, b) for a, b in pairs] + [(b, a) for a, b in pairs])


def exchange_x(to_odd, to_even):
    return swap(to_odd, "gx", 1), swap(to_even, "gx", 0)


def exchange_y(to_odd, to_even):
    from_odd = swap(to_odd, "gy", 1)
    return from_odd, lax.all_gather(to_even, "gy", axis_index_groups=partners("gy", 0))


def body(populations, cotangent, porosity, cell_type, rates, start_step):
    block = (27, NX, NY, LANES)
    wide = (27, PLANES, ROWS, LANES)
    inner, ahead = (27, NX, ROWS, LANES), (2, 27, NY, LANES)
    tiles = (PLAN_X[FIRST, 1][1], NY, LANES), (PLAN_X[FIRST, -1][1], NY, LANES)
    rows = (PLAN_Y[FIRST, 1][1], LANES), (PLAN_Y[FIRST, -1][1], LANES)
    rates_here, start_here = pltpu.SMEM((27,), jnp.float32), pltpu.SMEM((1,), jnp.int32)
    post, cell, speed_zero, to_odd, to_even = call(
        first_kernel, (rates, start_step, populations, cotangent, porosity, cell_type), (),
        (block, (2, NX, NY, LANES), (5, NX, NY, LANES)) + tiles,
        (
            rates_here, start_here, block, (NX, NY, LANES), pltpu.VMEM((NX, NY, LANES), jnp.int32),
            (2, 9, NY, LANES), inner, (2, NX, NY, LANES), (5, NX, NY, LANES), *tiles, ahead,
            pltpu.SemaphoreType.DMA((8,)),
        ),
        FIRST_LIMIT,
        far_outs=5,
    )
    kept = (post, cotangent, cell)
    post, held, cell = call(
        holding_kernel, kept, (), tuple(a.shape for a in kept), (pltpu.SemaphoreType.DMA((len(kept),)),)
    )
    x_halos = exchange_x(to_odd, to_even)
    to_odd, to_even = call(second_kernel, (), (post, held, cell) + x_halos, rows)
    y_halos = exchange_y(to_odd, to_even)
    wide_values = (5, PLANES, ROWS, LANES)
    wides = (wide, wide, wide, wide, (2, PLANES, ROWS, LANES), wide_values, wide_values)
    scalars = (rates_here, start_here, pltpu.SemaphoreType.DMA((2,)))
    wides = call(
        third_early_kernel, (rates, start_step), (post, held, cell) + x_halos, wides, scalars
    )
    odd_y, even_y = y_halos
    kept = tuple(a.shape for a in wides)
    wides = call(
        third_middle_kernel, (rates, start_step), tuple(wides) + (even_y,), kept, scalars,
        aliases={2 + n: n for n in range(len(wides))},
    )
    tiles = (PLAN_X[SECOND, 1][1], NY, LANES), (PLAN_X[SECOND, -1][1], NY, LANES)
    rows = (PLAN_Y[SECOND, 1][1], LANES), (PLAN_Y[SECOND, -1][1], LANES)
    *wides, post, adjoint, gain, to_odd, to_even = call(
        third_late_kernel, (rates, start_step), tuple(wides) + (odd_y,),
        kept + (block, block, (NX, NY, LANES)) + tiles,
        scalars[:2] + (inner, ahead) + scalars[2:], aliases={2 + n: n for n in range(len(wides))},
    )
    wide_cell, speed_one, speed_two = wides[4:]
    x_halos = exchange_x(to_odd, to_even)
    to_odd, to_even = call(fourth_kernel, (), (post, adjoint, speed_two) + x_halos, rows)
    y_halos = exchange_y(to_odd, to_even)
    scalars = (rates_here, pltpu.SemaphoreType.DMA((1,)))
    wide_gain = (PLANES, ROWS, LANES)
    wides = call(
        fifth_early_kernel, (rates,), (post, adjoint, wide_cell, speed_one, speed_two) + x_halos,
        (wide_values, wide, wide, wide, wide, wide_gain, wide_gain), scalars, aliases={5: 0},
    )
    odd_y, even_y = y_halos
    kept = tuple(a.shape for a in wides)
    wides = call(
        fifth_middle_kernel, (rates,), (wide_cell, speed_one, even_y) + tuple(wides), kept, scalars,
        aliases={4 + n: n for n in range(len(wides))},
    )
    return call(
        fifth_late_kernel, (rates,),
        (wide_cell, speed_zero, speed_one, gain, porosity, odd_y) + tuple(wides),
        (block, block, (NX, NY, LANES)) + kept,
        (rates_here, block, block, (NX, NY, LANES), pltpu.SemaphoreType.DMA((3,))),
        aliases={7 + n: 3 + n for n in range(len(wides))}, far_outs=3,
    )[:3]


def solution(mesh):
    return jax.shard_map(
        body,
        mesh=mesh,
        in_specs=(
            P(None, "gx", "gy", None),
            P(None, "gx", "gy", None),
            P("gx", "gy", None),
            P("gx", "gy", None),
            P(),
            P(),
        ),
        out_specs=(P(None, "gx", "gy", None), P(None, "gx", "gy", None), P("gx", "gy", None)),
        check_vma=False,
    )
```
